32 devices in a mesh: depth: 4 (over x, core), height: 8 (over z, y).
Axes of the slice: x: 2, y: 2, z: 4, core: 2. Of those that a mesh axis runs over, the one named last changes fastest.
Arguments:
- fixed_image: float32 [32, 32, 128], P('depth', 'height'), as said below
- moving_image: float32 [32, 32, 128], P('depth', 'height'), as said below
- conv_one: float32 [64, 1, 3, 3, 3], replicated, may hold values from -1.25 to 1.25
- gain_one: float32 [64], replicated, may hold values from 0.1 to 1.9
- shift_one: float32 [64], replicated, may hold values from -3 to 3
- conv_two: bfloat16 [27, 4096], replicated, may hold values from -0.15625 to 0.15625
- gain_two: float32 [64], replicated, may hold values from 0.1 to 1.9
- shift_two: float32 [64], replicated, may hold values from -3 to 3
- sharpness: float32 [1], replicated, may hold values from 1 to 4
Outputs:
- displacement: float32 [3, 32, 32, 128], P(None, 'depth', 'height')
The draws below stay inside these ranges and needn't reach their ends.
Inputs may be any that keep to these rules, and one draw needn't show every extreme that they name: `fixed_image`: intensities of a scan; the two scans show the same anatomy. `moving_image`: intensities of a scan; the two scans show the same anatomy.
All inputs are finite; a program needn't handle non-finite values.
Results may differ from the reference program's by a relative error of at most 0.0049.
Values may be sent and summed in bfloat16 or wider, within the bound.
No kernel may reach another device: no remote copies, remote signals or barrier semaphores. Data moves between devices by JAX's collectives and lax.ppermute only.
A program may use at most 64 MiB of HBM per device.

```python
import math
import jax
import jax.numpy as jnp
from jax import lax

C = 64
RADIUS = 3
WIDTH = 128
DEPTH = 32
HEIGHT = 32


def base_volume(key):
    noise = jax.random.normal(jax.random.fold_in(key, 17), (DEPTH, HEIGHT, WIDTH), jnp.float32)
    depth_pos = jnp.arange(DEPTH, dtype=jnp.float32) / DEPTH
    height_pos = jnp.arange(HEIGHT, dtype=jnp.float32) / HEIGHT
    across = jnp.ones((WIDTH,), jnp.float32)
    envelope = jnp.exp(jnp.log(3.0) * (depth_pos[:, None, None] + height_pos[None, :, None])) * across[None, None, :]
    return (noise, envelope)


def draw_fixed_image(key, part):
    noise, envelope = base_volume(key)
    return noise * envelope


def draw_moving_image(key, part):
    noise, envelope = base_volume(key)
    moved = jnp.roll(noise, (1, -2, 1), axis=(0, 1, 2))
    jitter = 0.3 * jax.random.normal(jax.random.fold_in(key, 29), (DEPTH, HEIGHT, WIDTH), jnp.float32)
    return (moved + jitter) * envelope


def scatter_about(stream_key, shape, width, reach, kind=jnp.bfloat16):
    entries = jax.random.normal(stream_key, shape, jnp.float32) * width
    return jnp.minimum(jnp.maximum(entries, -reach), reach).astype(kind)


def setup_inputs(seed: int = 0) -> dict:
    seeds = jax.random.split(jax.random.key(seed), 10)
    return {
        "fixed_image": draw_fixed_image(jax.random.fold_in(seeds[9], 71), 0),
        "moving_image": draw_moving_image(jax.random.fold_in(seeds[9], 71), 0),
        "conv_one": scatter_about(seeds[2], (C, 1, 3, 3, 3), 27 ** -0.5, 1.25, jnp.float32),
        "gain_one": jnp.clip(1.0 + 0.18 * jax.random.normal(seeds[3], (C,), jnp.float32), 0.1, 1.9),
        "shift_one": scatter_about(seeds[4], (C,), 0.5, 3.0, jnp.float32),
        "conv_two": scatter_about(seeds[5], (27, C * C), (27 * C) ** -0.5, 0.15625),
        "gain_two": jnp.clip(1.0 + 0.18 * jax.random.normal(seeds[6], (C,), jnp.float32), 0.1, 1.9),
        "shift_two": scatter_about(seeds[7], (C,), 0.5, 3.0, jnp.float32),
        "sharpness": jnp.clip(jnp.exp(jax.random.uniform(seeds[8], (1,), jnp.float32, math.log(1.0), math.log(4.0))), 1.0, 4.0),
    }


def convolve(field, kernel):
    return lax.conv_general_dilated(field, kernel, (1, 1, 1), [(1, 1), (1, 1), (1, 1)], dimension_numbers=('NCDHW', 'OIDHW', 'NCDHW'), precision=lax.Precision.HIGHEST)

def kernel_two(flat_kernel):
    return jnp.transpose(flat_kernel.reshape(3, 3, 3, C, C), (4, 3, 0, 1, 2))

def instance_norm(raw, gain, shift):
    mean_val = lax.optimization_barrier(jnp.mean(raw, axis=(2, 3, 4), keepdims=True))
    mean_sq = lax.optimization_barrier(jnp.mean(raw * raw, axis=(2, 3, 4), keepdims=True))
    scaled = (raw - mean_val) * lax.rsqrt(mean_sq - mean_val * mean_val + 1e-05)
    scaled = scaled * gain[None, :, None, None, None] + shift[None, :, None, None, None]
    return jax.nn.leaky_relu(scaled, 0.01).astype(jnp.bfloat16)

def reference(fixed_image, moving_image, conv_one, gain_one, shift_one, conv_two, gain_two, shift_two, sharpness):
    both_images = jnp.stack([fixed_image, moving_image])[:, None].astype(jnp.float32)
    first_raw = convolve(both_images, conv_one.astype(jnp.float32))
    first_feat = instance_norm(first_raw, gain_one, shift_one)
    second_raw = convolve(first_feat.astype(jnp.float32), kernel_two(conv_two).astype(jnp.float32))
    features = instance_norm(second_raw, gain_two, shift_two)
    fixed_feat = features[0].astype(jnp.float32)
    padded = jnp.pad(features[1], ((0, 0), (RADIUS, RADIUS), (RADIUS, RADIUS), (RADIUS, RADIUS)))
    span = 2 * RADIUS + 1
    factor = sharpness[0] / C

    def step(state, offset):
        running_max, running_sum, running_vec = state
        depth_shift = (offset // (span * span)).astype(jnp.int32)
        height_shift = (offset // span % span).astype(jnp.int32)
        width_shift = (offset % span).astype(jnp.int32)
        window = lax.dynamic_slice(padded, (jnp.int32(0), depth_shift, height_shift, width_shift), (C, DEPTH, HEIGHT, WIDTH))
        difference = fixed_feat - window.astype(jnp.float32)
        scores = -factor * lax.optimization_barrier(jnp.sum(difference * difference, axis=0))
        new_max = jnp.maximum(running_max, scores)
        keep = jnp.exp(running_max - new_max)
        weights = jnp.exp(scores - new_max)
        vector = jnp.stack([depth_shift, height_shift, width_shift]).astype(jnp.float32) - RADIUS
        running_sum = running_sum * keep + weights
        running_vec = running_vec * keep[None] + weights[None] * vector[:, None, None, None]
        return ((new_max, running_sum, running_vec), None)
    start = (jnp.full((DEPTH, HEIGHT, WIDTH), -jnp.inf, jnp.float32), jnp.zeros((DEPTH, HEIGHT, WIDTH), jnp.float32), jnp.zeros((3, DEPTH, HEIGHT, WIDTH), jnp.float32))
    final, _ = lax.scan(step, start, jnp.arange(span * span * span, dtype=jnp.int32))
    return final[2] / final[1][None]
```

```python
import functools
import jax
import jax.numpy as jnp
from jax import lax
from jax.experimental import pallas as pl
from jax.experimental.pallas import tpu as pltpu
from jax.sharding import PartitionSpec as P

RADIUS = 3
TILE = 8
F32 = jnp.float32
BF16 = jnp.bfloat16
FAR = -1e30
LOG2E = 1.4426950408889634


def leaky(v):
    return jnp.maximum(v, 0.01 * v)


def block_swap(rows):
    rows = list(rows)
    lane = lax.broadcasted_iota(jnp.int32, rows[0].shape, 1)
    for bit in range(4):
        step = 1 << bit
        low = (lane // (TILE * step)) % 2 == 0
        for q in range(16):
            if q & step:
                continue
            a, c = rows[q], rows[q + step]
            rows[q] = jnp.where(low, a, pltpu.roll(c, TILE * step, 1))
            rows[q + step] = jnp.where(low, pltpu.roll(a, 128 - TILE * step, 1), c)
    return rows


def match_kernel(normalize, slab, strip, mov_ref, fix_ref, coef_ref, place_ref, sharp_ref, out_ref, even, odd, fixed, score, found):
    ch = fix_ref.shape[1]
    tall, wide = slab + 2 * RADIUS, strip + 2 * RADIUS
    groups = slab // 4
    span = 4 + 2 * RADIUS
    z0, y0 = place_ref[0], place_ref[1]
    zn, yn = place_ref[2], place_ref[3]

    def feature(raw, scan):
        if not normalize:
            return raw.astype(F32)
        v = raw * coef_ref[2 * scan] + coef_ref[2 * scan + 1]
        return leaky(v).astype(BF16).astype(F32)

    row = lax.broadcasted_iota(jnp.int32, (128, 128), 0)
    col = lax.broadcasted_iota(jnp.int32, (128, 128), 1)
    onehot_x = jnp.where(col == 64 + row % 16, 1.0, 0.0)
    sub = lax.broadcasted_iota(jnp.int32, (64, 128), 0)

    def plane(z, _):
        for y in range(wide):
            f = feature(mov_ref[z, :, y * 128:(y + 1) * 128], 1)
            zz, yy = z0 + z - RADIUS, y0 + y - RADIUS
            inside = (zz >= 0) & (zz < zn) & (yy >= 0) & (yy < yn)
            f = jnp.where(inside, f, 0.0)
            norm = jnp.sum(f * f, axis=0, keepdims=True)
            hi = norm.astype(BF16).astype(F32)
            mid = (norm - hi).astype(BF16).astype(F32)
            low = norm - hi - mid
            extra = jnp.where(sub == 48, hi, jnp.where(sub == 49, mid, jnp.where(sub == 50, low, 0.0)))
            t = jnp.concatenate([f, extra], axis=0).T
            ones = jnp.where((col == 64 + 16 + y) | (col == 64 + 32 + z), 1.0, onehot_x)
            even[z, y] = (jnp.where(row >= 4, pltpu.roll(t, 4, 0), 0.0) + ones).astype(BF16)
            odd[z, y] = (jnp.where(row < 124, pltpu.roll(t, 124, 0), 0.0) + ones).astype(BF16)
        return _

    lax.fori_loop(0, tall, plane, 0)

    k = lax.broadcasted_iota(jnp.int32, (64, 128 * groups), 0)
    lane = lax.broadcasted_iota(jnp.int32, (64, 128 * groups), 1)
    fx, fy, fz = lane % 8, (lane // 8) % 4, lane // 32
    span_x = jnp.abs(k - fx - 4)
    span_y = jnp.abs(k - 16 - fy - 3)
    span_z = jnp.abs(k - 32 - fz - 3)
    apart = jnp.where(k < 16, span_x, jnp.where(k < 32, span_y, jnp.where(k < 48, span_z, 0)))
    tail = jnp.where(apart > RADIUS, FAR, 0.0)
    tail = jnp.where((k >= 48) & (k < 51), -0.5, tail).astype(BF16)
    for j in range(16):
        fixed[j, 64:128, :] = tail
    for g in range(groups):
        for part in range(ch // 16):
            rows = []
            for q in range(16):
                raw = fix_ref[4 * g + q // 4, part * 16:(part + 1) * 16, (q % 4) * 128:(q % 4 + 1) * 128]
                if normalize:
                    v = raw * coef_ref[0, part * 16:(part + 1) * 16] + coef_ref[1, part * 16:(part + 1) * 16]
                    rows.append(leaky(v).astype(BF16).astype(F32))
                else:
                    rows.append(raw.astype(F32))
            for j, v in enumerate(block_swap(rows)):
                fixed[j, part * 16:(part + 1) * 16, g * 128:(g + 1) * 128] = v.astype(BF16)

    factor = sharp_ref[0] * (2.0 * LOG2E / ch)
    count = wide * 16
    lane1 = lax.broadcasted_iota(jnp.int32, (1, 128), 1)
    x_in, y_in, z_in = lane1 % 8, (lane1 // 8) % 4, lane1 // 32
    pos = lax.broadcasted_iota(jnp.int32, (16, 128), 0).astype(F32)

    def tiles(m, _):
        for parity, held in enumerate((even, odd)):
            j = 2 * m + parity
            weights = fixed[j]
            peak = [jnp.full((8, 128), -3e38, F32) for _g in range(groups)]
            for z in range(tall):
                items = held[z, :, pl.ds(pl.multiple_of(16 * m, 16), 16), :].reshape(count, 128)
                users = [g for g in range(groups) if 4 * g <= z < 4 * g + span]
                s = jnp.dot(items, weights[:, users[0] * 128:(users[-1] + 1) * 128], preferred_element_type=F32)
                for i, g in enumerate(users):
                    part = s[:, i * 128:(i + 1) * 128]
                    score[g, z - 4 * g] = part
                    peak[g] = jnp.maximum(peak[g], jnp.max(part.reshape(count // 8, 8, 128), axis=0))
            for g in range(groups):
                top = jnp.max(peak[g], axis=0, keepdims=True) * factor
                run = jnp.zeros((count, 128), F32)
                acc = jnp.zeros((count, 128), F32)
                for z in range(span - 1, -1, -1):
                    run = run + jnp.exp2(score[g, z] * factor - top)
                    if z:
                        acc = acc + run
                acc_z = jnp.sum(acc, axis=0, keepdims=True)
                by_y = run.reshape(wide, 16, 128)
                by_x = jnp.sum(by_y, axis=0)
                total = jnp.sum(by_x, axis=0, keepdims=True)
                acc_x = jnp.sum(by_x * pos, axis=0, keepdims=True)
                acc_y = jnp.zeros((8, 128), F32)
                part_run = jnp.zeros((8, 128), F32)
                for y in range(wide - 1, 0, -1):
                    part_run = part_run + by_y[y, 0:8] + by_y[y, 8:16]
                    acc_y = acc_y + part_run
                acc_y = jnp.sum(acc_y, axis=0, keepdims=True)
                inv = 1.0 / total
                dz = acc_z * inv - (z_in + RADIUS).astype(F32)
                dy = acc_y * inv - (y_in + RADIUS).astype(F32)
                dx = acc_x * inv - (x_in + 4).astype(F32)
                found[g, j] = jnp.concatenate([dz, dy, dx, jnp.zeros((5, 128), F32)], axis=0)
        return _

    lax.fori_loop(0, 8, tiles, 0)
    for g in range(groups):
        for q, v in enumerate(block_swap([found[g, j] for j in range(16)])):
            for comp in range(3):
                out_ref[comp, 4 * g + q // 4, pl.ds(q % 4, 1), :] = v[comp:comp + 1]


def match(moving, fixed, coef, place, sharpness, slab, strip, normalize):
    tall, wide = slab + 2 * RADIUS, strip + 2 * RADIUS
    groups = slab // 4
    vm = pl.BlockSpec(memory_space=pltpu.VMEM)
    sm = pl.BlockSpec(memory_space=pltpu.SMEM)
    return pl.pallas_call(
        functools.partial(match_kernel, normalize, slab, strip),
        out_shape=jax.ShapeDtypeStruct((3, slab, strip, 128), F32),
        in_specs=[vm, vm, vm, sm, sm],
        out_specs=vm,
        scratch_shapes=[
            pltpu.VMEM((tall, wide, 128, 128), BF16),
            pltpu.VMEM((tall, wide, 128, 128), BF16),
            pltpu.VMEM((16, 128, 128 * groups), BF16),
            pltpu.VMEM((groups, 4 + 2 * RADIUS, wide * 16, 128), F32),
            pltpu.VMEM((groups, 16, 8, 128), F32),
        ],
        compiler_params=pltpu.CompilerParams(vmem_limit_bytes=48 * 1024 * 1024),
        name="match",
    )(moving, fixed, coef, place, sharpness)


def extended(array, sides, width):
    for axis, dim in sides:
        size, length = (lax.axis_size(axis), array.shape[dim])
        up = [(i, (i + 1) % size) for i in range(size - 1)]
        down = [(j, i) for i, j in up]
        last = lax.slice_in_dim(array, length - width, length, axis=dim)
        first = lax.slice_in_dim(array, 0, width, axis=dim)
        before = lax.ppermute(last, axis, up)
        after = lax.ppermute(first, axis, down)
        array = jnp.concatenate([before, array, after], axis=dim)
    return array


def convolve_valid(field, kernel, precise):
    return lax.conv_general_dilated(
        field,
        kernel,
        (1, 1, 1),
        "VALID",
        dimension_numbers=("NCDHW", "OIDHW", "NCDHW"),
        precision=precise,
        preferred_element_type=jnp.float32,
    )


def widen_last(field, amount):
    spec = [(0, 0)] * (field.ndim - 1) + [(amount, amount)]
    return jnp.pad(field, spec)


def normalized(raw, totals, squares, cell_count, gain, shift):
    mean_val = totals / cell_count
    mean_sq = squares / cell_count
    inv_dev = lax.rsqrt(mean_sq - mean_val * mean_val + 1e-05)
    scale_all = (inv_dev * gain[None, :])[:, :, None, None, None]
    offset_all = (shift[None, :] - mean_val * inv_dev * gain[None, :])[:, :, None, None, None]
    return jax.nn.leaky_relu(raw * scale_all + offset_all, 0.01).astype(jnp.bfloat16)


def local(
    fixed_image,
    moving_image,
    conv_one,
    gain_one,
    shift_one,
    conv_two,
    gain_two,
    shift_two,
    sharpness,
):
    slab_cells, strip_cells, width_cells = fixed_image.shape
    channels = gain_one.shape[0]
    cell_count = float(
        slab_cells * strip_cells * width_cells * lax.axis_size("depth") * lax.axis_size("height")
    )
    both_images = jnp.stack([fixed_image, moving_image])
    highest = lax.Precision.HIGHEST
    kernel_second = jnp.transpose(conv_two.reshape(3, 3, 3, channels, channels), (4, 3, 0, 1, 2))
    widened = extended(both_images, (("depth", 1), ("height", 2)), 1)
    widened = widen_last(widened, 1)
    first_raw = convolve_valid(widened[:, None], conv_one, highest)
    totals, squares = lax.psum(
        (jnp.sum(first_raw, axis=(2, 3, 4)), jnp.sum(first_raw * first_raw, axis=(2, 3, 4))),
        ("depth", "height"),
    )
    first_feat = normalized(first_raw, totals, squares, cell_count, gain_one, shift_one)
    first_wide = extended(first_feat, (("depth", 2), ("height", 3)), 1)
    first_wide = widen_last(first_wide, 1)
    second_raw = convolve_valid(first_wide, kernel_second, None)
    totals_two, squares_two = lax.psum(
        (jnp.sum(second_raw, axis=(2, 3, 4)), jnp.sum(second_raw * second_raw, axis=(2, 3, 4))),
        ("depth", "height"),
    )
    features = normalized(second_raw, totals_two, squares_two, cell_count, gain_two, shift_two)
    moving = extended(features[1], (("depth", 1), ("height", 2)), RADIUS)
    tall, wide = slab_cells + 2 * RADIUS, strip_cells + 2 * RADIUS
    moving = jnp.transpose(moving, (1, 0, 2, 3)).reshape(tall, channels, wide * width_cells)
    fixed = jnp.transpose(features[0], (1, 0, 2, 3)).reshape(slab_cells, channels, strip_cells * width_cells)
    place = jnp.stack([
        lax.axis_index("depth") * slab_cells,
        lax.axis_index("height") * strip_cells,
        jnp.int32(slab_cells * lax.axis_size("depth")),
        jnp.int32(strip_cells * lax.axis_size("height")),
    ]).astype(jnp.int32)
    coef = jnp.zeros((4, channels, 128), jnp.float32)
    return match(moving, fixed, coef, place, sharpness, slab_cells, strip_cells, False)


def solution(mesh):
    placed = (
        P("depth", "height", None),
        P("depth", "height", None),
        P(),
        P(),
        P(),
        P(),
        P(),
        P(),
        P(),
    )
    return jax.shard_map(
        local,
        mesh=mesh,
        in_specs=placed,
        out_specs=P(None, "depth", "height", None),
        check_vma=False,
    )
```

```python
import functools

import jax
import jax.numpy as jnp
import numpy as np
from jax import lax
from jax.experimental import pallas as pl
from jax.experimental.pallas import tpu as pltpu
from jax.sharding import PartitionSpec as P

RADIUS = 3
TILE = 8
F32 = jnp.float32
BF16 = jnp.bfloat16
FAR = -1e30
LOG2E = 1.4426950408889634
NUM = (((1,), (0,)), ((), ()))
AXES = ("depth", "height")


def leaky(v):
    return jnp.maximum(v, 0.01 * v)


def pair_table():
    axis_types = {}
    for k in range(3):
        for l in range(3):
            if k == l:
                axis_types[k, l] = {1: 0, 2: 1, 0: 2}[k]
            else:
                axis_types[k, l] = {1: 3, -1: 4, 2: 5, -2: 6}[l - k]
    table = np.zeros((729, 256), np.float32)
    taps = [(a, b, c) for a in range(3) for b in range(3) for c in range(3)]
    for i, k in enumerate(taps):
        for j, l in enumerate(taps):
            p, q = (k, l) if l[0] >= k[0] else (l, k)
            inner = axis_types[p[1], q[1]] * 7 + axis_types[p[2], q[2]]
            if p[0] != q[0]:
                table[i * 27 + j, (2 + q[0] - p[0]) * 49 + inner] += 1
            else:
                table[i * 27 + j, inner] += 1
                if p[0] == 2:
                    table[i * 27 + j, 49 + inner] -= 1
                if p[0] == 0:
                    table[i * 27 + j, 98 + inner] -= 1
    return table


def front_kernel(nd, nh, slab, strip, own_ref, other_ref, taps_ref, pairs_ref, two_ref, par_ref, place_ref,
                 mov_ref, fix_ref, sums_ref, img, bank_hi, bank_lo, gram, pieces, toep, plane_hi, plane_lo, feat_m, feat_f):
    zn, yn = nd * slab, nh * strip
    z0, y0, core = place_ref[0], place_ref[1], place_ref[4]
    count = float(zn * yn * 128)
    lane8 = lax.broadcasted_iota(jnp.int32, (8, 128), 1)
    sub8 = lax.broadcasted_iota(jnp.int32, (8, 128), 0)

    img[...] = jnp.zeros(img.shape, F32)
    for slot, src in enumerate((own_ref, other_ref)):
        scan = core if slot == 0 else 1 - core

        def gather(i, _):
            d, p = i // (nh // 2), i % (nh // 2)
            one = d * nh + 2 * p
            at = pl.multiple_of(8 + 8 * p, 8)
            for z in range(slab):
                both = jnp.concatenate([src[one, strip * z:strip * (z + 1)], src[one + 1, strip * z:strip * (z + 1)]], axis=0)
                img[scan, 5 + slab * d + z, pl.ds(at, 8), :] = both
            return _

        lax.fori_loop(0, nd * nh // 2, gather, 0)

    base = taps_ref[...]
    spot = lax.broadcasted_iota(jnp.int32, base.shape, 1)
    base_hi = base.astype(BF16).astype(F32)
    base = jnp.where((spot >= 144) & (spot < 288), (base - base_hi).astype(BF16).astype(F32), base_hi)
    for yo in range(12):
        toep[64 * yo:64 * yo + 64, :] = (pltpu.roll(base, yo, 1) if yo else base).astype(BF16)

    row_y = lax.broadcasted_iota(jnp.int32, (yn, 128), 0)
    step_rows = 256
    par_t = [jnp.broadcast_to(par_ref[i:i + 1, :], (128, 128)).T for i in range(2)]
    gain, shift = par_t[0][0:64], par_t[1][0:64]

    def statistics(scan):
        def build(z, _):
            at = pl.multiple_of(z * yn, yn)
            for ty in range(7):
                move = (0, 0, 0, 1, -1, 2, -2)[ty]
                v = img[scan, 5 + z, 8 + move:8 + move + yn, :]
                if ty == 1:
                    v = jnp.where(row_y == 0, 0.0, v)
                if ty == 2:
                    v = jnp.where(row_y == yn - 1, 0.0, v)
                hi = v.astype(BF16)
                bank_hi[pl.ds(at, yn), 128 * ty:128 * ty + 128] = hi
                bank_lo[pl.ds(at, yn), 128 * ty:128 * ty + 128] = (v - hi.astype(F32)).astype(BF16)
            return _

        lax.fori_loop(0, zn, build, 0)
        zero = jnp.zeros((2 * yn, 896), BF16)
        bank_hi[zn * yn:(zn + 2) * yn, :] = zero
        bank_lo[zn * yn:(zn + 2) * yn, :] = zero

        def product(at, length, far):
            a_hi = bank_hi[pl.ds(at, length), 0:128]
            a_lo = bank_lo[pl.ds(at, length), 0:128]
            b_hi = bank_hi[pl.ds(at + far, length), :]
            b_lo = bank_lo[pl.ds(at + far, length), :]
            left = jnp.concatenate([a_hi, a_hi, a_lo], axis=0)
            right = jnp.concatenate([b_hi, b_lo, b_hi], axis=0)
            return lax.dot_general(left, right, (((0,), (0,)), ((), ())), preferred_element_type=F32)

        gram[...] = jnp.zeros(gram.shape, F32)

        def chunk(i, _):
            at = pl.multiple_of(i * step_rows, step_rows)
            for far in range(3):
                gram[(0, 3, 4)[far]] += product(at, step_rows, far * yn)
            return _

        lax.fori_loop(0, zn * yn // step_rows, chunk, 0)
        gram[1] = product(0, yn, 0)
        gram[2] = product((zn - 1) * yn, yn, 0)

        def diagonals(tz, _):
            for ty in range(7):
                blk = gram[tz, :, 128 * ty:128 * ty + 128]
                halves = []
                for odd in range(2):
                    acc = jnp.zeros((8, 128), F32)
                    for m in range(8):
                        i = 2 * m + odd
                        acc = jnp.where((lane8 + 4 - 8 * odd) // 16 == m, blk[8 * i:8 * i + 8], acc)
                    halves.append(acc)
                for tx in range(7):
                    move = (0, 0, 0, 1, -1, 2, -2)[tx]
                    total = jnp.zeros((8, 128), F32)
                    for odd in range(2):
                        hit = (lane8 - sub8 - move - 8 * odd + 16) % 16 == 0
                        total = total + jnp.where(hit, halves[odd], 0.0)
                    if tx == 1:
                        total = jnp.where(lane8 == 0, 0.0, total)
                    if tx == 2:
                        total = jnp.where(lane8 == 127, 0.0, total)
                    pieces[pl.ds(pl.multiple_of(tz * 392 + (ty * 7 + tx) * 8, 8), 8), :] = total
            return _

        lax.fori_loop(0, 5, diagonals, 0)

        def add(z, total):
            return total + img[scan, 5 + z, 8:8 + yn, :]

        whole = lax.fori_loop(0, zn, add, jnp.zeros((yn, 128), F32))
        first, last = img[scan, 5, 8:8 + yn, :], img[scan, 4 + zn, 8:8 + yn, :]
        for kz in range(3):
            plane = (whole - last, whole, whole - first)[kz]
            for ky in range(3):
                v = plane
                if ky == 0:
                    v = jnp.where(row_y == yn - 1, 0.0, v)
                if ky == 2:
                    v = jnp.where(row_y == 0, 0.0, v)
                v = jnp.sum(v.reshape(yn // 8, 8, 128), axis=0)
                for kx in range(3):
                    w = v
                    if kx == 0:
                        w = jnp.where(lane8 == 127, 0.0, w)
                    if kx == 2:
                        w = jnp.where(lane8 == 0, 0.0, w)
                    at = 2048 + (kz * 9 + ky * 3 + kx) * 8
                    pieces[at:at + 8, :] = w
        pieces[1960:2048, :] = jnp.zeros((88, 128), F32)
        pieces[2264:2304, :] = jnp.zeros((40, 128), F32)
        rows = pieces[pl.ds(0, 288, stride=8), :]
        for s in range(1, 8):
            rows = rows + pieces[pl.ds(s, 288, stride=8), :]
        second = lax.dot_general(pairs_ref[:, 0:256], rows[0:256], NUM, precision=lax.Precision.HIGHEST, preferred_element_type=F32)
        mean = lax.dot_general(pairs_ref[:, 256:288], rows[256:288], NUM, precision=lax.Precision.HIGHEST, preferred_element_type=F32)
        mean = jnp.sum(mean, axis=1, keepdims=True) / count
        second = jnp.sum(second, axis=1, keepdims=True) / count
        scale = lax.rsqrt(second - mean * mean + 1e-05) * gain
        return scale, shift - mean * scale

    lane = lax.broadcasted_iota(jnp.int32, (16, 128), 1)
    lane64 = lax.broadcasted_iota(jnp.int32, (64, 128), 1)
    half = (y0 // strip) % 2

    def encode(scan, planes, rows, near, feat, out):
        scale, offset = statistics(scan)
        low = pl.multiple_of((y0 // 8) * 8, 8)

        def load(i, _):
            v = img[scan, z0 + 5 - near - 1 + i, pl.ds(low, 24), :]
            v = pltpu.roll(v, 24 - (8 - near - 1) - 4 * half, 0)[0:16]
            before = jnp.where(lane == 0, 0.0, pltpu.roll(v, 1, 1))
            after = jnp.where(lane == 127, 0.0, pltpu.roll(v, 127, 1))
            v = jnp.concatenate([before, v, after], axis=0)
            hi = v.astype(BF16)
            plane_hi[i] = hi
            plane_lo[i] = (v - hi.astype(F32)).astype(BF16)
            return _

        lax.fori_loop(0, planes + 2, load, 0)

        def first(i, _):
            sides = []
            for u in range(2):
                hi = plane_hi[pl.ds(2 * i + u, 3)].reshape(144, 128)
                lo = plane_lo[pl.ds(2 * i + u, 3)].reshape(144, 128)
                sides.append(jnp.concatenate([hi, hi, lo, jnp.zeros((80, 128), BF16)], axis=0))
            raw = jnp.dot(toep[0:64 * rows, :], jnp.concatenate(sides, axis=1), preferred_element_type=F32)
            for u in range(2):
                z = z0 - near + 2 * i + u
                for yo in range(rows):
                    y = y0 - near + yo
                    v = leaky(raw[64 * yo:64 * yo + 64, 128 * u:128 * u + 128] * scale + offset)
                    v = jnp.where((z >= 0) & (z < zn) & (y >= 0) & (y < yn), v, 0.0)
                    feat[2 * i + u, :, 128 * yo:128 * yo + 128] = v.astype(BF16)
            return _

        lax.fori_loop(0, planes // 2, first, 0)
        wide = rows - 2
        rim = near - 1

        def second(z, state):
            total, square = state
            taps = [feat[z + a, :, 128 * b:128 * (b + wide)] for a in range(3) for b in range(3)]
            raw = jnp.dot(two_ref[...], jnp.concatenate(taps, axis=0), preferred_element_type=F32)
            mine = jnp.where((z >= rim) & (z < rim + slab), 1.0, 0.0)
            for y in range(wide):
                cut = slice(128 * y, 128 * y + 128)
                before = jnp.where(lane64 == 0, 0.0, pltpu.roll(raw[0:64, cut], 1, 1))
                after = jnp.where(lane64 == 127, 0.0, pltpu.roll(raw[128:192, cut], 127, 1))
                v = before + raw[64:128, cut] + after
                out[z, :, cut] = v
                if rim <= y < rim + strip:
                    total = total + v * mine
                    square = square + v * v * mine
            return total, square

        return lax.fori_loop(0, planes - 2, second, (jnp.zeros((64, 128), F32), jnp.zeros((64, 128), F32)))

    f_sum, f_square = encode(0, slab + 2, strip + 2, 1, feat_f, fix_ref)
    m_sum, m_square = encode(1, slab + 8, strip + 8, 4, feat_m, mov_ref)
    sums_ref[0:1, :] = jnp.sum(jnp.concatenate([f_sum, m_sum], axis=0).T, axis=0, keepdims=True)
    sums_ref[1:2, :] = jnp.sum(jnp.concatenate([f_square, m_square], axis=0).T, axis=0, keepdims=True)


def front(own, other, taps, pairs, two, par, place, nd, nh, slab, strip):
    zn, yn = nd * slab, nh * strip
    vm = pl.BlockSpec(memory_space=pltpu.VMEM)
    sm = pl.BlockSpec(memory_space=pltpu.SMEM)
    return pl.pallas_call(
        functools.partial(front_kernel, nd, nh, slab, strip),
        out_shape=(
            jax.ShapeDtypeStruct((slab + 6, 64, (strip + 6) * 128), F32),
            jax.ShapeDtypeStruct((slab, 64, strip * 128), F32),
            jax.ShapeDtypeStruct((2, 128), F32),
        ),
        in_specs=[vm] * 6 + [sm],
        out_specs=(vm, vm, vm),
        scratch_shapes=[
            pltpu.VMEM((2, zn + 10, yn + 24, 128), F32),
            pltpu.VMEM(((zn + 2) * yn, 896), BF16),
            pltpu.VMEM(((zn + 2) * yn, 896), BF16),
            pltpu.VMEM((5, 128, 896), F32),
            pltpu.VMEM((2304, 128), F32),
            pltpu.VMEM((768, 512), BF16),
            pltpu.VMEM((slab + 10, 48, 128), BF16),
            pltpu.VMEM((slab + 10, 48, 128), BF16),
            pltpu.VMEM((slab + 8, 64, (strip + 8) * 128), BF16),
            pltpu.VMEM((slab + 2, 64, (strip + 2) * 128), BF16),
        ],
        compiler_params=pltpu.CompilerParams(vmem_limit_bytes=56 * 1024 * 1024),
        name="front",
    )(own, other, taps, pairs, two, par, place)


def parameters(conv_one, gain_one, shift_one, conv_two, gain_two, shift_two):
    w = conv_one.reshape(64, 3, 3, 3)
    base = jnp.pad(jnp.transpose(w, (0, 1, 3, 2)), ((0, 0), (0, 0), (0, 0), (0, 13))).reshape(64, 144)
    base = jnp.concatenate([base, base, base, jnp.zeros((64, 80), F32)], axis=1)
    flat = conv_one.reshape(64, 27)
    products = (flat[:, :, None] * flat[:, None, :]).reshape(64, 729)
    quad = jnp.dot(products, pair_table(), precision=lax.Precision.HIGHEST)
    pairs = jnp.concatenate([quad, flat, jnp.zeros((64, 5), F32)], axis=1)
    two = conv_two.reshape(3, 3, 3, 64, 64).transpose(2, 4, 0, 1, 3).reshape(192, 576)
    par = jnp.stack([jnp.concatenate([v, v]) for v in (gain_one, shift_one, gain_two, shift_two)])
    return base, pairs, two, par


def block_swap(rows):
    rows = list(rows)
    lane = lax.broadcasted_iota(jnp.int32, rows[0].shape, 1)
    for bit in range(4):
        step = 1 << bit
        low = (lane // (TILE * step)) % 2 == 0
        for q in range(16):
            if q & step:
                continue
            a, c = rows[q], rows[q + step]
            rows[q] = jnp.where(low, a, pltpu.roll(c, TILE * step, 1))
            rows[q + step] = jnp.where(low, pltpu.roll(a, 128 - TILE * step, 1), c)
    return rows


def match_kernel(slab, strip, mov_ref, fix_ref, sums_ref, par_ref, place_ref, sharp_ref, out_ref, even, odd, fixed, score, found):
    ch = fix_ref.shape[1]
    tall, wide = slab + 2 * RADIUS, strip + 2 * RADIUS
    groups = slab // 4
    span = 4 + 2 * RADIUS
    z0, y0 = place_ref[0], place_ref[1]
    zn, yn = place_ref[2], place_ref[3]

    sums = jnp.sum(sums_ref[...], axis=0) / (zn * yn * 128).astype(F32)
    mean, square = sums[0:1], sums[1:2]
    scale = lax.rsqrt(square - mean * mean + 1e-05) * par_ref[2:3]
    offset = par_ref[3:4] - mean * scale
    scale = jnp.broadcast_to(scale, (128, 128)).T
    offset = jnp.broadcast_to(offset, (128, 128)).T

    def feature(raw, scan):
        v = raw * scale[64 * scan:64 * scan + 64] + offset[64 * scan:64 * scan + 64]
        return leaky(v).astype(BF16).astype(F32)

    row = lax.broadcasted_iota(jnp.int32, (128, 128), 0)
    col = lax.broadcasted_iota(jnp.int32, (128, 128), 1)
    onehot_x = jnp.where(col == 64 + row % 16, 1.0, 0.0)
    sub = lax.broadcasted_iota(jnp.int32, (64, 128), 0)

    def plane(z, _):
        for y in range(wide):
            f = feature(mov_ref[z, :, y * 128:(y + 1) * 128], 1)
            zz, yy = z0 + z - RADIUS, y0 + y - RADIUS
            inside = (zz >= 0) & (zz < zn) & (yy >= 0) & (yy < yn)
            f = jnp.where(inside, f, 0.0)
            norm = jnp.sum(f * f, axis=0, keepdims=True)
            hi = norm.astype(BF16).astype(F32)
            mid = (norm - hi).astype(BF16).astype(F32)
            low = norm - hi - mid
            extra = jnp.where(sub == 48, hi, jnp.where(sub == 49, mid, jnp.where(sub == 50, low, 0.0)))
            t = jnp.concatenate([f, extra], axis=0).T
            ones = jnp.where((col == 64 + 16 + y) | (col == 64 + 32 + z), 1.0, onehot_x)
            even[z, y] = (jnp.where(row >= 4, pltpu.roll(t, 4, 0), 0.0) + ones).astype(BF16)
            odd[z, y] = (jnp.where(row < 124, pltpu.roll(t, 124, 0), 0.0) + ones).astype(BF16)
        return _

    lax.fori_loop(0, tall, plane, 0)

    k = lax.broadcasted_iota(jnp.int32, (64, 128 * groups), 0)
    lane = lax.broadcasted_iota(jnp.int32, (64, 128 * groups), 1)
    fx, fy, fz = lane % 8, (lane // 8) % 4, lane // 32
    span_x = jnp.abs(k - fx - 4)
    span_y = jnp.abs(k - 16 - fy - 3)
    span_z = jnp.abs(k - 32 - fz - 3)
    apart = jnp.where(k < 16, span_x, jnp.where(k < 32, span_y, jnp.where(k < 48, span_z, 0)))
    tail = jnp.where(apart > RADIUS, FAR, 0.0)
    tail = jnp.where((k >= 48) & (k < 51), -0.5, tail).astype(BF16)
    for j in range(16):
        fixed[j, 64:128, :] = tail
    for g in range(groups):
        for part in range(ch // 16):
            rows = []
            for q in range(16):
                raw = fix_ref[4 * g + q // 4, part * 16:(part + 1) * 16, (q % 4) * 128:(q % 4 + 1) * 128]
                at = slice(part * 16, part * 16 + 16)
                rows.append(leaky(raw * scale[at] + offset[at]).astype(BF16).astype(F32))
            for j, v in enumerate(block_swap(rows)):
                fixed[j, part * 16:(part + 1) * 16, g * 128:(g + 1) * 128] = v.astype(BF16)

    factor = sharp_ref[0] * (2.0 * LOG2E / ch)
    count = wide * 16
    lane1 = lax.broadcasted_iota(jnp.int32, (1, 128), 1)
    x_in, y_in, z_in = lane1 % 8, (lane1 // 8) % 4, lane1 // 32
    pos = lax.broadcasted_iota(jnp.int32, (16, 128), 0).astype(F32)

    def tiles(m, _):
        for parity, held in enumerate((even, odd)):
            j = 2 * m + parity
            weights = fixed[j]
            peak = [jnp.full((8, 128), -3e38, F32) for _g in range(groups)]
            for z in range(tall):
                items = held[z, :, pl.ds(pl.multiple_of(16 * m, 16), 16), :].reshape(count, 128)
                users = [g for g in range(groups) if 4 * g <= z < 4 * g + span]
                s = jnp.dot(items, weights[:, users[0] * 128:(users[-1] + 1) * 128], preferred_element_type=F32)
                for i, g in enumerate(users):
                    part = s[:, i * 128:(i + 1) * 128]
                    score[g, z - 4 * g] = part
                    peak[g] = jnp.maximum(peak[g], jnp.max(part.reshape(count // 8, 8, 128), axis=0))
            for g in range(groups):
                top = jnp.max(peak[g], axis=0, keepdims=True) * factor
                run = jnp.zeros((count, 128), F32)
                acc = jnp.zeros((count, 128), F32)
                for z in range(span - 1, -1, -1):
                    run = run + jnp.exp2(score[g, z] * factor - top)
                    if z:
                        acc = acc + run
                acc_z = jnp.sum(acc, axis=0, keepdims=True)
                by_y = run.reshape(wide, 16, 128)
                by_x = jnp.sum(by_y, axis=0)
                total = jnp.sum(by_x, axis=0, keepdims=True)
                acc_x = jnp.sum(by_x * pos, axis=0, keepdims=True)
                acc_y = jnp.zeros((8, 128), F32)
                part_run = jnp.zeros((8, 128), F32)
                for y in range(wide - 1, 0, -1):
                    part_run = part_run + by_y[y, 0:8] + by_y[y, 8:16]
                    acc_y = acc_y + part_run
                acc_y = jnp.sum(acc_y, axis=0, keepdims=True)
                inv = 1.0 / total
                dz = acc_z * inv - (z_in + RADIUS).astype(F32)
                dy = acc_y * inv - (y_in + RADIUS).astype(F32)
                dx = acc_x * inv - (x_in + 4).astype(F32)
                found[g, j] = jnp.concatenate([dz, dy, dx, jnp.zeros((5, 128), F32)], axis=0)
        return _

    lax.fori_loop(0, 8, tiles, 0)
    for g in range(groups):
        for q, v in enumerate(block_swap([found[g, j] for j in range(16)])):
            for comp in range(3):
                out_ref[comp, 4 * g + q // 4, pl.ds(q % 4, 1), :] = v[comp:comp + 1]


def match(moving, fixed, sums, par, place, sharpness, slab, strip):
    tall, wide = slab + 2 * RADIUS, strip + 2 * RADIUS
    groups = slab // 4
    vm = pl.BlockSpec(memory_space=pltpu.VMEM)
    sm = pl.BlockSpec(memory_space=pltpu.SMEM)
    return pl.pallas_call(
        functools.partial(match_kernel, slab, strip),
        out_shape=jax.ShapeDtypeStruct((3, slab, strip, 128), F32),
        in_specs=[vm, vm, vm, vm, sm, sm],
        out_specs=vm,
        scratch_shapes=[
            pltpu.VMEM((tall, wide, 128, 128), BF16),
            pltpu.VMEM((tall, wide, 128, 128), BF16),
            pltpu.VMEM((16, 128, 128 * groups), BF16),
            pltpu.VMEM((groups, 4 + 2 * RADIUS, wide * 16, 128), F32),
            pltpu.VMEM((groups, 16, 8, 128), F32),
        ],
        compiler_params=pltpu.CompilerParams(vmem_limit_bytes=48 * 1024 * 1024),
        name="match",
    )(moving, fixed, sums, par, place, sharpness)


def exchange(fixed_image, moving_image):
    depth, height = lax.axis_size("depth"), lax.axis_size("height")
    slab, strip, width = fixed_image.shape
    both = jnp.stack([fixed_image, moving_image]).reshape(2, slab * strip, width)
    sent = jnp.broadcast_to(both[None, :, None], (depth // 2, 2, height) + both.shape[1:])
    own = lax.all_to_all(sent.reshape((depth * height,) + both.shape[1:]), AXES, 0, 0)
    other = lax.ppermute(own, "depth", [(i, i ^ 1) for i in range(depth)])
    return own, other


def local(fixed_image, moving_image, conv_one, gain_one, shift_one, conv_two, gain_two, shift_two, sharpness):
    depth, height = lax.axis_size("depth"), lax.axis_size("height")
    slab, strip, _ = fixed_image.shape
    own, other = exchange(fixed_image, moving_image)
    base, pairs, two, par = parameters(conv_one, gain_one, shift_one, conv_two, gain_two, shift_two)
    row, column = lax.axis_index("depth"), lax.axis_index("height")
    place = jnp.stack([row * slab, column * strip, slab * depth, strip * height, row % 2]).astype(jnp.int32)
    moving, fixed, sums = front(own, other, base, pairs, two, par, place, depth, height, slab, strip)
    sent = jnp.broadcast_to(sums[None], (depth * height,) + sums.shape)
    sums = lax.all_to_all(sent, AXES, 0, 0)
    return match(moving, fixed, sums, par, place, sharpness, slab, strip)


def solution(mesh):
    image = P("depth", "height", None)
    return jax.shard_map(
        local,
        mesh=mesh,
        in_specs=(image, image) + (P(),) * 7,
        out_specs=P(None, "depth", "height", None),
        check_vma=False,
    )
```

```python
import functools

import jax
import jax.numpy as jnp
import numpy as np
from jax import lax
from jax.experimental import pallas as pl
from jax.experimental.pallas import tpu as pltpu
from jax.sharding import PartitionSpec as P

RADIUS = 3
TILE = 8
F32 = jnp.float32
BF16 = jnp.bfloat16
FAR = -1e30
LOG2E = 1.4426950408889634
NUM = (((1,), (0,)), ((), ()))
AXES = ("depth", "height")


def leaky(v):
    return jnp.maximum(v, 0.01 * v)


def lag_list(far):
    return [(y, x) for y in range(-2, 3) for x in range(-2, 3) if (far, y, x) >= (0, 0, 0)]


def lag_index():
    keys = [("a", "a", far, y, x, "a") for far in range(3) for y, x in lag_list(far)]
    keys += [(e, "a", 0, y, x, "a") for e in "fl" for y, x in lag_list(0)]
    keys += [("a", e, far, 0, x, "a") for e in "fl" for far in range(3) for y, x in lag_list(far) if y == 0]
    keys += [(d, e, 0, 0, x, "a") for d in "fl" for e in "fl" for y, x in lag_list(0) if y == 0]
    keys += [k[:5] + (e,) for e in "fl" for k in list(keys) if k[4] == 0]
    return {k: i for i, k in enumerate(keys)}


LAGS = lag_index()


def pair_table():
    table = np.zeros((729, 256), np.float32)
    taps = [(a, b, c) for a in range(3) for b in range(3) for c in range(3)]
    for i, k in enumerate(taps):
        for j, l in enumerate(taps):
            p, q = (k, l) if l >= k else (l, k)
            lag = tuple(v - u for u, v in zip(p, q))
            kinds = [[("a", 1)] + ([("f" if u == 2 else "l", -1)] if u == v != 1 else []) for u, v in zip(p, q)]
            for d, sd in kinds[0]:
                for h, sh in kinds[1]:
                    for w, sw in kinds[2]:
                        table[i * 27 + j, LAGS[(d, h) + lag + (w,)]] += sd * sh * sw
    return table


def moments_kernel(nd, nh, slab, strip, own_ref, pairs_ref, par_ref, out_ref, img, slid, pieces):
    zn, yn = nd * slab, nh * strip
    count = float(zn * yn * 128)
    lane8 = lax.broadcasted_iota(jnp.int32, (8, 128), 1)
    sub8 = lax.broadcasted_iota(jnp.int32, (8, 128), 0)
    row_y = lax.broadcasted_iota(jnp.int32, (yn, 128), 0)
    side = lax.broadcasted_iota(jnp.int32, (yn, 128), 1)
    gain, shift = [jnp.broadcast_to(par_ref[i:i + 1, :], (128, 128)).T[0:64] for i in range(2)]

    img[0:2] = jnp.zeros((2, yn + 16, 128), F32)
    img[:, 0:8, :] = jnp.zeros((zn + 2, 8, 128), F32)
    img[:, 8 + yn:16 + yn, :] = jnp.zeros((zn + 2, 8, 128), F32)
    slid[:, :, 0:8, :] = jnp.zeros((4, zn, 8, 128), F32)
    slid[:, :, 8 + yn:16 + yn, :] = jnp.zeros((4, zn, 8, 128), F32)

    def gather(d, _):
        for p in range(nh // 2):
            pair = own_ref[pl.ds(d * nh + 2 * p, 2)]
            for z in range(slab):
                both = jnp.concatenate([pair[0, strip * z:strip * (z + 1)], pair[1, strip * z:strip * (z + 1)]], axis=0)
                img[2 + slab * d + z, 8 + 8 * p:16 + 8 * p, :] = both
        return _

    lax.fori_loop(0, nd, gather, 0)

    def slide(i, _):
        at = 4 * i
        for u in range(4):
            v = img[2 + at + u, 8:8 + yn]
            for n, move in enumerate((-2, -1, 1, 2)):
                kept = (side + move >= 0) & (side + move < 128)
                slid[n, at + u, 8:8 + yn] = jnp.where(kept, pltpu.roll(v, (128 - move) % 128, 1), 0.0)
        return _

    lax.fori_loop(0, zn // 4, slide, 0)

    def other(z, y, x):
        if x == 0:
            return img[2 + z, y:y + 8, :]
        return slid[x + 2 if x < 0 else x + 1, z, y:y + 8, :]

    def put(key, v):
        at = 8 * LAGS[key]
        pieces[at:at + 8, :] = v
        if key[4] == 0:
            for e, end in (("f", 0), ("l", 127)):
                at = 8 * LAGS[key[:5] + (e,)]
                pieces[at:at + 8, :] = jnp.where(lane8 == end, v, 0.0)

    def products(z, y, lags, state, fars):
        state = [list(v) for v in state]
        for i in range(yn // 8):
            held = {far: img[2 + z - far, 8 + 8 * i:16 + 8 * i, :] for far in fars}
            moved = {x: other(z, 8 + 8 * i + y, x) for x in range(-2, 3)}
            part = 0 if y or 0 < i < yn // 8 - 1 else 1 if i == 0 else 2
            for n, (far, x) in enumerate(lags):
                if far in fars:
                    state[part][n] = state[part][n] + held[far] * moved[x]
        return tuple(tuple(v) for v in state)

    def record(d, y, lags, state, fars):
        for n, (far, x) in enumerate(lags):
            if far not in fars:
                continue
            if y == 0:
                put((d, "a", far, y, x, "a"), state[0][n] + state[1][n] + state[2][n])
                put((d, "f", far, y, x, "a"), jnp.where(sub8 == 0, state[1][n], 0.0))
                put((d, "l", far, y, x, "a"), jnp.where(sub8 == 7, state[2][n], 0.0))
            else:
                put((d, "a", far, y, x, "a"), state[0][n])

    nothing = jnp.zeros((8, 128), F32)
    pieces[8 * len(LAGS):2048, :] = jnp.zeros((2048 - 8 * len(LAGS), 128), F32)
    for y in range(-2, 3):
        lags = [(far, x) for far in range(3) for x in range(-2, 3) if (far, y, x) >= (0, 0, 0)]
        empty = ((nothing,) * len(lags),) * (1 if y else 3)
        state = lax.fori_loop(0, zn, lambda z, state: products(z, y, lags, state, (0, 1, 2)), empty)
        record("a", y, lags, state, (0, 1, 2))
        if y >= 0:
            for d, z in (("f", 0), ("l", zn - 1)):
                record(d, y, lags, products(z, y, lags, empty, (0,)), (0,))

    def add(z, total):
        return total + img[2 + z, 8:8 + yn, :]

    whole = lax.fori_loop(0, zn, add, jnp.zeros((yn, 128), F32))
    first, last = img[2, 8:8 + yn, :], img[1 + zn, 8:8 + yn, :]
    for kz in range(3):
        plane = (whole - last, whole, whole - first)[kz]
        for ky in range(3):
            v = plane
            if ky == 0:
                v = jnp.where(row_y == yn - 1, 0.0, v)
            if ky == 2:
                v = jnp.where(row_y == 0, 0.0, v)
            v = jnp.sum(v.reshape(yn // 8, 8, 128), axis=0)
            for kx in range(3):
                w = v
                if kx == 0:
                    w = jnp.where(lane8 == 127, 0.0, w)
                if kx == 2:
                    w = jnp.where(lane8 == 0, 0.0, w)
                at = 2048 + (kz * 9 + ky * 3 + kx) * 8
                pieces[at:at + 8, :] = w
    pieces[2264:2304, :] = jnp.zeros((40, 128), F32)
    rows = pieces[pl.ds(0, 288, stride=8), :]
    for s in range(1, 8):
        rows = rows + pieces[pl.ds(s, 288, stride=8), :]
    second = lax.dot_general(pairs_ref[:, 0:256], rows[0:256], NUM, precision=lax.Precision.HIGHEST, preferred_element_type=F32)
    mean = lax.dot_general(pairs_ref[:, 256:288], rows[256:288], NUM, precision=lax.Precision.HIGHEST, preferred_element_type=F32)
    mean = jnp.sum(mean, axis=1, keepdims=True) / count
    second = jnp.sum(second, axis=1, keepdims=True) / count
    scale = lax.rsqrt(second - mean * mean + 1e-05) * gain
    out_ref[0:64, :] = jnp.broadcast_to(scale, (64, 128))
    out_ref[64:128, :] = jnp.broadcast_to(shift - mean * scale, (64, 128))


def moments(own, pairs, par, nd, nh, slab, strip):
    zn, yn = nd * slab, nh * strip
    vm = pl.BlockSpec(memory_space=pltpu.VMEM)
    return pl.pallas_call(
        functools.partial(moments_kernel, nd, nh, slab, strip),
        out_shape=jax.ShapeDtypeStruct((128, 128), F32),
        in_specs=[vm] * 3,
        out_specs=vm,
        scratch_shapes=[
            pltpu.VMEM((zn + 2, yn + 16, 128), F32),
            pltpu.VMEM((4, zn, yn + 16, 128), F32),
            pltpu.VMEM((2304, 128), F32),
        ],
        compiler_params=pltpu.CompilerParams(vmem_limit_bytes=60 * 1024 * 1024),
        cost_estimate=pl.CostEstimate(flops=10 ** 9, bytes_accessed=10 ** 6, transcendentals=0),
        name="moments",
    )(own, pairs, par)


def convolved(weights, feat, z, first, wide, lane64):
    taps = [feat[z + a, :, 128 * (f + b):128 * (f + b + n)] for a in range(3) for b in range(3) for f, n in [(first, wide)]]
    return joined(weights, jnp.concatenate(taps, axis=0), wide, lane64)


def joined(weights, taps, wide, lane64):
    raw = jnp.dot(weights, taps, preferred_element_type=F32)
    rows = []
    for y in range(wide):
        cut = slice(128 * y, 128 * y + 128)
        before = jnp.where(lane64 == 0, 0.0, pltpu.roll(raw[0:64, cut], 1, 1))
        after = jnp.where(lane64 == 127, 0.0, pltpu.roll(raw[128:192, cut], 127, 1))
        rows.append(before + raw[64:128, cut] + after)
    return rows


def encode_kernel(nd, nh, slab, strip, own_ref, other_ref, mine_ref, theirs_ref, taps_ref, two_ref, place_ref,
                  feat_ref, mov_ref, fix_ref, sums_ref, win, toep, plane_hi, plane_lo, feat_m, feat_f, sem):
    zn, yn = nd * slab, nh * strip
    z0, y0, core = place_ref[0], place_ref[1], place_ref[4]
    row, column = place_ref[5], place_ref[6]

    base = taps_ref[...]
    spot = lax.broadcasted_iota(jnp.int32, base.shape, 1)
    base_hi = base.astype(BF16).astype(F32)
    base = jnp.where((spot >= 144) & (spot < 288), (base - base_hi).astype(BF16).astype(F32), base_hi)
    for yo in range(strip + 8):
        toep[64 * yo:64 * yo + 64, :] = (pltpu.roll(base, yo, 1) if yo else base).astype(BF16)

    lane = lax.broadcasted_iota(jnp.int32, (16, 128), 1)
    lane64 = lax.broadcasted_iota(jnp.int32, (64, 128), 1)

    def encode(scan, planes, rows, near, feat):
        mine = core == scan
        for i in range(-1, 2):
            for j in range(-2, 3):
                d, h = row + i, column + j
                inside = (d >= 0) & (d < nd) & (h >= 0) & (h < nh)
                at = jnp.where(inside, d * nh + h, 0)
                block = jnp.where(mine, own_ref[at], other_ref[at])
                block = jnp.where(inside, block, 0.0)
                for z in range(slab):
                    win[slab * (i + 1) + z, strip * (j + 2):strip * (j + 3), :] = block[strip * z:strip * (z + 1)]
        for i in range(planes + 2):
            low = 8 - near - 1
            v = win[slab - near - 1 + i, low:low + 16, :]
            before = jnp.where(lane == 0, 0.0, pltpu.roll(v, 1, 1))
            after = jnp.where(lane == 127, 0.0, pltpu.roll(v, 127, 1))
            v = jnp.concatenate([before, v, after], axis=0)
            hi = v.astype(BF16)
            plane_hi[i] = hi
            plane_lo[i] = (v - hi.astype(F32)).astype(BF16)
        scale = jnp.where(mine, mine_ref[0:64], theirs_ref[0:64])
        offset = jnp.where(mine, mine_ref[64:128], theirs_ref[64:128])

        def first(i, _):
            sides = []
            for u in range(2):
                hi = plane_hi[pl.ds(2 * i + u, 3)].reshape(144, 128)
                lo = plane_lo[pl.ds(2 * i + u, 3)].reshape(144, 128)
                sides.append(jnp.concatenate([hi, hi, lo, jnp.zeros((80, 128), BF16)], axis=0))
            raw = jnp.dot(toep[0:64 * rows, :], jnp.concatenate(sides, axis=1), preferred_element_type=F32)
            for u in range(2):
                z = z0 - near + 2 * i + u
                for yo in range(rows):
                    y = y0 - near + yo
                    v = leaky(raw[64 * yo:64 * yo + 64, 128 * u:128 * u + 128] * scale + offset)
                    v = jnp.where((z >= 0) & (z < zn) & (y >= 0) & (y < yn), v, 0.0)
                    feat[2 * i + u, :, 128 * yo:128 * yo + 128] = v.astype(BF16)
            return _

        lax.fori_loop(0, planes // 2, first, 0)

    def second(feat, rim, out):
        def plane(z, state):
            total, square = state
            for y, v in enumerate(convolved(two_ref[...], feat, rim + z, rim, strip, lane64)):
                out[z, :, 128 * y:128 * y + 128] = v
                total = total + v
                square = square + v * v
            return total, square

        return lax.fori_loop(0, slab, plane, (jnp.zeros((64, 128), F32), jnp.zeros((64, 128), F32)))

    encode(1, slab + 8, strip + 8, 4, feat_m)
    send = pltpu.make_async_copy(feat_m, feat_ref, sem)
    send.start()
    m_sum, m_square = second(feat_m, 3, mov_ref)
    encode(0, slab + 2, strip + 2, 1, feat_f)
    f_sum, f_square = second(feat_f, 0, fix_ref)
    total = jnp.sum(jnp.concatenate([f_sum, m_sum], axis=0).T, axis=0, keepdims=True)
    square = jnp.sum(jnp.concatenate([f_square, m_square], axis=0).T, axis=0, keepdims=True)
    both = jnp.concatenate([total, square], axis=0)
    sums_ref[...] = jnp.broadcast_to(both[None], sums_ref.shape)
    send.wait()


def encode(own, other, mine, theirs, taps, two, place, nd, nh, slab, strip):
    vm = pl.BlockSpec(memory_space=pltpu.VMEM)
    sm = pl.BlockSpec(memory_space=pltpu.SMEM)
    feat = (slab + 8, 64, (strip + 8) * 128)
    return pl.pallas_call(
        functools.partial(encode_kernel, nd, nh, slab, strip),
        out_shape=(
            jax.ShapeDtypeStruct(feat, BF16),
            jax.ShapeDtypeStruct((slab, 64, strip * 128), F32),
            jax.ShapeDtypeStruct((slab, 64, strip * 128), F32),
            jax.ShapeDtypeStruct((nd * nh, 2, 128), F32),
        ),
        in_specs=[vm] * 6 + [sm],
        out_specs=(pl.BlockSpec(memory_space=pl.ANY), vm, vm, vm),
        scratch_shapes=[
            pltpu.VMEM((3 * slab, 24, 128), F32),
            pltpu.VMEM((64 * (strip + 8), 512), BF16),
            pltpu.VMEM((slab + 10, 48, 128), BF16),
            pltpu.VMEM((slab + 10, 48, 128), BF16),
            pltpu.VMEM(feat, BF16),
            pltpu.VMEM((slab + 2, 64, (strip + 2) * 128), BF16),
            pltpu.SemaphoreType.DMA(()),
        ],
        compiler_params=pltpu.CompilerParams(vmem_limit_bytes=60 * 1024 * 1024),
        name="encode",
    )(own, other, mine, theirs, taps, two, place)


def rim_kernel(slab, strip, feat_ref, two_ref, out_ref, feat, out, in_sem, out_sem):
    lane64 = lax.broadcasted_iota(jnp.int32, (64, 128), 1)
    wide = strip + 6
    loads = [pltpu.make_async_copy(feat_ref.at[z], feat.at[z], in_sem.at[z]) for z in range(slab + 8)]
    for load in loads:
        load.start()

    def whole(z):
        for y, v in enumerate(convolved(two_ref[...], feat, z, 0, wide, lane64)):
            out[z, :, 128 * y:128 * y + 128] = v

    def store(z):
        return pltpu.make_async_copy(out.at[z], out_ref.at[z], out_sem.at[z])

    for load in loads[:3]:
        load.wait()
    for z in range(RADIUS):
        if z:
            loads[z + 2].wait()
        whole(z)
        store(z).start()

    def middle(z, _):
        pltpu.make_async_copy(feat_ref.at[z + 2], feat.at[z + 2], in_sem.at[z + 2]).wait()
        taps = []
        for a in range(3):
            for b in range(3):
                left = feat[z + a, :, 128 * b:128 * (b + 3)]
                right = feat[z + a, :, 128 * (strip + 3 + b):128 * (strip + 6 + b)]
                taps.append(jnp.concatenate([left, right], axis=1))
        for y, v in enumerate(joined(two_ref[...], jnp.concatenate(taps, axis=0), 6, lane64)):
            to = y if y < 3 else y + strip
            out[z, :, 128 * to:128 * to + 128] = v
        store(z).start()
        return _

    lax.fori_loop(RADIUS, RADIUS + slab, middle, 0)
    for z in range(RADIUS + slab, slab + 6):
        loads[z + 2].wait()
        whole(z)
        store(z).start()
    for z in range(slab + 6):
        store(z).wait()


def rim(feat, two, slab, strip):
    hbm = pl.BlockSpec(memory_space=pl.ANY)
    vm = pl.BlockSpec(memory_space=pltpu.VMEM)
    shape = (slab + 6, 64, (strip + 6) * 128)
    return pl.pallas_call(
        functools.partial(rim_kernel, slab, strip),
        out_shape=jax.ShapeDtypeStruct(shape, F32),
        in_specs=[hbm, vm],
        out_specs=hbm,
        scratch_shapes=[
            pltpu.VMEM(feat.shape, BF16),
            pltpu.VMEM(shape, F32),
            pltpu.SemaphoreType.DMA((slab + 8,)),
            pltpu.SemaphoreType.DMA((slab + 6,)),
        ],
        compiler_params=pltpu.CompilerParams(vmem_limit_bytes=60 * 1024 * 1024),
        cost_estimate=pl.CostEstimate(flops=6 * 10 ** 9, bytes_accessed=10 ** 7, transcendentals=0),
        name="rim",
    )(feat, two)


def parameters(conv_one, gain_one, shift_one, conv_two, gain_two, shift_two):
    w = conv_one.reshape(64, 3, 3, 3)
    base = jnp.pad(jnp.transpose(w, (0, 1, 3, 2)), ((0, 0), (0, 0), (0, 0), (0, 13))).reshape(64, 144)
    base = jnp.concatenate([base, base, base, jnp.zeros((64, 80), F32)], axis=1)
    flat = conv_one.reshape(64, 27)
    products = (flat[:, :, None] * flat[:, None, :]).reshape(64, 729)
    quad = jnp.dot(products, pair_table(), precision=lax.Precision.HIGHEST)
    pairs = jnp.concatenate([quad, flat, jnp.zeros((64, 5), F32)], axis=1)
    two = conv_two.reshape(3, 3, 3, 64, 64).transpose(2, 4, 0, 1, 3).reshape(192, 576)
    par = jnp.stack([jnp.concatenate([v, v]) for v in (gain_one, shift_one, gain_two, shift_two)])
    return base, pairs, two, par


def block_swap(rows):
    rows = list(rows)
    lane = lax.broadcasted_iota(jnp.int32, rows[0].shape, 1)
    for bit in range(4):
        step = 1 << bit
        low = (lane // (TILE * step)) % 2 == 0
        for q in range(16):
            if q & step:
                continue
            a, c = rows[q], rows[q + step]
            rows[q] = jnp.where(low, a, pltpu.roll(c, TILE * step, 1))
            rows[q + step] = jnp.where(low, pltpu.roll(a, 128 - TILE * step, 1), c)
    return rows


def match_kernel(slab, strip, rim_hbm, mov_hbm, fix_hbm, sums_ref, par_ref, place_ref, sharp_ref, out_ref,
                 rim_ref, mov_ref, fix_ref, even, odd, fixed, score, found, rim_sem, mov_sem, fix_sem):
    ch = fix_ref.shape[1]
    loads = [pltpu.make_async_copy(rim_hbm.at[z], rim_ref.at[z], rim_sem.at[z]) for z in range(slab + 2 * RADIUS)]
    load_mov = pltpu.make_async_copy(mov_hbm, mov_ref, mov_sem)
    load_fix = pltpu.make_async_copy(fix_hbm, fix_ref, fix_sem)
    for load in loads[:RADIUS] + [load_mov] + loads[RADIUS:] + [load_fix]:
        load.start()
    tall, wide = slab + 2 * RADIUS, strip + 2 * RADIUS
    groups = slab // 4
    span = 4 + 2 * RADIUS
    z0, y0 = place_ref[0], place_ref[1]
    zn, yn = place_ref[2], place_ref[3]

    sums = jnp.sum(sums_ref[...], axis=0) / (zn * yn * 128).astype(F32)
    mean, square = sums[0:1], sums[1:2]
    scale = lax.rsqrt(square - mean * mean + 1e-05) * par_ref[2:3]
    offset = par_ref[3:4] - mean * scale
    scale = jnp.broadcast_to(scale, (128, 128)).T
    offset = jnp.broadcast_to(offset, (128, 128)).T

    def feature(raw, scan):
        v = raw * scale[64 * scan:64 * scan + 64] + offset[64 * scan:64 * scan + 64]
        return leaky(v).astype(BF16).astype(F32)

    row = lax.broadcasted_iota(jnp.int32, (128, 128), 0)
    col = lax.broadcasted_iota(jnp.int32, (128, 128), 1)
    onehot_x = jnp.where(col == 64 + row % 16, 1.0, 0.0)
    sub = lax.broadcasted_iota(jnp.int32, (64, 128), 0)

    def plane(z, middle):
        pltpu.make_async_copy(rim_hbm.at[z], rim_ref.at[z], rim_sem.at[z]).wait()
        for y in range(wide):
            if middle and RADIUS <= y < RADIUS + strip:
                raw = mov_ref[z - RADIUS, :, (y - RADIUS) * 128:(y - RADIUS + 1) * 128]
            else:
                raw = rim_ref[z, :, y * 128:(y + 1) * 128]
            f = feature(raw, 1)
            zz, yy = z0 + z - RADIUS, y0 + y - RADIUS
            inside = (zz >= 0) & (zz < zn) & (yy >= 0) & (yy < yn)
            f = jnp.where(inside, f, 0.0)
            norm = jnp.sum(f * f, axis=0, keepdims=True)
            hi = norm.astype(BF16).astype(F32)
            mid = (norm - hi).astype(BF16).astype(F32)
            low = norm - hi - mid
            extra = jnp.where(sub == 48, hi, jnp.where(sub == 49, mid, jnp.where(sub == 50, low, 0.0)))
            t = jnp.concatenate([f, extra], axis=0).T
            ones = jnp.where((col == 64 + 16 + y) | (col == 64 + 32 + z), 1.0, onehot_x)
            even[z, y] = (jnp.where(row >= 4, pltpu.roll(t, 4, 0), 0.0) + ones).astype(BF16)
            odd[z, y] = (jnp.where(row < 124, pltpu.roll(t, 124, 0), 0.0) + ones).astype(BF16)

    def planes(low, high, middle):
        def step(z, _):
            plane(z, middle)
            return _
        lax.fori_loop(low, high, step, 0)

    planes(0, RADIUS, False)
    load_mov.wait()
    planes(RADIUS, RADIUS + slab, True)
    planes(RADIUS + slab, tall, False)
    load_fix.wait()

    k = lax.broadcasted_iota(jnp.int32, (64, 128 * groups), 0)
    lane = lax.broadcasted_iota(jnp.int32, (64, 128 * groups), 1)
    fx, fy, fz = lane % 8, (lane // 8) % 4, lane // 32
    span_x = jnp.abs(k - fx - 4)
    span_y = jnp.abs(k - 16 - fy - 3)
    span_z = jnp.abs(k - 32 - fz - 3)
    apart = jnp.where(k < 16, span_x, jnp.where(k < 32, span_y, jnp.where(k < 48, span_z, 0)))
    tail = jnp.where(apart > RADIUS, FAR, 0.0)
    tail = jnp.where((k >= 48) & (k < 51), -0.5, tail).astype(BF16)
    for j in range(16):
        fixed[j, 64:128, :] = tail
    for g in range(groups):
        for part in range(ch // 16):
            rows = []
            for q in range(16):
                raw = fix_ref[4 * g + q // 4, part * 16:(part + 1) * 16, (q % 4) * 128:(q % 4 + 1) * 128]
                at = slice(part * 16, part * 16 + 16)
                rows.append(leaky(raw * scale[at] + offset[at]).astype(BF16).astype(F32))
            for j, v in enumerate(block_swap(rows)):
                fixed[j, part * 16:(part + 1) * 16, g * 128:(g + 1) * 128] = v.astype(BF16)

    factor = sharp_ref[0] * (2.0 * LOG2E / ch)
    count = wide * 16
    lane1 = lax.broadcasted_iota(jnp.int32, (1, 128), 1)
    x_in, y_in, z_in = lane1 % 8, (lane1 // 8) % 4, lane1 // 32
    pos = lax.broadcasted_iota(jnp.int32, (16, 128), 0).astype(F32)

    def tiles(m, _):
        for parity, held in enumerate((even, odd)):
            j = 2 * m + parity
            weights = fixed[j]
            peak = [jnp.full((8, 128), -3e38, F32) for _g in range(groups)]
            for z in range(tall):
                items = held[z, :, pl.ds(pl.multiple_of(16 * m, 16), 16), :].reshape(count, 128)
                users = [g for g in range(groups) if 4 * g <= z < 4 * g + span]
                s = jnp.dot(items, weights[:, users[0] * 128:(users[-1] + 1) * 128], preferred_element_type=F32)
                for i, g in enumerate(users):
                    part = s[:, i * 128:(i + 1) * 128]
                    score[g, z - 4 * g] = part
                    peak[g] = jnp.maximum(peak[g], jnp.max(part.reshape(count // 8, 8, 128), axis=0))
            for g in range(groups):
                top = jnp.max(peak[g], axis=0, keepdims=True) * factor
                run = jnp.zeros((count, 128), F32)
                acc = jnp.zeros((count, 128), F32)
                for z in range(span - 1, -1, -1):
                    run = run + jnp.exp2(score[g, z] * factor - top)
                    if z:
                        acc = acc + run
                acc_z = jnp.sum(acc, axis=0, keepdims=True)
                by_y = run.reshape(wide, 16, 128)
                by_x = jnp.sum(by_y, axis=0)
                total = jnp.sum(by_x, axis=0, keepdims=True)
                acc_x = jnp.sum(by_x * pos, axis=0, keepdims=True)
                acc_y = jnp.zeros((8, 128), F32)
                part_run = jnp.zeros((8, 128), F32)
                for y in range(wide - 1, 0, -1):
                    part_run = part_run + by_y[y, 0:8] + by_y[y, 8:16]
                    acc_y = acc_y + part_run
                acc_y = jnp.sum(acc_y, axis=0, keepdims=True)
                inv = 1.0 / total
                dz = acc_z * inv - (z_in + RADIUS).astype(F32)
                dy = acc_y * inv - (y_in + RADIUS).astype(F32)
                dx = acc_x * inv - (x_in + 4).astype(F32)
                found[g, j] = jnp.concatenate([dz, dy, dx, jnp.zeros((5, 128), F32)], axis=0)
        return _

    lax.fori_loop(0, 8, tiles, 0)
    for g in range(groups):
        for q, v in enumerate(block_swap([found[g, j] for j in range(16)])):
            for comp in range(3):
                out_ref[comp, 4 * g + q // 4, pl.ds(q % 4, 1), :] = v[comp:comp + 1]


def match(around, moving, fixed, sums, par, place, sharpness, slab, strip):
    tall, wide = slab + 2 * RADIUS, strip + 2 * RADIUS
    groups = slab // 4
    vm = pl.BlockSpec(memory_space=pltpu.VMEM)
    sm = pl.BlockSpec(memory_space=pltpu.SMEM)
    hbm = pl.BlockSpec(memory_space=pl.ANY)
    return pl.pallas_call(
        functools.partial(match_kernel, slab, strip),
        out_shape=jax.ShapeDtypeStruct((3, slab, strip, 128), F32),
        in_specs=[hbm, hbm, hbm, vm, vm, sm, sm],
        out_specs=vm,
        scratch_shapes=[
            pltpu.VMEM(around.shape, F32),
            pltpu.VMEM(moving.shape, F32),
            pltpu.VMEM(fixed.shape, F32),
            pltpu.VMEM((tall, wide, 128, 128), BF16),
            pltpu.VMEM((tall, wide, 128, 128), BF16),
            pltpu.VMEM((16, 128, 128 * groups), BF16),
            pltpu.VMEM((groups, 4 + 2 * RADIUS, wide * 16, 128), F32),
            pltpu.VMEM((groups, 16, 8, 128), F32),
            pltpu.SemaphoreType.DMA((tall,)),
            pltpu.SemaphoreType.DMA(()),
            pltpu.SemaphoreType.DMA(()),
        ],
        compiler_params=pltpu.CompilerParams(vmem_limit_bytes=60 * 1024 * 1024),
        name="match",
    )(around, moving, fixed, sums, par, place, sharpness)


def gathered(fixed_image, moving_image):
    depth, height = lax.axis_size("depth"), lax.axis_size("height")
    slab, strip, width = fixed_image.shape
    both = jnp.stack([fixed_image, moving_image]).reshape(2, slab * strip, width)
    power = jnp.clip(jnp.floor(jnp.log2(jnp.max(jnp.abs(both), axis=(1, 2), keepdims=True))) - 13.0, -113.0, 113.0)
    scaled = (both * jnp.exp2(-power)).astype(jnp.float16)
    power = jnp.broadcast_to(power, (2, 8, width)).astype(jnp.float16)
    sent = jnp.concatenate([scaled, power], axis=1)
    sent = jnp.broadcast_to(sent[None, :, None], (depth // 2, 2, height) + sent.shape[1:])
    return lax.all_to_all(sent.reshape((depth * height,) + sent.shape[3:]), AXES, 0, 0)


def restored(blocks):
    power = jnp.exp2(blocks[:, -8:-7].astype(F32))
    return blocks[:, :-8].astype(F32) * power


def local(fixed_image, moving_image, conv_one, gain_one, shift_one, conv_two, gain_two, shift_two, sharpness):
    depth, height = lax.axis_size("depth"), lax.axis_size("height")
    slab, strip, _ = fixed_image.shape
    swap = [(i, i ^ 1) for i in range(depth)]
    blocks = gathered(fixed_image, moving_image)
    base, pairs, two, par = parameters(conv_one, gain_one, shift_one, conv_two, gain_two, shift_two)
    row, column = lax.axis_index("depth"), lax.axis_index("height")
    place = jnp.stack([row * slab, column * strip, slab * depth, strip * height, row % 2, row, column]).astype(jnp.int32)
    other = restored(lax.ppermute(blocks, "depth", swap))
    own = restored(blocks)
    mine = moments(own, pairs, par, depth, height, slab, strip)
    theirs = lax.ppermute(mine, "depth", swap)
    feat, moving, fixed, sums = encode(own, other, mine, theirs, base, two, place, depth, height, slab, strip)
    sums = lax.all_to_all(sums, AXES, 0, 0)
    around = rim(feat, two, slab, strip)
    return match(around, moving, fixed, sums, par, place, sharpness, slab, strip)


def solution(mesh):
    image = P("depth", "height", None)
    return jax.shard_map(
        local,
        mesh=mesh,
        in_specs=(image, image) + (P(),) * 7,
        out_specs=P(None, "depth", "height", None),
        check_vma=False,
    )
```

```python
import functools

import jax
import jax.numpy as jnp
import numpy as np
from jax import lax
from jax.experimental import pallas as pl
from jax.experimental.pallas import tpu as pltpu
from jax.sharding import PartitionSpec as P

RADIUS = 3
TILE = 8
F32 = jnp.float32
BF16 = jnp.bfloat16
FAR = -1e30
LOG2E = 1.4426950408889634
NUM = (((1,), (0,)), ((), ()))
AXES = ("depth", "height")


def leaky(v):
    return jnp.maximum(v, 0.01 * v)


def lag_list(far):
    return [(y, x) for y in range(-2, 3) for x in range(-2, 3) if (far, y, x) >= (0, 0, 0)]


def lag_index():
    keys = [("a", "a", far, y, x, "a") for far in range(3) for y, x in lag_list(far)]
    keys += [(e, "a", 0, y, x, "a") for e in "fl" for y, x in lag_list(0)]
    keys += [("a", e, far, 0, x, "a") for e in "fl" for far in range(3) for y, x in lag_list(far) if y == 0]
    keys += [(d, e, 0, 0, x, "a") for d in "fl" for e in "fl" for y, x in lag_list(0) if y == 0]
    keys += [k[:5] + (e,) for e in "fl" for k in list(keys) if k[4] == 0]
    return {k: i for i, k in enumerate(keys)}


LAGS = lag_index()


def pair_table():
    table = np.zeros((729, 256), np.float32)
    taps = [(a, b, c) for a in range(3) for b in range(3) for c in range(3)]
    for i, k in enumerate(taps):
        for j, l in enumerate(taps):
            p, q = (k, l) if l >= k else (l, k)
            lag = tuple(v - u for u, v in zip(p, q))
            kinds = [[("a", 1)] + ([("f" if u == 2 else "l", -1)] if u == v != 1 else []) for u, v in zip(p, q)]
            for d, sd in kinds[0]:
                for h, sh in kinds[1]:
                    for w, sw in kinds[2]:
                        table[i * 27 + j, LAGS[(d, h) + lag + (w,)]] += sd * sh * sw
    return table


def moments_kernel(nd, nh, slab, strip, own_ref, pairs_ref, par_ref, out_ref, img, slid, pieces):
    zn, yn = nd * slab, nh * strip
    count = float(zn * yn * 128)
    lane8 = lax.broadcasted_iota(jnp.int32, (8, 128), 1)
    sub8 = lax.broadcasted_iota(jnp.int32, (8, 128), 0)
    row_y = lax.broadcasted_iota(jnp.int32, (yn, 128), 0)
    side = lax.broadcasted_iota(jnp.int32, (yn, 128), 1)
    gain, shift = [jnp.broadcast_to(par_ref[i:i + 1, :], (128, 128)).T[0:64] for i in range(2)]

    img[0:2] = jnp.zeros((2, yn + 16, 128), F32)
    img[:, 0:8, :] = jnp.zeros((zn + 2, 8, 128), F32)
    img[:, 8 + yn:16 + yn, :] = jnp.zeros((zn + 2, 8, 128), F32)
    slid[:, :, 0:8, :] = jnp.zeros((4, zn, 8, 128), F32)
    slid[:, :, 8 + yn:16 + yn, :] = jnp.zeros((4, zn, 8, 128), F32)

    def gather(d, _):
        for p in range(nh // 2):
            pair = own_ref[pl.ds(d * nh + 2 * p, 2)]
            for z in range(slab):
                both = jnp.concatenate([pair[0, strip * z:strip * (z + 1)], pair[1, strip * z:strip * (z + 1)]], axis=0)
                img[2 + slab * d + z, 8 + 8 * p:16 + 8 * p, :] = both
        return _

    lax.fori_loop(0, nd, gather, 0)

    def slide(i, _):
        at = 4 * i
        for u in range(4):
            v = img[2 + at + u, 8:8 + yn]
            for n, move in enumerate((-2, -1, 1, 2)):
                kept = (side + move >= 0) & (side + move < 128)
                slid[n, at + u, 8:8 + yn] = jnp.where(kept, pltpu.roll(v, (128 - move) % 128, 1), 0.0)
        return _

    lax.fori_loop(0, zn // 4, slide, 0)

    def other(z, y, x):
        if x == 0:
            return img[2 + z, y:y + 8, :]
        return slid[x + 2 if x < 0 else x + 1, z, y:y + 8, :]

    def put(key, v):
        at = 8 * LAGS[key]
        pieces[at:at + 8, :] = v
        if key[4] == 0:
            for e, end in (("f", 0), ("l", 127)):
                at = 8 * LAGS[key[:5] + (e,)]
                pieces[at:at + 8, :] = jnp.where(lane8 == end, v, 0.0)

    def products(z, y, lags, state, fars):
        state = [list(v) for v in state]
        for i in range(yn // 8):
            held = {far: img[2 + z - far, 8 + 8 * i:16 + 8 * i, :] for far in fars}
            moved = {x: other(z, 8 + 8 * i + y, x) for x in range(-2, 3)}
            part = 0 if y or 0 < i < yn // 8 - 1 else 1 if i == 0 else 2
            for n, (far, x) in enumerate(lags):
                if far in fars:
                    state[part][n] = state[part][n] + held[far] * moved[x]
        return tuple(tuple(v) for v in state)

    def record(d, y, lags, state, fars):
        for n, (far, x) in enumerate(lags):
            if far not in fars:
                continue
            if y == 0:
                put((d, "a", far, y, x, "a"), state[0][n] + state[1][n] + state[2][n])
                put((d, "f", far, y, x, "a"), jnp.where(sub8 == 0, state[1][n], 0.0))
                put((d, "l", far, y, x, "a"), jnp.where(sub8 == 7, state[2][n], 0.0))
            else:
                put((d, "a", far, y, x, "a"), state[0][n])

    nothing = jnp.zeros((8, 128), F32)
    pieces[8 * len(LAGS):2048, :] = jnp.zeros((2048 - 8 * len(LAGS), 128), F32)
    for y in range(-2, 3):
        lags = [(far, x) for far in range(3) for x in range(-2, 3) if (far, y, x) >= (0, 0, 0)]
        empty = ((nothing,) * len(lags),) * (1 if y else 3)
        state = lax.fori_loop(0, zn, lambda z, state: products(z, y, lags, state, (0, 1, 2)), empty)
        record("a", y, lags, state, (0, 1, 2))
        if y >= 0:
            for d, z in (("f", 0), ("l", zn - 1)):
                record(d, y, lags, products(z, y, lags, empty, (0,)), (0,))

    def add(z, total):
        return total + img[2 + z, 8:8 + yn, :]

    whole = lax.fori_loop(0, zn, add, jnp.zeros((yn, 128), F32))
    first, last = img[2, 8:8 + yn, :], img[1 + zn, 8:8 + yn, :]
    for kz in range(3):
        plane = (whole - last, whole, whole - first)[kz]
        for ky in range(3):
            v = plane
            if ky == 0:
                v = jnp.where(row_y == yn - 1, 0.0, v)
            if ky == 2:
                v = jnp.where(row_y == 0, 0.0, v)
            v = jnp.sum(v.reshape(yn // 8, 8, 128), axis=0)
            for kx in range(3):
                w = v
                if kx == 0:
                    w = jnp.where(lane8 == 127, 0.0, w)
                if kx == 2:
                    w = jnp.where(lane8 == 0, 0.0, w)
                at = 2048 + (kz * 9 + ky * 3 + kx) * 8
                pieces[at:at + 8, :] = w
    pieces[2264:2304, :] = jnp.zeros((40, 128), F32)
    rows = pieces[pl.ds(0, 288, stride=8), :]
    for s in range(1, 8):
        rows = rows + pieces[pl.ds(s, 288, stride=8), :]
    second = lax.dot_general(pairs_ref[:, 0:256], rows[0:256], NUM, precision=lax.Precision.HIGHEST, preferred_element_type=F32)
    mean = lax.dot_general(pairs_ref[:, 256:288], rows[256:288], NUM, precision=lax.Precision.HIGHEST, preferred_element_type=F32)
    mean = jnp.sum(mean, axis=1, keepdims=True) / count
    second = jnp.sum(second, axis=1, keepdims=True) / count
    scale = lax.rsqrt(second - mean * mean + 1e-05) * gain
    out_ref[0:64, :] = jnp.broadcast_to(scale, (64, 128))
    out_ref[64:128, :] = jnp.broadcast_to(shift - mean * scale, (64, 128))


def moments(own, pairs, par, nd, nh, slab, strip):
    zn, yn = nd * slab, nh * strip
    vm = pl.BlockSpec(memory_space=pltpu.VMEM)
    return pl.pallas_call(
        functools.partial(moments_kernel, nd, nh, slab, strip),
        out_shape=jax.ShapeDtypeStruct((128, 128), F32),
        in_specs=[vm] * 3,
        out_specs=vm,
        scratch_shapes=[
            pltpu.VMEM((zn + 2, yn + 16, 128), F32),
            pltpu.VMEM((4, zn, yn + 16, 128), F32),
            pltpu.VMEM((2304, 128), F32),
        ],
        compiler_params=pltpu.CompilerParams(vmem_limit_bytes=40 * 1024 * 1024),
        cost_estimate=pl.CostEstimate(flops=10 ** 9, bytes_accessed=10 ** 6, transcendentals=0),
        name="moments",
    )(own, pairs, par)


def convolved(weights, feat, z, first, wide, lane64):
    taps = [feat[z + a, :, 128 * (f + b):128 * (f + b + n)] for a in range(3) for b in range(3) for f, n in [(first, wide)]]
    return joined(weights, jnp.concatenate(taps, axis=0), wide, lane64)


def joined(weights, taps, wide, lane64):
    raw = jnp.dot(weights, taps, preferred_element_type=F32)
    rows = []
    for y in range(wide):
        cut = slice(128 * y, 128 * y + 128)
        before = jnp.where(lane64 == 0, 0.0, pltpu.roll(raw[0:64, cut], 1, 1))
        after = jnp.where(lane64 == 127, 0.0, pltpu.roll(raw[128:192, cut], 127, 1))
        rows.append(before + raw[64:128, cut] + after)
    return rows


def banded(taps_ref, toep, rows):
    base = taps_ref[...]
    spot = lax.broadcasted_iota(jnp.int32, base.shape, 1)
    base_hi = base.astype(BF16).astype(F32)
    base = jnp.where((spot >= 144) & (spot < 288), (base - base_hi).astype(BF16).astype(F32), base_hi)
    for yo in range(rows):
        toep[64 * yo:64 * yo + 64, :] = (pltpu.roll(base, yo, 1) if yo else base).astype(BF16)


def first_layer(scans, slab, strip, near, group, nd, nh, own_ref, other_ref, mine_ref, theirs_ref, place_ref, win, toep, plane_hi, plane_lo, feat):
    planes, rows = slab + 2 * near, strip + 2 * near
    zn, yn = nd * slab, nh * strip
    z0, y0, core = place_ref[0], place_ref[1], place_ref[4]
    row, column = place_ref[5], place_ref[6]
    lane = lax.broadcasted_iota(jnp.int32, (16, 128), 1)
    reach = -(-(near + 1) // strip)
    for s, scan in enumerate(scans):
        mine = core == scan
        for i in range(-1, 2):
            for j in range(-reach, reach + 1):
                d, h = row + i, column + j
                inside = (d >= 0) & (d < nd) & (h >= 0) & (h < nh)
                at = jnp.where(inside, d * nh + h, 0)
                block = jnp.where(mine, own_ref[at], other_ref[at])
                block = jnp.where(inside, block, 0.0)
                for z in range(slab):
                    win[s, slab * (i + 1) + z, strip * (j + 2):strip * (j + 3), :] = block[strip * z:strip * (z + 1)]
        for i in range(planes + 2):
            low = 2 * strip - near - 1
            v = win[s, slab - near - 1 + i, low:low + 16, :]
            before = jnp.where(lane == 0, 0.0, pltpu.roll(v, 1, 1))
            after = jnp.where(lane == 127, 0.0, pltpu.roll(v, 127, 1))
            v = jnp.concatenate([before, v, after], axis=0)
            hi = v.astype(BF16)
            plane_hi[s, i] = hi
            plane_lo[s, i] = (v - hi.astype(F32)).astype(BF16)
    scales = [jnp.where(core == scan, mine_ref[0:64], theirs_ref[0:64]) for scan in scans]
    offsets = [jnp.where(core == scan, mine_ref[64:128], theirs_ref[64:128]) for scan in scans]

    def first(i, _):
        sides = []
        for s in range(len(scans)):
            for u in range(group):
                hi = plane_hi[s, pl.ds(group * i + u, 3)].reshape(144, 128)
                lo = plane_lo[s, pl.ds(group * i + u, 3)].reshape(144, 128)
                sides.append(jnp.concatenate([hi, hi, lo, jnp.zeros((80, 128), BF16)], axis=0))
        raw = jnp.dot(toep[0:64 * rows, :], jnp.concatenate(sides, axis=1), preferred_element_type=F32)
        for s in range(len(scans)):
            for u in range(group):
                z = z0 - near + group * i + u
                cut = slice(128 * (s * group + u), 128 * (s * group + u) + 128)
                for yo in range(rows):
                    y = y0 - near + yo
                    v = leaky(raw[64 * yo:64 * yo + 64, cut] * scales[s] + offsets[s])
                    v = jnp.where((z >= 0) & (z < zn) & (y >= 0) & (y < yn), v, 0.0)
                    to = 128 * (s * rows + yo)
                    feat[group * i + u, :, to:to + 128] = v.astype(BF16)
        return _

    lax.fori_loop(0, planes // group, first, 0)


def encode_kernel(nd, nh, slab, strip, own_ref, other_ref, mine_ref, theirs_ref, taps_ref, two_ref, place_ref,
                  mov_hbm, fix_hbm, sums_ref, win, toep, plane_hi, plane_lo, feat, mov_ref, fix_ref, mov_sem, fix_sem):
    rows = strip + 2
    banded(taps_ref, toep, rows)
    first_layer((0, 1), slab, strip, 1, 2, nd, nh, own_ref, other_ref, mine_ref, theirs_ref, place_ref, win, toep, plane_hi, plane_lo, feat)
    lane64 = lax.broadcasted_iota(jnp.int32, (64, 128), 1)
    zero = jnp.zeros((64, 128), F32)

    def stores(z):
        return (
            pltpu.make_async_copy(mov_ref.at[z], mov_hbm.at[z], mov_sem.at[z]),
            pltpu.make_async_copy(fix_ref.at[z], fix_hbm.at[z], fix_sem.at[z]),
        )

    def plane(z, state):
        state = list(state)
        taps = []
        for a in range(3):
            for b in range(3):
                cuts = [feat[z + a, :, 128 * (s * rows + b):128 * (s * rows + b + strip)] for s in range(2)]
                taps.append(jnp.concatenate(cuts, axis=1))
        for i, v in enumerate(joined(two_ref[...], jnp.concatenate(taps, axis=0), 2 * strip, lane64)):
            s, y = i // strip, i % strip
            (fix_ref, mov_ref)[s][z, :, 128 * y:128 * y + 128] = v
            state[s] = state[s] + v
            state[2 + s] = state[2 + s] + v * v
        for store in stores(z):
            store.start()
        return tuple(state)

    sums = lax.fori_loop(0, slab, plane, (zero,) * 4)
    total = jnp.sum(jnp.concatenate(sums[0:2], axis=0).T, axis=0, keepdims=True)
    square = jnp.sum(jnp.concatenate(sums[2:4], axis=0).T, axis=0, keepdims=True)
    both = jnp.concatenate([total, square], axis=0)
    sums_ref[...] = jnp.broadcast_to(both[None], sums_ref.shape)
    for z in range(slab):
        for store in stores(z):
            store.wait()


def encode(own, other, mine, theirs, taps, two, place, nd, nh, slab, strip):
    vm = pl.BlockSpec(memory_space=pltpu.VMEM)
    sm = pl.BlockSpec(memory_space=pltpu.SMEM)
    hbm = pl.BlockSpec(memory_space=pl.ANY)
    return pl.pallas_call(
        functools.partial(encode_kernel, nd, nh, slab, strip),
        out_shape=(
            jax.ShapeDtypeStruct((slab, 64, strip * 128), F32),
            jax.ShapeDtypeStruct((slab, 64, strip * 128), F32),
            jax.ShapeDtypeStruct((nd * nh, 2, 128), F32),
        ),
        in_specs=[vm] * 6 + [sm],
        out_specs=(hbm, hbm, vm),
        scratch_shapes=[
            pltpu.VMEM((2, 3 * slab, 24, 128), F32),
            pltpu.VMEM((64 * (strip + 2), 512), BF16),
            pltpu.VMEM((2, slab + 4, 48, 128), BF16),
            pltpu.VMEM((2, slab + 4, 48, 128), BF16),
            pltpu.VMEM((slab + 2, 64, 2 * (strip + 2) * 128), BF16),
            pltpu.VMEM((slab, 64, strip * 128), F32),
            pltpu.VMEM((slab, 64, strip * 128), F32),
            pltpu.SemaphoreType.DMA((slab,)),
            pltpu.SemaphoreType.DMA((slab,)),
        ],
        compiler_params=pltpu.CompilerParams(vmem_limit_bytes=60 * 1024 * 1024),
        name="encode",
    )(own, other, mine, theirs, taps, two, place)


def rim_kernel(nd, nh, slab, strip, own_ref, other_ref, mine_ref, theirs_ref, taps_ref, two_ref, place_ref,
               edge_ref, side_ref, win, toep, plane_hi, plane_lo, feat, edge, side, edge_sem, side_sem):
    lane64 = lax.broadcasted_iota(jnp.int32, (64, 128), 1)
    wide = strip + 6
    banded(taps_ref, toep, strip + 8)
    first_layer((1,), slab, strip, 4, 4, nd, nh, own_ref, other_ref, mine_ref, theirs_ref, place_ref, win, toep, plane_hi, plane_lo, feat)

    def store_edge(i):
        return pltpu.make_async_copy(edge.at[i], edge_ref.at[i], edge_sem.at[i])

    def store_side(i):
        return pltpu.make_async_copy(side.at[i], side_ref.at[i], side_sem.at[i])

    def whole(i, _):
        z = jnp.where(i < RADIUS, i, i + slab)
        for y, v in enumerate(convolved(two_ref[...], feat, z, 0, wide, lane64)):
            edge[i, :, 128 * y:128 * y + 128] = v
        store_edge(i).start()
        return _

    def middle(i, _):
        z = RADIUS + 2 * i
        taps = []
        for a in range(3):
            for b in range(3):
                cuts = [feat[z + u + a, :, 128 * (c + b):128 * (c + b + 3)] for u in range(2) for c in (0, strip + 3)]
                taps.append(jnp.concatenate(cuts, axis=1))
        for y, v in enumerate(joined(two_ref[...], jnp.concatenate(taps, axis=0), 12, lane64)):
            side[2 * i + y // 6, :, 128 * (y % 6):128 * (y % 6) + 128] = v
        store_side(2 * i).start()
        store_side(2 * i + 1).start()
        return _

    lax.fori_loop(0, 2 * RADIUS, whole, 0)
    lax.fori_loop(0, slab // 2, middle, 0)
    for i in range(2 * RADIUS):
        store_edge(i).wait()
    for i in range(slab):
        store_side(i).wait()


def rim(own, other, mine, theirs, taps, two, place, nd, nh, slab, strip):
    hbm = pl.BlockSpec(memory_space=pl.ANY)
    vm = pl.BlockSpec(memory_space=pltpu.VMEM)
    sm = pl.BlockSpec(memory_space=pltpu.SMEM)
    edge = (6, 64, (strip + 6) * 128)
    side = (slab, 64, 6 * 128)
    return pl.pallas_call(
        functools.partial(rim_kernel, nd, nh, slab, strip),
        out_shape=(jax.ShapeDtypeStruct(edge, F32), jax.ShapeDtypeStruct(side, F32)),
        in_specs=[vm] * 6 + [sm],
        out_specs=(hbm, hbm),
        scratch_shapes=[
            pltpu.VMEM((1, 3 * slab, 24, 128), F32),
            pltpu.VMEM((64 * (strip + 8), 512), BF16),
            pltpu.VMEM((1, slab + 10, 48, 128), BF16),
            pltpu.VMEM((1, slab + 10, 48, 128), BF16),
            pltpu.VMEM((slab + 8, 64, (strip + 8) * 128), BF16),
            pltpu.VMEM(edge, F32),
            pltpu.VMEM(side, F32),
            pltpu.SemaphoreType.DMA((6,)),
            pltpu.SemaphoreType.DMA((slab,)),
        ],
        compiler_params=pltpu.CompilerParams(vmem_limit_bytes=60 * 1024 * 1024),
        cost_estimate=pl.CostEstimate(flops=6 * 10 ** 9, bytes_accessed=10 ** 7, transcendentals=0),
        name="rim",
    )(own, other, mine, theirs, taps, two, place)


def parameters(conv_one, gain_one, shift_one, conv_two, gain_two, shift_two):
    w = conv_one.reshape(64, 3, 3, 3)
    base = jnp.pad(jnp.transpose(w, (0, 1, 3, 2)), ((0, 0), (0, 0), (0, 0), (0, 13))).reshape(64, 144)
    base = jnp.concatenate([base, base, base, jnp.zeros((64, 80), F32)], axis=1)
    flat = conv_one.reshape(64, 27)
    products = (flat[:, :, None] * flat[:, None, :]).reshape(64, 729)
    quad = jnp.dot(products, pair_table(), precision=lax.Precision.HIGHEST)
    pairs = jnp.concatenate([quad, flat, jnp.zeros((64, 5), F32)], axis=1)
    two = conv_two.reshape(3, 3, 3, 64, 64).transpose(2, 4, 0, 1, 3).reshape(192, 576)
    par = jnp.stack([jnp.concatenate([v, v]) for v in (gain_one, shift_one, gain_two, shift_two)])
    return base, pairs, two, par


def block_swap(rows):
    rows = list(rows)
    lane = lax.broadcasted_iota(jnp.int32, rows[0].shape, 1)
    for bit in range(4):
        step = 1 << bit
        low = (lane // (TILE * step)) % 2 == 0
        for q in range(16):
            if q & step:
                continue
            a, c = rows[q], rows[q + step]
            rows[q] = jnp.where(low, a, pltpu.roll(c, TILE * step, 1))
            rows[q + step] = jnp.where(low, pltpu.roll(a, 128 - TILE * step, 1), c)
    return rows


def match_kernel(slab, strip, edge_hbm, side_hbm, mov_hbm, fix_hbm, sums_ref, par_ref, place_ref, sharp_ref, out_ref,
                 edge_ref, side_ref, mov_ref, fix_ref, turned, even, odd, fixed, score, peak, found,
                 edge_sem, side_sem, mov_sem, fix_sem):
    ch = fix_ref.shape[1]
    load_fix = pltpu.make_async_copy(fix_hbm, fix_ref, fix_sem)

    def load_edge(i):
        return pltpu.make_async_copy(edge_hbm.at[i], edge_ref.at[i], edge_sem.at[i])

    def load_side(i):
        return pltpu.make_async_copy(side_hbm.at[i], side_ref.at[i], side_sem.at[i])

    def load_mov(i):
        return pltpu.make_async_copy(mov_hbm.at[i], mov_ref.at[i], mov_sem.at[i])

    for i in range(RADIUS):
        load_edge(i).start()
    tall, wide = slab + 2 * RADIUS, strip + 2 * RADIUS
    groups = slab // 4
    span = 4 + 2 * RADIUS
    z0, y0 = place_ref[0], place_ref[1]
    zn, yn = place_ref[2], place_ref[3]

    sums = jnp.sum(sums_ref[...], axis=0) / (zn * yn * 128).astype(F32)
    mean, square = sums[0:1], sums[1:2]
    scale = lax.rsqrt(square - mean * mean + 1e-05) * par_ref[2:3]
    offset = par_ref[3:4] - mean * scale
    scale = jnp.broadcast_to(scale, (128, 128)).T
    offset = jnp.broadcast_to(offset, (128, 128)).T

    def feature(raw, scan):
        v = raw * scale[64 * scan:64 * scan + 64] + offset[64 * scan:64 * scan + 64]
        return leaky(v).astype(BF16).astype(F32)

    row16 = lax.broadcasted_iota(jnp.int32, (16, 128), 0)
    col16 = lax.broadcasted_iota(jnp.int32, (16, 128), 1)
    onehot_x = jnp.where(col16 == 64 + row16, 1.0, 0.0)
    sub8 = lax.broadcasted_iota(jnp.int32, (8, 128), 0)
    blank = jnp.zeros((8, 128), F32)
    for i in range(2):
        turned[i, 0:8] = blank
        turned[i, 128:136] = blank

    def plane(z, middle):
        if middle:
            load_side(z - RADIUS).wait()
            load_mov(z - RADIUS).wait()
        else:
            at = jnp.where(z < RADIUS, z, z - slab)
            load_edge(at).wait()
        zz = z0 + z - RADIUS
        for y in range(wide):
            if not middle:
                raw = edge_ref[at, :, y * 128:(y + 1) * 128]
            elif RADIUS <= y < RADIUS + strip:
                raw = mov_ref[z - RADIUS, :, (y - RADIUS) * 128:(y - RADIUS + 1) * 128]
            else:
                c = y if y < RADIUS else y - strip
                raw = side_ref[z - RADIUS, :, c * 128:(c + 1) * 128]
            f = feature(raw, 1)
            yy = y0 + y - RADIUS
            f = jnp.where((zz >= 0) & (zz < zn) & (yy >= 0) & (yy < yn), f, 0.0)
            norm = jnp.sum(f * f, axis=0, keepdims=True)
            hi = norm.astype(BF16).astype(F32)
            mid = (norm - hi).astype(BF16).astype(F32)
            low = norm - hi - mid
            extra = jnp.where(sub8 == 0, hi, jnp.where(sub8 == 1, mid, jnp.where(sub8 == 2, low, 0.0)))
            t = jnp.concatenate([f] + [blank] * 6 + [extra, blank], axis=0).T
            turned[y % 2, 4:132] = t
            ones = jnp.where((col16 == 64 + 16 + y) | (col16 == 64 + 32 + z) | ((col16 >= 115) & (col16 < 118)), 1.0, onehot_x).astype(BF16)[None]
            even[z, y] = (turned[y % 2, 0:128].astype(BF16).reshape(8, 16, 128) + ones).reshape(128, 128)
            odd[z, y] = (turned[y % 2, 8:136].astype(BF16).reshape(8, 16, 128) + ones).reshape(128, 128)

    def before(z, _):
        load_side(z).start()
        load_mov(z).start()
        plane(z, False)
        return _

    def among(z, _):
        i = z - RADIUS

        @pl.when(i < slab - RADIUS)
        def more():
            load_side(i + RADIUS).start()
            load_mov(i + RADIUS).start()

        @pl.when(i >= slab - RADIUS)
        def last():
            load_edge(i - slab + 2 * RADIUS).start()

        @pl.when(i == slab - 1)
        def end():
            load_fix.start()

        plane(z, True)
        return _

    def after(z, _):
        plane(z, False)
        return _

    lax.fori_loop(0, RADIUS, before, 0)
    lax.fori_loop(RADIUS, RADIUS + slab, among, 0)
    lax.fori_loop(RADIUS + slab, tall, after, 0)
    load_fix.wait()

    k = lax.broadcasted_iota(jnp.int32, (64, 128 * groups), 0)
    lane = lax.broadcasted_iota(jnp.int32, (64, 128 * groups), 1)
    fx, fy, fz = lane % 8, (lane // 8) % 4, lane // 32
    span_x = jnp.abs(k - fx - 4)
    span_y = jnp.abs(k - 16 - fy - 3)
    span_z = jnp.abs(k - 32 - fz - 3)
    apart = jnp.where(k < 16, span_x, jnp.where(k < 32, span_y, jnp.where(k < 48, span_z, 0)))
    tail = jnp.where(apart > RADIUS, FAR, 0.0)
    tail = tail.astype(BF16)
    for j in range(16):
        fixed[j, 64:112, :] = tail[0:48]
    row16f = lax.broadcasted_iota(jnp.int32, (16, 128), 0)
    for g in range(groups):
        norms = [jnp.zeros((16, 128), F32)] * 16
        for part in range(ch // 16):
            rows = []
            for q in range(16):
                raw = fix_ref[4 * g + q // 4, part * 16:(part + 1) * 16, (q % 4) * 128:(q % 4 + 1) * 128]
                at = slice(part * 16, part * 16 + 16)
                rows.append(leaky(raw * scale[at] + offset[at]).astype(BF16).astype(F32))
            for j, v in enumerate(block_swap(rows)):
                fixed[j, part * 16:(part + 1) * 16, g * 128:(g + 1) * 128] = v.astype(BF16)
                norms[j] = norms[j] + v * v
        for j in range(16):
            norm = -0.5 * jnp.sum(norms[j], axis=0, keepdims=True)
            hi = norm.astype(BF16).astype(F32)
            mid = (norm - hi).astype(BF16).astype(F32)
            end = jnp.where(row16f < 3, -0.5, jnp.where(row16f == 3, hi, jnp.where(row16f == 4, mid, jnp.where(row16f == 5, norm - hi - mid, 0.0))))
            fixed[j, 112:128, g * 128:(g + 1) * 128] = end.astype(BF16)

    factor = sharp_ref[0] * (2.0 * LOG2E / ch)
    count = wide * 16
    lane1 = lax.broadcasted_iota(jnp.int32, (1, 128), 1)
    x_in, y_in, z_in = lane1 % 8, (lane1 // 8) % 4, lane1 // 32
    pos = lax.broadcasted_iota(jnp.int32, (16, 128), 0).astype(F32)

    marks = sorted({0, tall} | {4 * g for g in range(groups)} | {4 * g + span for g in range(groups)})

    def scores(m, parity):
        held = (even, odd)[parity]
        weights = fixed[2 * m + parity]
        best = [jnp.full((8, 128), -3e38, F32) for _g in range(groups)]
        for low, high in zip(marks[:-1], marks[1:]):
            items = held[low:high, :, pl.ds(pl.multiple_of(16 * m, 16), 16), :].reshape((high - low) * count, 128)
            users = [g for g in range(groups) if 4 * g <= low < 4 * g + span]
            s = jnp.dot(items, weights[:, users[0] * 128:(users[-1] + 1) * 128], preferred_element_type=F32)
            for i, g in enumerate(users):
                part = s[:, i * 128:(i + 1) * 128]
                score[parity, g, low - 4 * g:high - 4 * g] = part.reshape(high - low, count, 128)
                best[g] = jnp.maximum(best[g], jnp.max(part.reshape(-1, 8, 128), axis=0))
        for g in range(groups):
            peak[parity, g] = best[g]

    def sums_of(weight):
        zero = jnp.zeros((16, 128), F32)
        state = [[zero] * 4 for _g in range(groups)]
        for y in range(wide - 1, -1, -1):
            for g, at in enumerate(weight(y)):
                by_x, acc_z, part, acc_y = state[g]
                run, acc = zero, zero
                for z in range(span - 1, -1, -1):
                    run = run + at(z)
                    if z:
                        acc = acc + run
                if y:
                    part = part + run
                    acc_y = acc_y + part
                state[g] = [by_x + run, acc_z + acc, part, acc_y]
        return [[jnp.sum(v, axis=0, keepdims=True) for v in (by_x, acc_z, acc_y, by_x * pos)] for by_x, acc_z, _p, acc_y in state]

    def settle(g, j, total, acc_z, acc_y, acc_x):
        inv = 1.0 / total
        dz = acc_z * inv - (z_in + RADIUS).astype(F32)
        dy = acc_y * inv - (y_in + RADIUS).astype(F32)
        dx = acc_x * inv - (x_in + 4).astype(F32)
        found[g, j] = jnp.concatenate([dz, dy, dx, total, jnp.zeros((4, 128), F32)], axis=0)

    def tiles(m, least):
        for parity, held in enumerate((even, odd)):
            weights = fixed[2 * m + parity]

            def weight(y):
                items = held[:, y, pl.ds(pl.multiple_of(16 * m, 16), 16), :].reshape(tall * 16, 128)
                s = jnp.dot(items, weights, preferred_element_type=F32)

                def of(g):
                    first = 64 * g
                    return lambda z: jnp.exp2(s[first + 16 * z:first + 16 * z + 16, 128 * g:128 * g + 128] * factor)

                return [of(g) for g in range(groups)]

            for g, sums in enumerate(sums_of(weight)):
                settle(g, 2 * m + parity, *sums)
                least = jnp.minimum(least, sums[0])
        return least

    least = lax.fori_loop(0, 8, tiles, jnp.full((1, 128), 1.0, F32))

    @pl.when(jnp.logical_not(jnp.min(least) > 1e-18))
    def again():
        def tiles_again(m, _):
            for parity in range(2):
                scores(m, parity)
                tops = [jnp.max(peak[parity, g], axis=0, keepdims=True) * factor for g in range(groups)]

                def weight(y):
                    def of(g):
                        return lambda z: jnp.exp2(score[parity, g, z, 16 * y:16 * y + 16] * factor - tops[g])

                    return [of(g) for g in range(groups)]

                for g, sums in enumerate(sums_of(weight)):
                    settle(g, 2 * m + parity, *sums)
            return _

        lax.fori_loop(0, 8, tiles_again, 0)

    for g in range(groups):
        for q, v in enumerate(block_swap([found[g, j] for j in range(16)])):
            for comp in range(3):
                out_ref[comp, 4 * g + q // 4, pl.ds(q % 4, 1), :] = v[comp:comp + 1]


def match(edge, side, moving, fixed, sums, par, place, sharpness, slab, strip):
    tall, wide = slab + 2 * RADIUS, strip + 2 * RADIUS
    groups = slab // 4
    vm = pl.BlockSpec(memory_space=pltpu.VMEM)
    sm = pl.BlockSpec(memory_space=pltpu.SMEM)
    hbm = pl.BlockSpec(memory_space=pl.ANY)
    return pl.pallas_call(
        functools.partial(match_kernel, slab, strip),
        out_shape=jax.ShapeDtypeStruct((3, slab, strip, 128), F32),
        in_specs=[hbm] * 4 + [vm, vm, sm, sm],
        out_specs=vm,
        scratch_shapes=[
            pltpu.VMEM(edge.shape, F32),
            pltpu.VMEM(side.shape, F32),
            pltpu.VMEM(moving.shape, F32),
            pltpu.VMEM(fixed.shape, F32),
            pltpu.VMEM((2, 136, 128), F32),
            pltpu.VMEM((tall, wide, 128, 128), BF16),
            pltpu.VMEM((tall, wide, 128, 128), BF16),
            pltpu.VMEM((16, 128, 128 * groups), BF16),
            pltpu.VMEM((2, groups, 4 + 2 * RADIUS, wide * 16, 128), F32),
            pltpu.VMEM((2, groups, 8, 128), F32),
            pltpu.VMEM((groups, 16, 8, 128), F32),
            pltpu.SemaphoreType.DMA((2 * RADIUS,)),
            pltpu.SemaphoreType.DMA((slab,)),
            pltpu.SemaphoreType.DMA((slab,)),
            pltpu.SemaphoreType.DMA(()),
        ],
        compiler_params=pltpu.CompilerParams(vmem_limit_bytes=60 * 1024 * 1024),
        name="match",
    )(edge, side, moving, fixed, sums, par, place, sharpness)


def gathered(fixed_image, moving_image):
    depth, height = lax.axis_size("depth"), lax.axis_size("height")
    slab, strip, width = fixed_image.shape
    both = jnp.stack([fixed_image, moving_image]).reshape(2, slab * strip, width)
    power = jnp.clip(jnp.floor(jnp.log2(jnp.max(jnp.abs(both), axis=(1, 2), keepdims=True))) - 13.0, -113.0, 113.0)
    scaled = jnp.pad(both * jnp.exp2(-power), ((0, 0), (0, 8), (0, 0)))
    spot = lax.broadcasted_iota(jnp.int32, scaled.shape, 1)
    sent = jnp.where(spot < slab * strip, scaled, power).astype(jnp.float16)
    sent = jnp.broadcast_to(sent[None, :, None], (depth // 2, 2, height) + sent.shape[1:])
    return lax.all_to_all(sent.reshape((depth * height,) + sent.shape[3:]), AXES, 0, 0)


def restored(blocks):
    power = jnp.exp2(blocks[:, -8:-7].astype(F32))
    return blocks[:, :-8].astype(F32) * power


def local(fixed_image, moving_image, conv_one, gain_one, shift_one, conv_two, gain_two, shift_two, sharpness):
    depth, height = lax.axis_size("depth"), lax.axis_size("height")
    slab, strip, _ = fixed_image.shape
    swap = [(i, i ^ 1) for i in range(depth)]
    blocks = gathered(fixed_image, moving_image)
    base, pairs, two, par = parameters(conv_one, gain_one, shift_one, conv_two, gain_two, shift_two)
    row, column = lax.axis_index("depth"), lax.axis_index("height")
    place = jnp.stack([row * slab, column * strip, slab * depth, strip * height, row % 2, row, column]).astype(jnp.int32)
    other = restored(lax.ppermute(blocks, "depth", swap))
    own = restored(blocks)
    mine = moments(own, pairs, par, depth, height, slab, strip)
    theirs = lax.ppermute(mine, "depth", swap)
    moving, fixed, sums = encode(own, other, mine, theirs, base, two, place, depth, height, slab, strip)
    sums = lax.all_to_all(sums, AXES, 0, 0)
    edge, side = rim(own, other, mine, theirs, base, two, place, depth, height, slab, strip)
    return match(edge, side, moving, fixed, sums, par, place, sharpness, slab, strip)


def solution(mesh):
    image = P("depth", "height", None)
    return jax.shard_map(
        local,
        mesh=mesh,
        in_specs=(image, image) + (P(),) * 7,
        out_specs=P(None, "depth", "height", None),
        check_vma=False,
    )
```

```python
import functools

import jax
import jax.numpy as jnp
import numpy as np
from jax import lax
from jax.experimental import pallas as pl
from jax.experimental.pallas import tpu as pltpu
from jax.sharding import PartitionSpec as P

RADIUS = 3
TILE = 8
F32 = jnp.float32
BF16 = jnp.bfloat16
FAR = -1e30
LOG2E = 1.4426950408889634
NUM = (((1,), (0,)), ((), ()))
AXES = ("depth", "height")


def leaky(v):
    return jnp.maximum(v, 0.01 * v)


def lag_list(far):
    return [(y, x) for y in range(-2, 3) for x in range(-2, 3) if (far, y, x) >= (0, 0, 0)]


def lag_index():
    keys = [("a", "a", far, y, x, "a") for far in range(3) for y, x in lag_list(far)]
    keys += [(e, "a", 0, y, x, "a") for e in "fl" for y, x in lag_list(0)]
    keys += [("a", e, far, 0, x, "a") for e in "fl" for far in range(3) for y, x in lag_list(far) if y == 0]
    keys += [(d, e, 0, 0, x, "a") for d in "fl" for e in "fl" for y, x in lag_list(0) if y == 0]
    keys += [k[:5] + (e,) for e in "fl" for k in list(keys) if k[4] == 0]
    return {k: i for i, k in enumerate(keys)}


LAGS = lag_index()


def pair_table():
    table = np.zeros((729, 256), np.float32)
    taps = [(a, b, c) for a in range(3) for b in range(3) for c in range(3)]
    for i, k in enumerate(taps):
        for j, l in enumerate(taps):
            p, q = (k, l) if l >= k else (l, k)
            lag = tuple(v - u for u, v in zip(p, q))
            kinds = [[("a", 1)] + ([("f" if u == 2 else "l", -1)] if u == v != 1 else []) for u, v in zip(p, q)]
            for d, sd in kinds[0]:
                for h, sh in kinds[1]:
                    for w, sw in kinds[2]:
                        table[i * 27 + j, LAGS[(d, h) + lag + (w,)]] += sd * sh * sw
    return table


def moments_kernel(nd, nh, slab, strip, own_ref, pairs_ref, par_ref, out_ref, img, slid, pieces):
    zn, yn = nd * slab, nh * strip
    count = float(zn * yn * 128)
    lane8 = lax.broadcasted_iota(jnp.int32, (8, 128), 1)
    sub8 = lax.broadcasted_iota(jnp.int32, (8, 128), 0)
    row_y = lax.broadcasted_iota(jnp.int32, (yn, 128), 0)
    side = lax.broadcasted_iota(jnp.int32, (yn, 128), 1)
    gain, shift = [jnp.broadcast_to(par_ref[i:i + 1, :], (128, 128)).T[0:64] for i in range(2)]

    img[0:2] = jnp.zeros((2, yn + 16, 128), F32)
    img[:, 0:8, :] = jnp.zeros((zn + 2, 8, 128), F32)
    img[:, 8 + yn:16 + yn, :] = jnp.zeros((zn + 2, 8, 128), F32)
    slid[:, :, 0:8, :] = jnp.zeros((4, zn, 8, 128), F32)
    slid[:, :, 8 + yn:16 + yn, :] = jnp.zeros((4, zn, 8, 128), F32)

    def gather(d, _):
        for p in range(nh // 2):
            pair = own_ref[pl.ds(d * nh + 2 * p, 2)]
            for z in range(slab):
                both = jnp.concatenate([pair[0, strip * z:strip * (z + 1)], pair[1, strip * z:strip * (z + 1)]], axis=0)
                img[2 + slab * d + z, 8 + 8 * p:16 + 8 * p, :] = both
        return _

    lax.fori_loop(0, nd, gather, 0)

    def slide(i, _):
        at = 4 * i
        for u in range(4):
            v = img[2 + at + u, 8:8 + yn]
            for n, move in enumerate((-2, -1, 1, 2)):
                kept = (side + move >= 0) & (side + move < 128)
                slid[n, at + u, 8:8 + yn] = jnp.where(kept, pltpu.roll(v, (128 - move) % 128, 1), 0.0)
        return _

    lax.fori_loop(0, zn // 4, slide, 0)

    def other(z, y, x):
        if x == 0:
            return img[2 + z, y:y + 8, :]
        return slid[x + 2 if x < 0 else x + 1, z, y:y + 8, :]

    def put(key, v):
        at = 8 * LAGS[key]
        pieces[at:at + 8, :] = v
        if key[4] == 0:
            for e, end in (("f", 0), ("l", 127)):
                at = 8 * LAGS[key[:5] + (e,)]
                pieces[at:at + 8, :] = jnp.where(lane8 == end, v, 0.0)

    def products(z, y, lags, state, fars):
        state = [list(v) for v in state]
        for i in range(yn // 8):
            held = {far: img[2 + z - far, 8 + 8 * i:16 + 8 * i, :] for far in fars}
            moved = {x: other(z, 8 + 8 * i + y, x) for x in range(-2, 3)}
            part = 0 if y or 0 < i < yn // 8 - 1 else 1 if i == 0 else 2
            for n, (far, x) in enumerate(lags):
                if far in fars:
                    state[part][n] = state[part][n] + held[far] * moved[x]
        return tuple(tuple(v) for v in state)

    def record(d, y, lags, state, fars):
        for n, (far, x) in enumerate(lags):
            if far not in fars:
                continue
            if y == 0:
                put((d, "a", far, y, x, "a"), state[0][n] + state[1][n] + state[2][n])
                put((d, "f", far, y, x, "a"), jnp.where(sub8 == 0, state[1][n], 0.0))
                put((d, "l", far, y, x, "a"), jnp.where(sub8 == 7, state[2][n], 0.0))
            else:
                put((d, "a", far, y, x, "a"), state[0][n])

    nothing = jnp.zeros((8, 128), F32)
    pieces[8 * len(LAGS):2048, :] = jnp.zeros((2048 - 8 * len(LAGS), 128), F32)
    for y in range(-2, 3):
        lags = [(far, x) for far in range(3) for x in range(-2, 3) if (far, y, x) >= (0, 0, 0)]
        empty = ((nothing,) * len(lags),) * (1 if y else 3)
        state = lax.fori_loop(0, zn, lambda z, state: products(z, y, lags, state, (0, 1, 2)), empty)
        record("a", y, lags, state, (0, 1, 2))
        if y >= 0:
            for d, z in (("f", 0), ("l", zn - 1)):
                record(d, y, lags, products(z, y, lags, empty, (0,)), (0,))

    def add(z, total):
        return total + img[2 + z, 8:8 + yn, :]

    whole = lax.fori_loop(0, zn, add, jnp.zeros((yn, 128), F32))
    first, last = img[2, 8:8 + yn, :], img[1 + zn, 8:8 + yn, :]
    for kz in range(3):
        plane = (whole - last, whole, whole - first)[kz]
        for ky in range(3):
            v = plane
            if ky == 0:
                v = jnp.where(row_y == yn - 1, 0.0, v)
            if ky == 2:
                v = jnp.where(row_y == 0, 0.0, v)
            v = jnp.sum(v.reshape(yn // 8, 8, 128), axis=0)
            for kx in range(3):
                w = v
                if kx == 0:
                    w = jnp.where(lane8 == 127, 0.0, w)
                if kx == 2:
                    w = jnp.where(lane8 == 0, 0.0, w)
                at = 2048 + (kz * 9 + ky * 3 + kx) * 8
                pieces[at:at + 8, :] = w
    pieces[2264:2304, :] = jnp.zeros((40, 128), F32)
    rows = pieces[pl.ds(0, 288, stride=8), :]
    for s in range(1, 8):
        rows = rows + pieces[pl.ds(s, 288, stride=8), :]
    second = lax.dot_general(pairs_ref[:, 0:256], rows[0:256], NUM, precision=lax.Precision.HIGHEST, preferred_element_type=F32)
    mean = lax.dot_general(pairs_ref[:, 256:288], rows[256:288], NUM, precision=lax.Precision.HIGHEST, preferred_element_type=F32)
    mean = jnp.sum(mean, axis=1, keepdims=True) / count
    second = jnp.sum(second, axis=1, keepdims=True) / count
    scale = lax.rsqrt(second - mean * mean + 1e-05) * gain
    out_ref[0:64, :] = jnp.broadcast_to(scale, (64, 128))
    out_ref[64:128, :] = jnp.broadcast_to(shift - mean * scale, (64, 128))


def moments(own, pairs, par, nd, nh, slab, strip):
    zn, yn = nd * slab, nh * strip
    vm = pl.BlockSpec(memory_space=pltpu.VMEM)
    return pl.pallas_call(
        functools.partial(moments_kernel, nd, nh, slab, strip),
        out_shape=jax.ShapeDtypeStruct((128, 128), F32),
        in_specs=[vm] * 3,
        out_specs=vm,
        scratch_shapes=[
            pltpu.VMEM((zn + 2, yn + 16, 128), F32),
            pltpu.VMEM((4, zn, yn + 16, 128), F32),
            pltpu.VMEM((2304, 128), F32),
        ],
        compiler_params=pltpu.CompilerParams(vmem_limit_bytes=40 * 1024 * 1024),
        cost_estimate=pl.CostEstimate(flops=10 ** 9, bytes_accessed=10 ** 6, transcendentals=0),
        name="moments",
    )(own, pairs, par)


def convolved(weights, feat, z, first, wide, lane64):
    taps = [feat[z + a, :, 128 * (f + b):128 * (f + b + n)] for a in range(3) for b in range(3) for f, n in [(first, wide)]]
    return joined(weights, jnp.concatenate(taps, axis=0), wide, lane64)


def joined(weights, taps, wide, lane64):
    raw = jnp.dot(weights, taps, preferred_element_type=F32)
    rows = []
    for y in range(wide):
        cut = slice(128 * y, 128 * y + 128)
        before = jnp.where(lane64 == 0, 0.0, pltpu.roll(raw[0:64, cut], 1, 1))
        after = jnp.where(lane64 == 127, 0.0, pltpu.roll(raw[128:192, cut], 127, 1))
        rows.append(before + raw[64:128, cut] + after)
    return rows


def banded(taps_ref, toep, rows):
    base = taps_ref[...]
    spot = lax.broadcasted_iota(jnp.int32, base.shape, 1)
    base_hi = base.astype(BF16).astype(F32)
    base = jnp.where((spot >= 144) & (spot < 288), (base - base_hi).astype(BF16).astype(F32), base_hi)
    for yo in range(rows):
        toep[64 * yo:64 * yo + 64, :] = (pltpu.roll(base, yo, 1) if yo else base).astype(BF16)


def first_layer(scans, slab, strip, near, group, nd, nh, own_ref, other_ref, mine_ref, theirs_ref, place_ref, win, toep, plane_hi, plane_lo, feat):
    planes, rows = slab + 2 * near, strip + 2 * near
    zn, yn = nd * slab, nh * strip
    z0, y0, core = place_ref[0], place_ref[1], place_ref[4]
    row, column = place_ref[5], place_ref[6]
    lane = lax.broadcasted_iota(jnp.int32, (16, 128), 1)
    reach = -(-(near + 1) // strip)
    for s, scan in enumerate(scans):
        mine = core == scan
        for i in range(-1, 2):
            for j in range(-reach, reach + 1):
                d, h = row + i, column + j
                inside = (d >= 0) & (d < nd) & (h >= 0) & (h < nh)
                at = jnp.where(inside, d * nh + h, 0)
                block = jnp.where(mine, own_ref[at], other_ref[at])
                block = jnp.where(inside, block, 0.0)
                for z in range(slab):
                    win[s, slab * (i + 1) + z, strip * (j + 2):strip * (j + 3), :] = block[strip * z:strip * (z + 1)]
        for i in range(planes + 2):
            low = 2 * strip - near - 1
            v = win[s, slab - near - 1 + i, low:low + 16, :]
            before = jnp.where(lane == 0, 0.0, pltpu.roll(v, 1, 1))
            after = jnp.where(lane == 127, 0.0, pltpu.roll(v, 127, 1))
            v = jnp.concatenate([before, v, after], axis=0)
            hi = v.astype(BF16)
            plane_hi[s, i] = hi
            plane_lo[s, i] = (v - hi.astype(F32)).astype(BF16)
    scales = [jnp.where(core == scan, mine_ref[0:64], theirs_ref[0:64]) for scan in scans]
    offsets = [jnp.where(core == scan, mine_ref[64:128], theirs_ref[64:128]) for scan in scans]

    def first(i, _):
        sides = []
        for s in range(len(scans)):
            for u in range(group):
                hi = plane_hi[s, pl.ds(group * i + u, 3)].reshape(144, 128)
                lo = plane_lo[s, pl.ds(group * i + u, 3)].reshape(144, 128)
                sides.append(jnp.concatenate([hi, hi, lo, jnp.zeros((80, 128), BF16)], axis=0))
        raw = jnp.dot(toep[0:64 * rows, :], jnp.concatenate(sides, axis=1), preferred_element_type=F32)
        for s in range(len(scans)):
            for u in range(group):
                z = z0 - near + group * i + u
                cut = slice(128 * (s * group + u), 128 * (s * group + u) + 128)
                for yo in range(rows):
                    y = y0 - near + yo
                    v = leaky(raw[64 * yo:64 * yo + 64, cut] * scales[s] + offsets[s])
                    v = jnp.where((z >= 0) & (z < zn) & (y >= 0) & (y < yn), v, 0.0)
                    to = 128 * (s * rows + yo)
                    feat[group * i + u, :, to:to + 128] = v.astype(BF16)
        return _

    lax.fori_loop(0, planes // group, first, 0)


def encode_kernel(nd, nh, slab, strip, own_ref, other_ref, mine_ref, theirs_ref, taps_ref, two_ref, place_ref,
                  raw_hbm, sums_ref, win, toep, plane_hi, plane_lo, feat, raw, sem):
    rows = strip + 2
    banded(taps_ref, toep, rows)
    first_layer((0, 1), slab, strip, 1, 2, nd, nh, own_ref, other_ref, mine_ref, theirs_ref, place_ref, win, toep, plane_hi, plane_lo, feat)
    lane64 = lax.broadcasted_iota(jnp.int32, (64, 128), 1)
    zero = jnp.zeros((64, 128), F32)

    def store(z):
        return pltpu.make_async_copy(raw.at[z], raw_hbm.at[z], sem.at[z])

    def plane(z, state):
        state = list(state)
        taps = []
        for a in range(3):
            for b in range(3):
                cuts = [feat[z + a, :, 128 * (s * rows + b):128 * (s * rows + b + strip)] for s in range(2)]
                taps.append(jnp.concatenate(cuts, axis=1))
        for i, v in enumerate(joined(two_ref[...], jnp.concatenate(taps, axis=0), 2 * strip, lane64)):
            s, y = i // strip, i % strip
            raw[z, s, :, 128 * y:128 * y + 128] = v
            state[s] = state[s] + v
            state[2 + s] = state[2 + s] + v * v
        store(z).start()
        return tuple(state)

    sums = lax.fori_loop(0, slab, plane, (zero,) * 4)
    total = jnp.sum(jnp.concatenate(sums[0:2], axis=0).T, axis=0, keepdims=True)
    square = jnp.sum(jnp.concatenate(sums[2:4], axis=0).T, axis=0, keepdims=True)
    both = jnp.concatenate([total, square], axis=0)
    sums_ref[...] = jnp.broadcast_to(both[None], sums_ref.shape)
    for z in range(slab):
        store(z).wait()


def encode(own, other, mine, theirs, taps, two, place, nd, nh, slab, strip):
    vm = pl.BlockSpec(memory_space=pltpu.VMEM)
    sm = pl.BlockSpec(memory_space=pltpu.SMEM)
    hbm = pl.BlockSpec(memory_space=pl.ANY)
    return pl.pallas_call(
        functools.partial(encode_kernel, nd, nh, slab, strip),
        out_shape=(
            jax.ShapeDtypeStruct((slab, 2, 64, strip * 128), F32),
            jax.ShapeDtypeStruct((nd * nh, 2, 128), F32),
        ),
        in_specs=[vm] * 6 + [sm],
        out_specs=(hbm, vm),
        scratch_shapes=[
            pltpu.VMEM((2, 3 * slab, 24, 128), F32),
            pltpu.VMEM((64 * (strip + 2), 512), BF16),
            pltpu.VMEM((2, slab + 4, 48, 128), BF16),
            pltpu.VMEM((2, slab + 4, 48, 128), BF16),
            pltpu.VMEM((slab + 2, 64, 2 * (strip + 2) * 128), BF16),
            pltpu.VMEM((slab, 2, 64, strip * 128), F32),
            pltpu.SemaphoreType.DMA((slab,)),
        ],
        compiler_params=pltpu.CompilerParams(vmem_limit_bytes=52 * 1024 * 1024),
        name="encode",
    )(own, other, mine, theirs, taps, two, place)


def rim_kernel(nd, nh, slab, strip, own_ref, other_ref, mine_ref, theirs_ref, taps_ref, two_ref, place_ref,
               edge_ref, side_ref, win, toep, plane_hi, plane_lo, feat, edge, side, edge_sem, side_sem):
    lane64 = lax.broadcasted_iota(jnp.int32, (64, 128), 1)
    wide = strip + 6
    banded(taps_ref, toep, strip + 8)
    first_layer((1,), slab, strip, 4, 4, nd, nh, own_ref, other_ref, mine_ref, theirs_ref, place_ref, win, toep, plane_hi, plane_lo, feat)

    def store_edge(i):
        return pltpu.make_async_copy(edge.at[i], edge_ref.at[i], edge_sem.at[i])

    def store_side(i):
        return pltpu.make_async_copy(side.at[i], side_ref.at[i], side_sem.at[i])

    def whole(i, _):
        z = jnp.where(i < RADIUS, i, i + slab)
        for y, v in enumerate(convolved(two_ref[...], feat, z, 0, wide, lane64)):
            edge[i, :, 128 * y:128 * y + 128] = v
        store_edge(i).start()
        return _

    def middle(i, _):
        z = RADIUS + 2 * i
        taps = []
        for a in range(3):
            for b in range(3):
                cuts = [feat[z + u + a, :, 128 * (c + b):128 * (c + b + 3)] for u in range(2) for c in (0, strip + 3)]
                taps.append(jnp.concatenate(cuts, axis=1))
        for y, v in enumerate(joined(two_ref[...], jnp.concatenate(taps, axis=0), 12, lane64)):
            side[2 * i + y // 6, :, 128 * (y % 6):128 * (y % 6) + 128] = v
        store_side(2 * i).start()
        store_side(2 * i + 1).start()
        return _

    lax.fori_loop(0, 2 * RADIUS, whole, 0)
    lax.fori_loop(0, slab // 2, middle, 0)
    for i in range(2 * RADIUS):
        store_edge(i).wait()
    for i in range(slab):
        store_side(i).wait()


def rim(own, other, mine, theirs, taps, two, place, nd, nh, slab, strip):
    hbm = pl.BlockSpec(memory_space=pl.ANY)
    vm = pl.BlockSpec(memory_space=pltpu.VMEM)
    sm = pl.BlockSpec(memory_space=pltpu.SMEM)
    edge = (6, 64, (strip + 6) * 128)
    side = (slab, 64, 6 * 128)
    return pl.pallas_call(
        functools.partial(rim_kernel, nd, nh, slab, strip),
        out_shape=(jax.ShapeDtypeStruct(edge, F32), jax.ShapeDtypeStruct(side, F32)),
        in_specs=[vm] * 6 + [sm],
        out_specs=(hbm, hbm),
        scratch_shapes=[
            pltpu.VMEM((1, 3 * slab, 24, 128), F32),
            pltpu.VMEM((64 * (strip + 8), 512), BF16),
            pltpu.VMEM((1, slab + 10, 48, 128), BF16),
            pltpu.VMEM((1, slab + 10, 48, 128), BF16),
            pltpu.VMEM((slab + 8, 64, (strip + 8) * 128), BF16),
            pltpu.VMEM(edge, F32),
            pltpu.VMEM(side, F32),
            pltpu.SemaphoreType.DMA((6,)),
            pltpu.SemaphoreType.DMA((slab,)),
        ],
        compiler_params=pltpu.CompilerParams(vmem_limit_bytes=52 * 1024 * 1024),
        cost_estimate=pl.CostEstimate(flops=6 * 10 ** 9, bytes_accessed=10 ** 7, transcendentals=0),
        name="rim",
    )(own, other, mine, theirs, taps, two, place)


def parameters(conv_one, gain_one, shift_one, conv_two, gain_two, shift_two):
    w = conv_one.reshape(64, 3, 3, 3)
    base = jnp.pad(jnp.transpose(w, (0, 1, 3, 2)), ((0, 0), (0, 0), (0, 0), (0, 13))).reshape(64, 144)
    base = jnp.concatenate([base, base, base, jnp.zeros((64, 80), F32)], axis=1)
    flat = conv_one.reshape(64, 27)
    products = (flat[:, :, None] * flat[:, None, :]).reshape(64, 729)
    quad = jnp.dot(products, pair_table(), precision=lax.Precision.HIGHEST)
    pairs = jnp.concatenate([quad, flat, jnp.zeros((64, 5), F32)], axis=1)
    two = conv_two.reshape(3, 3, 3, 64, 64).transpose(2, 4, 0, 1, 3).reshape(192, 576)
    par = jnp.stack([jnp.concatenate([v, v]) for v in (gain_one, shift_one, gain_two, shift_two)])
    return base, pairs, two, par


def block_swap(rows):
    rows = list(rows)
    lane = lax.broadcasted_iota(jnp.int32, rows[0].shape, 1)
    for bit in range(4):
        step = 1 << bit
        low = (lane // (TILE * step)) % 2 == 0
        for q in range(16):
            if q & step:
                continue
            a, c = rows[q], rows[q + step]
            rows[q] = jnp.where(low, a, pltpu.roll(c, TILE * step, 1))
            rows[q + step] = jnp.where(low, pltpu.roll(a, 128 - TILE * step, 1), c)
    return rows


def match_kernel(slab, strip, edge_hbm, side_hbm, raw_hbm, sums_ref, par_ref, place_ref, sharp_ref, out_ref,
                 edge_ref, side_ref, raw_ref, turned, even, odd, fixed, score, peak, found,
                 edge_sem, side_sem, raw_sem):
    ch = raw_ref.shape[2]
    def load_edge(i):
        return pltpu.make_async_copy(edge_hbm.at[i], edge_ref.at[i], edge_sem.at[i])

    def load_side(i):
        return pltpu.make_async_copy(side_hbm.at[i], side_ref.at[i], side_sem.at[i])

    def load_raw(i):
        return pltpu.make_async_copy(raw_hbm.at[i], raw_ref.at[i], raw_sem.at[i])

    ahead = [load_edge(i) for i in range(RADIUS)]
    ahead += [load(i) for i in range(slab) for load in (load_side, load_raw)]
    ahead += [load_edge(RADIUS + i) for i in range(RADIUS)]
    for load in ahead:
        load.start()
    tall, wide = slab + 2 * RADIUS, strip + 2 * RADIUS
    groups = slab // 4
    span = 4 + 2 * RADIUS
    z0, y0 = place_ref[0], place_ref[1]
    zn, yn = place_ref[2], place_ref[3]

    sums = jnp.sum(sums_ref[...], axis=0) / (zn * yn * 128).astype(F32)
    mean, square = sums[0:1], sums[1:2]
    scale = lax.rsqrt(square - mean * mean + 1e-05) * par_ref[2:3]
    offset = par_ref[3:4] - mean * scale
    scale = jnp.broadcast_to(scale, (128, 128)).T
    offset = jnp.broadcast_to(offset, (128, 128)).T

    def feature(raw, scan):
        v = raw * scale[64 * scan:64 * scan + 64] + offset[64 * scan:64 * scan + 64]
        return leaky(v).astype(BF16).astype(F32)

    row16 = lax.broadcasted_iota(jnp.int32, (16, 128), 0)
    col16 = lax.broadcasted_iota(jnp.int32, (16, 128), 1)
    onehot_x = jnp.where((col16 == 80 + row16) | ((col16 >= 67) & (col16 < 70)), 1.0, 0.0)
    sub8 = lax.broadcasted_iota(jnp.int32, (8, 128), 0)
    blank = jnp.zeros((8, 128), F32)
    for i in range(2):
        turned[i] = jnp.zeros((136, 128), F32)

    def plane(z, middle):
        if middle:
            load_side(z - RADIUS).wait()
            load_raw(z - RADIUS).wait()
        else:
            at = jnp.where(z < RADIUS, z, z - slab)
            load_edge(at).wait()
        zz = z0 + z - RADIUS
        for y in range(wide):
            if not middle:
                raw = edge_ref[at, :, y * 128:(y + 1) * 128]
            elif RADIUS <= y < RADIUS + strip:
                raw = raw_ref[z - RADIUS, 1, :, (y - RADIUS) * 128:(y - RADIUS + 1) * 128]
            else:
                c = y if y < RADIUS else y - strip
                raw = side_ref[z - RADIUS, :, c * 128:(c + 1) * 128]
            f = feature(raw, 1)
            yy = y0 + y - RADIUS
            f = jnp.where((zz >= 0) & (zz < zn) & (yy >= 0) & (yy < yn), f, 0.0)
            norm = jnp.sum(f * f, axis=0, keepdims=True)
            hi = norm.astype(BF16).astype(F32)
            mid = (norm - hi).astype(BF16).astype(F32)
            low = norm - hi - mid
            extra = jnp.where(sub8 == 0, hi, jnp.where(sub8 == 1, mid, jnp.where(sub8 == 2, low, 0.0)))
            turned[y % 2, 4:132, 0:72] = jnp.concatenate([f, extra], axis=0).T
            ones = jnp.where((col16 == 96 + y) | (col16 == 112 + z), 1.0, onehot_x).astype(BF16)[None]
            even[z, y] = (turned[y % 2, 0:128].astype(BF16).reshape(8, 16, 128) + ones).reshape(128, 128)
            odd[z, y] = (turned[y % 2, 8:136].astype(BF16).reshape(8, 16, 128) + ones).reshape(128, 128)

    def among(z, _):
        plane(z, True)
        return _

    def after(z, _):
        plane(z, False)
        return _

    lax.fori_loop(0, RADIUS, after, 0)
    lax.fori_loop(RADIUS, RADIUS + slab, among, 0)
    lax.fori_loop(RADIUS + slab, tall, after, 0)

    k = lax.broadcasted_iota(jnp.int32, (64, 128 * groups), 0)
    lane = lax.broadcasted_iota(jnp.int32, (64, 128 * groups), 1)
    fx, fy, fz = lane % 8, (lane // 8) % 4, lane // 32
    span_x = jnp.abs(k - fx - 4)
    span_y = jnp.abs(k - 16 - fy - 3)
    span_z = jnp.abs(k - 32 - fz - 3)
    apart = jnp.where(k < 16, span_x, jnp.where(k < 32, span_y, jnp.where(k < 48, span_z, 0)))
    tail = jnp.where(apart > RADIUS, FAR, 0.0)
    tail = tail.astype(BF16)
    for j in range(16):
        fixed[j, 80:128, :] = tail[0:48]
    row16f = lax.broadcasted_iota(jnp.int32, (16, 128), 0)
    for g in range(groups):
        norms = [jnp.zeros((16, 128), F32)] * 16
        for part in range(ch // 16):
            rows = []
            for q in range(16):
                raw = raw_ref[4 * g + q // 4, 0, part * 16:(part + 1) * 16, (q % 4) * 128:(q % 4 + 1) * 128]
                at = slice(part * 16, part * 16 + 16)
                rows.append(leaky(raw * scale[at] + offset[at]).astype(BF16))
            for j, v in enumerate(block_swap(rows)):
                fixed[j, part * 16:(part + 1) * 16, g * 128:(g + 1) * 128] = v
                norms[j] = norms[j] + v.astype(F32) * v.astype(F32)
        for j in range(16):
            norm = -0.5 * jnp.sum(norms[j], axis=0, keepdims=True)
            hi = norm.astype(BF16).astype(F32)
            mid = (norm - hi).astype(BF16).astype(F32)
            end = jnp.where(row16f < 3, -0.5, jnp.where(row16f == 3, hi, jnp.where(row16f == 4, mid, jnp.where(row16f == 5, norm - hi - mid, 0.0))))
            fixed[j, 64:80, g * 128:(g + 1) * 128] = end.astype(BF16)

    factor = sharp_ref[0] * (2.0 * LOG2E / ch)
    count = wide * 16
    lane1 = lax.broadcasted_iota(jnp.int32, (1, 128), 1)
    x_in, y_in, z_in = lane1 % 8, (lane1 // 8) % 4, lane1 // 32
    pos = lax.broadcasted_iota(jnp.int32, (16, 128), 0).astype(F32)

    marks = sorted({0, tall} | {4 * g for g in range(groups)} | {4 * g + span for g in range(groups)})

    def scores(m, parity):
        held = (even, odd)[parity]
        weights = fixed[2 * m + parity]
        best = [jnp.full((8, 128), -3e38, F32) for _g in range(groups)]
        for low, high in zip(marks[:-1], marks[1:]):
            items = held[low:high, :, pl.ds(pl.multiple_of(16 * m, 16), 16), :].reshape((high - low) * count, 128)
            users = [g for g in range(groups) if 4 * g <= low < 4 * g + span]
            s = jnp.dot(items, weights[:, users[0] * 128:(users[-1] + 1) * 128], preferred_element_type=F32)
            for i, g in enumerate(users):
                part = s[:, i * 128:(i + 1) * 128]
                score[parity, g, low - 4 * g:high - 4 * g] = part.reshape(high - low, count, 128)
                best[g] = jnp.maximum(best[g], jnp.max(part.reshape(-1, 8, 128), axis=0))
        for g in range(groups):
            peak[parity, g] = best[g]

    def sums_of(weight):
        zero = jnp.zeros((16, 128), F32)
        state = [[zero] * 4 for _g in range(groups)]
        for y in range(wide - 1, -1, -1):
            for g, at in enumerate(weight(y)):
                by_x, acc_z, part, acc_y = state[g]
                run, acc = zero, zero
                for z in range(span - 1, -1, -1):
                    run = run + at(z)
                    if z:
                        acc = acc + run
                if y:
                    part = part + run
                    acc_y = acc_y + part
                state[g] = [by_x + run, acc_z + acc, part, acc_y]
        return [[jnp.sum(v, axis=0, keepdims=True) for v in (by_x, acc_z, acc_y, by_x * pos)] for by_x, acc_z, _p, acc_y in state]

    def settle(g, j, total, acc_z, acc_y, acc_x):
        inv = 1.0 / total
        dz = acc_z * inv - (z_in + RADIUS).astype(F32)
        dy = acc_y * inv - (y_in + RADIUS).astype(F32)
        dx = acc_x * inv - (x_in + 4).astype(F32)
        found[g, j] = jnp.concatenate([dz, dy, dx, total, jnp.zeros((4, 128), F32)], axis=0)

    def tiles(m, least):
        for parity, held in enumerate((even, odd)):
            weights = fixed[2 * m + parity]

            def weight(y):
                items = held[:, y, pl.ds(pl.multiple_of(16 * m, 16), 16), :].reshape(tall * 16, 128)
                s = jnp.dot(items, weights, preferred_element_type=F32)

                def of(g):
                    first = 64 * g
                    return lambda z: jnp.exp2(s[first + 16 * z:first + 16 * z + 16, 128 * g:128 * g + 128] * factor)

                return [of(g) for g in range(groups)]

            for g, sums in enumerate(sums_of(weight)):
                settle(g, 2 * m + parity, *sums)
                least = jnp.minimum(least, sums[0])
        return least

    least = lax.fori_loop(0, 8, tiles, jnp.full((1, 128), 1.0, F32))

    @pl.when(jnp.logical_not(jnp.min(least) > 1e-18))
    def again():
        def tiles_again(m, _):
            for parity in range(2):
                scores(m, parity)
                tops = [jnp.max(peak[parity, g], axis=0, keepdims=True) * factor for g in range(groups)]

                def weight(y):
                    def of(g):
                        return lambda z: jnp.exp2(score[parity, g, z, 16 * y:16 * y + 16] * factor - tops[g])

                    return [of(g) for g in range(groups)]

                for g, sums in enumerate(sums_of(weight)):
                    settle(g, 2 * m + parity, *sums)
            return _

        lax.fori_loop(0, 8, tiles_again, 0)

    for g in range(groups):
        for q, v in enumerate(block_swap([found[g, j] for j in range(16)])):
            for comp in range(3):
                out_ref[comp, 4 * g + q // 4, pl.ds(q % 4, 1), :] = v[comp:comp + 1]


def match(edge, side, raw, sums, par, place, sharpness, slab, strip):
    tall, wide = slab + 2 * RADIUS, strip + 2 * RADIUS
    groups = slab // 4
    vm = pl.BlockSpec(memory_space=pltpu.VMEM)
    sm = pl.BlockSpec(memory_space=pltpu.SMEM)
    hbm = pl.BlockSpec(memory_space=pl.ANY)
    return pl.pallas_call(
        functools.partial(match_kernel, slab, strip),
        out_shape=jax.ShapeDtypeStruct((3, slab, strip, 128), F32),
        in_specs=[hbm] * 3 + [vm, vm, sm, sm],
        out_specs=vm,
        scratch_shapes=[
            pltpu.VMEM(edge.shape, F32),
            pltpu.VMEM(side.shape, F32),
            pltpu.VMEM(raw.shape, F32),
            pltpu.VMEM((2, 136, 128), F32),
            pltpu.VMEM((tall, wide, 128, 128), BF16),
            pltpu.VMEM((tall, wide, 128, 128), BF16),
            pltpu.VMEM((16, 128, 128 * groups), BF16),
            pltpu.VMEM((2, groups, 4 + 2 * RADIUS, wide * 16, 128), F32),
            pltpu.VMEM((2, groups, 8, 128), F32),
            pltpu.VMEM((groups, 16, 8, 128), F32),
            pltpu.SemaphoreType.DMA((2 * RADIUS,)),
            pltpu.SemaphoreType.DMA((slab,)),
            pltpu.SemaphoreType.DMA((slab,)),
        ],
        compiler_params=pltpu.CompilerParams(vmem_limit_bytes=60 * 1024 * 1024),
        name="match",
    )(edge, side, raw, sums, par, place, sharpness)


def gathered(fixed_image, moving_image):
    depth, height = lax.axis_size("depth"), lax.axis_size("height")
    slab, strip, width = fixed_image.shape
    both = jnp.stack([fixed_image, moving_image]).reshape(2, slab * strip, width)
    power = jnp.clip(jnp.floor(jnp.log2(jnp.max(jnp.abs(both), axis=(1, 2), keepdims=True))) - 13.0, -113.0, 113.0)
    scaled = jnp.pad(both * jnp.exp2(-power), ((0, 0), (0, 8), (0, 0)))
    spot = lax.broadcasted_iota(jnp.int32, scaled.shape, 1)
    sent = jnp.where(spot < slab * strip, scaled, power).astype(jnp.float16)
    sent = jnp.broadcast_to(sent[None, :, None], (depth // 2, 2, height) + sent.shape[1:])
    return lax.all_to_all(sent.reshape((depth * height,) + sent.shape[3:]), AXES, 0, 0)


def restored(blocks):
    power = jnp.exp2(blocks[:, -8:-7].astype(F32))
    return blocks[:, :-8].astype(F32) * power


def local(fixed_image, moving_image, conv_one, gain_one, shift_one, conv_two, gain_two, shift_two, sharpness):
    depth, height = lax.axis_size("depth"), lax.axis_size("height")
    slab, strip, _ = fixed_image.shape
    swap = [(i, i ^ 1) for i in range(depth)]
    blocks = gathered(fixed_image, moving_image)
    base, pairs, two, par = parameters(conv_one, gain_one, shift_one, conv_two, gain_two, shift_two)
    row, column = lax.axis_index("depth"), lax.axis_index("height")
    place = jnp.stack([row * slab, column * strip, slab * depth, strip * height, row % 2, row, column]).astype(jnp.int32)
    other = restored(lax.ppermute(blocks, "depth", swap))
    own = restored(blocks)
    mine = moments(own, pairs, par, depth, height, slab, strip)
    theirs = lax.ppermute(mine, "depth", swap)
    raw, sums = encode(own, other, mine, theirs, base, two, place, depth, height, slab, strip)
    sums = lax.all_to_all(sums, AXES, 0, 0)
    edge, side = rim(own, other, mine, theirs, base, two, place, depth, height, slab, strip)
    return match(edge, side, raw, sums, par, place, sharpness, slab, strip)


def solution(mesh):
    image = P("depth", "height", None)
    return jax.shard_map(
        local,
        mesh=mesh,
        in_specs=(image, image) + (P(),) * 7,
        out_specs=P(None, "depth", "height", None),
        check_vma=False,
    )
```

```python
import functools

import jax
import jax.numpy as jnp
import numpy as np
from jax import lax
from jax.experimental import pallas as pl
from jax.experimental.pallas import tpu as pltpu
from jax.sharding import PartitionSpec as P

RADIUS = 3
TILE = 8
F32 = jnp.float32
BF16 = jnp.bfloat16
FAR = -1e30
LOG2E = 1.4426950408889634
NUM = (((1,), (0,)), ((), ()))
AXES = ("depth", "height")


def leaky(v):
    return jnp.maximum(v, 0.01 * v)


def lag_list(far):
    return [(y, x) for y in range(-2, 3) for x in range(-2, 3) if (far, y, x) >= (0, 0, 0)]


def lag_index():
    keys = [("a", "a", far, y, x, "a") for far in range(3) for y, x in lag_list(far)]
    keys += [(e, "a", 0, y, x, "a") for e in "fl" for y, x in lag_list(0)]
    keys += [("a", e, far, 0, x, "a") for e in "fl" for far in range(3) for y, x in lag_list(far) if y == 0]
    keys += [(d, e, 0, 0, x, "a") for d in "fl" for e in "fl" for y, x in lag_list(0) if y == 0]
    keys += [k[:5] + (e,) for e in "fl" for k in list(keys) if k[4] == 0]
    return {k: i for i, k in enumerate(keys)}


LAGS = lag_index()


def pair_table():
    table = np.zeros((729, 256), np.float32)
    taps = [(a, b, c) for a in range(3) for b in range(3) for c in range(3)]
    for i, k in enumerate(taps):
        for j, l in enumerate(taps):
            p, q = (k, l) if l >= k else (l, k)
            lag = tuple(v - u for u, v in zip(p, q))
            kinds = [[("a", 1)] + ([("f" if u == 2 else "l", -1)] if u == v != 1 else []) for u, v in zip(p, q)]
            for d, sd in kinds[0]:
                for h, sh in kinds[1]:
                    for w, sw in kinds[2]:
                        table[i * 27 + j, LAGS[(d, h) + lag + (w,)]] += sd * sh * sw
    return table


def moments_kernel(nd, nh, slab, strip, own_ref, pairs_ref, par_ref, out_ref, img, slid, pieces):
    zn, yn = nd * slab, nh * strip
    count = float(zn * yn * 128)
    lane8 = lax.broadcasted_iota(jnp.int32, (8, 128), 1)
    sub8 = lax.broadcasted_iota(jnp.int32, (8, 128), 0)
    row_y = lax.broadcasted_iota(jnp.int32, (yn, 128), 0)
    side = lax.broadcasted_iota(jnp.int32, (yn, 128), 1)
    gain, shift = [jnp.broadcast_to(par_ref[i:i + 1, :], (128, 128)).T[0:64] for i in range(2)]

    img[0:2] = jnp.zeros((2, yn + 16, 128), F32)
    img[:, 0:8, :] = jnp.zeros((zn + 2, 8, 128), F32)
    img[:, 8 + yn:16 + yn, :] = jnp.zeros((zn + 2, 8, 128), F32)
    slid[:, :, 0:8, :] = jnp.zeros((4, zn, 8, 128), F32)
    slid[:, :, 8 + yn:16 + yn, :] = jnp.zeros((4, zn, 8, 128), F32)

    def gather(d, _):
        for p in range(nh // 2):
            pair = own_ref[pl.ds(d * nh + 2 * p, 2)]
            for z in range(slab):
                both = jnp.concatenate([pair[0, strip * z:strip * (z + 1)], pair[1, strip * z:strip * (z + 1)]], axis=0)
                img[2 + slab * d + z, 8 + 8 * p:16 + 8 * p, :] = both
        return _

    lax.fori_loop(0, nd, gather, 0)

    def slide(i, _):
        at = 4 * i
        for u in range(4):
            v = img[2 + at + u, 8:8 + yn]
            for n, move in enumerate((-2, -1, 1, 2)):
                kept = (side + move >= 0) & (side + move < 128)
                slid[n, at + u, 8:8 + yn] = jnp.where(kept, pltpu.roll(v, (128 - move) % 128, 1), 0.0)
        return _

    lax.fori_loop(0, zn // 4, slide, 0)

    def other(z, y, x):
        if x == 0:
            return img[2 + z, y:y + 8, :]
        return slid[x + 2 if x < 0 else x + 1, z, y:y + 8, :]

    def put(key, v):
        at = 8 * LAGS[key]
        pieces[at:at + 8, :] = v
        if key[4] == 0:
            for e, end in (("f", 0), ("l", 127)):
                at = 8 * LAGS[key[:5] + (e,)]
                pieces[at:at + 8, :] = jnp.where(lane8 == end, v, 0.0)

    def products(z, y, lags, state, fars):
        state = [list(v) for v in state]
        for i in range(yn // 8):
            held = {far: img[2 + z - far, 8 + 8 * i:16 + 8 * i, :] for far in fars}
            moved = {x: other(z, 8 + 8 * i + y, x) for x in range(-2, 3)}
            part = 0 if y or 0 < i < yn // 8 - 1 else 1 if i == 0 else 2
            for n, (far, x) in enumerate(lags):
                if far in fars:
                    state[part][n] = state[part][n] + held[far] * moved[x]
        return tuple(tuple(v) for v in state)

    def record(d, y, lags, state, fars):
        for n, (far, x) in enumerate(lags):
            if far not in fars:
                continue
            if y == 0:
                put((d, "a", far, y, x, "a"), state[0][n] + state[1][n] + state[2][n])
                put((d, "f", far, y, x, "a"), jnp.where(sub8 == 0, state[1][n], 0.0))
                put((d, "l", far, y, x, "a"), jnp.where(sub8 == 7, state[2][n], 0.0))
            else:
                put((d, "a", far, y, x, "a"), state[0][n])

    nothing = jnp.zeros((8, 128), F32)
    pieces[8 * len(LAGS):2048, :] = jnp.zeros((2048 - 8 * len(LAGS), 128), F32)
    for y in range(-2, 3):
        lags = [(far, x) for far in range(3) for x in range(-2, 3) if (far, y, x) >= (0, 0, 0)]
        empty = ((nothing,) * len(lags),) * (1 if y else 3)
        state = lax.fori_loop(0, zn, lambda z, state: products(z, y, lags, state, (0, 1, 2)), empty)
        record("a", y, lags, state, (0, 1, 2))
        if y >= 0:
            for d, z in (("f", 0), ("l", zn - 1)):
                record(d, y, lags, products(z, y, lags, empty, (0,)), (0,))

    def add(z, total):
        return total + img[2 + z, 8:8 + yn, :]

    whole = lax.fori_loop(0, zn, add, jnp.zeros((yn, 128), F32))
    first, last = img[2, 8:8 + yn, :], img[1 + zn, 8:8 + yn, :]
    for kz in range(3):
        plane = (whole - last, whole, whole - first)[kz]
        for ky in range(3):
            v = plane
            if ky == 0:
                v = jnp.where(row_y == yn - 1, 0.0, v)
            if ky == 2:
                v = jnp.where(row_y == 0, 0.0, v)
            v = jnp.sum(v.reshape(yn // 8, 8, 128), axis=0)
            for kx in range(3):
                w = v
                if kx == 0:
                    w = jnp.where(lane8 == 127, 0.0, w)
                if kx == 2:
                    w = jnp.where(lane8 == 0, 0.0, w)
                at = 2048 + (kz * 9 + ky * 3 + kx) * 8
                pieces[at:at + 8, :] = w
    pieces[2264:2304, :] = jnp.zeros((40, 128), F32)
    rows = pieces[pl.ds(0, 288, stride=8), :]
    for s in range(1, 8):
        rows = rows + pieces[pl.ds(s, 288, stride=8), :]
    second = lax.dot_general(pairs_ref[:, 0:256], rows[0:256], NUM, precision=lax.Precision.HIGHEST, preferred_element_type=F32)
    mean = lax.dot_general(pairs_ref[:, 256:288], rows[256:288], NUM, precision=lax.Precision.HIGHEST, preferred_element_type=F32)
    mean = jnp.sum(mean, axis=1, keepdims=True) / count
    second = jnp.sum(second, axis=1, keepdims=True) / count
    scale = lax.rsqrt(second - mean * mean + 1e-05) * gain
    out_ref[0:64, :] = jnp.broadcast_to(scale, (64, 128))
    out_ref[64:128, :] = jnp.broadcast_to(shift - mean * scale, (64, 128))


def moments(own, pairs, par, nd, nh, slab, strip):
    zn, yn = nd * slab, nh * strip
    vm = pl.BlockSpec(memory_space=pltpu.VMEM)
    return pl.pallas_call(
        functools.partial(moments_kernel, nd, nh, slab, strip),
        out_shape=jax.ShapeDtypeStruct((128, 128), F32),
        in_specs=[vm] * 3,
        out_specs=vm,
        scratch_shapes=[
            pltpu.VMEM((zn + 2, yn + 16, 128), F32),
            pltpu.VMEM((4, zn, yn + 16, 128), F32),
            pltpu.VMEM((2304, 128), F32),
        ],
        compiler_params=pltpu.CompilerParams(vmem_limit_bytes=40 * 1024 * 1024),
        cost_estimate=pl.CostEstimate(flops=10 ** 9, bytes_accessed=10 ** 6, transcendentals=0),
        name="moments",
    )(own, pairs, par)


def joined(weights, taps, wide, lane64):
    raw = jnp.dot(weights, taps, preferred_element_type=F32)
    rows = []
    for y in range(wide):
        cut = slice(128 * y, 128 * y + 128)
        before = jnp.where(lane64 == 0, 0.0, pltpu.roll(raw[0:64, cut], 1, 1))
        after = jnp.where(lane64 == 127, 0.0, pltpu.roll(raw[128:192, cut], 127, 1))
        rows.append(before + raw[64:128, cut] + after)
    return rows


def banded(taps_ref, toep, rows):
    base = taps_ref[...]
    spot = lax.broadcasted_iota(jnp.int32, base.shape, 1)
    base_hi = base.astype(BF16).astype(F32)
    base = jnp.where((spot >= 144) & (spot < 288), (base - base_hi).astype(BF16).astype(F32), base_hi)
    for yo in range(rows):
        toep[64 * yo:64 * yo + 64, :] = (pltpu.roll(base, yo, 1) if yo else base).astype(BF16)


def first_layer(scans, slab, strip, near, group, nd, nh, own_ref, other_ref, mine_ref, theirs_ref, place_ref, win, toep, plane_hi, plane_lo, feat):
    planes, rows = slab + 2 * near, strip + 2 * near
    zn, yn = nd * slab, nh * strip
    z0, y0, core = place_ref[0], place_ref[1], place_ref[4]
    row, column = place_ref[5], place_ref[6]
    lane = lax.broadcasted_iota(jnp.int32, (16, 128), 1)
    reach = -(-(near + 1) // strip)
    for s, scan in enumerate(scans):
        win[s, :, 16:24, :] = jnp.zeros((3 * slab, 8, 128), F32)
        mine = core == scan
        for i in range(-1, 2):
            for j in range(-reach, reach + 1):
                d, h = row + i, column + j
                inside = (d >= 0) & (d < nd) & (h >= 0) & (h < nh)
                at = jnp.where(inside, d * nh + h, 0)
                block = jnp.where(mine, own_ref[at], other_ref[at])
                block = jnp.where(inside, block, 0.0)
                for z in range(slab):
                    win[s, slab * (i + 1) + z, strip * (j + 2):strip * (j + 3), :] = block[strip * z:strip * (z + 1)]
        for i in range(planes + 2):
            low = 2 * strip - near - 1
            v = win[s, slab - near - 1 + i, low:low + 16, :]
            before = jnp.where(lane == 0, 0.0, pltpu.roll(v, 1, 1))
            after = jnp.where(lane == 127, 0.0, pltpu.roll(v, 127, 1))
            v = jnp.concatenate([before, v, after], axis=0)
            hi = v.astype(BF16)
            plane_hi[s, i] = hi
            plane_lo[s, i] = (v - hi.astype(F32)).astype(BF16)
    scales = [jnp.where(core == scan, mine_ref[0:64], theirs_ref[0:64]) for scan in scans]
    offsets = [jnp.where(core == scan, mine_ref[64:128], theirs_ref[64:128]) for scan in scans]

    def first(i, _):
        sides = []
        for s in range(len(scans)):
            for u in range(group):
                hi = plane_hi[s, pl.ds(group * i + u, 3)].reshape(144, 128)
                lo = plane_lo[s, pl.ds(group * i + u, 3)].reshape(144, 128)
                sides.append(jnp.concatenate([hi, hi, lo, jnp.zeros((80, 128), BF16)], axis=0))
        raw = jnp.dot(toep[0:64 * rows, :], jnp.concatenate(sides, axis=1), preferred_element_type=F32)
        for s in range(len(scans)):
            for u in range(group):
                z = z0 - near + group * i + u
                cut = slice(128 * (s * group + u), 128 * (s * group + u) + 128)
                for yo in range(rows):
                    y = y0 - near + yo
                    v = leaky(raw[64 * yo:64 * yo + 64, cut] * scales[s] + offsets[s])
                    v = jnp.where((z >= 0) & (z < zn) & (y >= 0) & (y < yn), v, 0.0)
                    to = 128 * (s * rows + yo)
                    feat[group * i + u, :, to:to + 128] = v.astype(BF16)
        return _

    lax.fori_loop(0, planes // group, first, 0)


def encode_kernel(nd, nh, slab, strip, own_ref, other_ref, mine_ref, theirs_ref, taps_ref, two_ref, place_ref,
                  raw_hbm, sums_ref, win, toep, plane_hi, plane_lo, feat, raw, sem):
    rows = strip + 2
    banded(taps_ref, toep, rows)
    first_layer((0, 1), slab, strip, 1, 5, nd, nh, own_ref, other_ref, mine_ref, theirs_ref, place_ref, win, toep, plane_hi, plane_lo, feat)
    lane64 = lax.broadcasted_iota(jnp.int32, (64, 128), 1)
    zero = jnp.zeros((64, 128), F32)

    def store(z):
        return pltpu.make_async_copy(raw.at[z], raw_hbm.at[z], sem.at[z])

    def plane(i, state):
        state = list(state)
        taps = []
        for a in range(3):
            for b in range(3):
                cuts = [feat[4 * i + u + a, :, 128 * (s * rows + b):128 * (s * rows + b + strip)] for u in range(4) for s in range(2)]
                taps.append(jnp.concatenate(cuts, axis=1))
        for n, v in enumerate(joined(two_ref[...], jnp.concatenate(taps, axis=0), 8 * strip, lane64)):
            u, s, y = n // (2 * strip), n // strip % 2, n % strip
            raw[4 * i + u, s, :, 128 * y:128 * y + 128] = v
            state[s] = state[s] + v
            state[2 + s] = state[2 + s] + v * v
        for u in range(4):
            store(4 * i + u).start()
        return tuple(state)

    sums = lax.fori_loop(0, slab // 4, plane, (zero,) * 4)
    total = jnp.sum(jnp.concatenate(sums[0:2], axis=0).T, axis=0, keepdims=True)
    square = jnp.sum(jnp.concatenate(sums[2:4], axis=0).T, axis=0, keepdims=True)
    both = jnp.concatenate([total, square], axis=0)
    sums_ref[...] = jnp.broadcast_to(both[None], sums_ref.shape)
    for z in range(slab):
        store(z).wait()


def encode(own, other, mine, theirs, taps, two, place, nd, nh, slab, strip):
    vm = pl.BlockSpec(memory_space=pltpu.VMEM)
    sm = pl.BlockSpec(memory_space=pltpu.SMEM)
    hbm = pl.BlockSpec(memory_space=pl.ANY)
    return pl.pallas_call(
        functools.partial(encode_kernel, nd, nh, slab, strip),
        out_shape=(
            jax.ShapeDtypeStruct((slab, 2, 64, strip * 128), F32),
            jax.ShapeDtypeStruct((nd * nh, 2, 128), F32),
        ),
        in_specs=[vm] * 6 + [sm],
        out_specs=(hbm, vm),
        scratch_shapes=[
            pltpu.VMEM((2, 3 * slab, 24, 128), F32),
            pltpu.VMEM((64 * (strip + 2), 512), BF16),
            pltpu.VMEM((2, slab + 4, 48, 128), BF16),
            pltpu.VMEM((2, slab + 4, 48, 128), BF16),
            pltpu.VMEM((slab + 2, 64, 2 * (strip + 2) * 128), BF16),
            pltpu.VMEM((slab, 2, 64, strip * 128), F32),
            pltpu.SemaphoreType.DMA((slab,)),
        ],
        compiler_params=pltpu.CompilerParams(vmem_limit_bytes=52 * 1024 * 1024),
        name="encode",
    )(own, other, mine, theirs, taps, two, place)


def rim_kernel(nd, nh, slab, strip, own_ref, other_ref, mine_ref, theirs_ref, taps_ref, two_ref, place_ref,
               edge_ref, side_ref, win, toep, plane_hi, plane_lo, feat, edge, side, edge_sem, side_sem):
    lane64 = lax.broadcasted_iota(jnp.int32, (64, 128), 1)
    wide = strip + 6
    banded(taps_ref, toep, strip + 8)
    first_layer((1,), slab, strip, 4, 8, nd, nh, own_ref, other_ref, mine_ref, theirs_ref, place_ref, win, toep, plane_hi, plane_lo, feat)

    def store_edge(i):
        return pltpu.make_async_copy(edge.at[i], edge_ref.at[i], edge_sem.at[i])

    def store_side(i):
        return pltpu.make_async_copy(side.at[i], side_ref.at[i], side_sem.at[i])

    def whole(i, _):
        at = [jnp.where(n < RADIUS, n, n + slab) for n in (2 * i, 2 * i + 1)]
        taps = []
        for a in range(3):
            for b in range(3):
                taps.append(jnp.concatenate([feat[z + a, :, 128 * b:128 * (b + wide)] for z in at], axis=1))
        for n, v in enumerate(joined(two_ref[...], jnp.concatenate(taps, axis=0), 2 * wide, lane64)):
            y = n % wide
            edge[2 * i + n // wide, :, 128 * y:128 * y + 128] = v
        store_edge(2 * i).start()
        store_edge(2 * i + 1).start()
        return _

    def middle(i, _):
        z = RADIUS + 4 * i
        taps = []
        for a in range(3):
            for b in range(3):
                cuts = [feat[z + u + a, :, 128 * (c + b):128 * (c + b + 3)] for u in range(4) for c in (0, strip + 3)]
                taps.append(jnp.concatenate(cuts, axis=1))
        for y, v in enumerate(joined(two_ref[...], jnp.concatenate(taps, axis=0), 24, lane64)):
            side[4 * i + y // 6, :, 128 * (y % 6):128 * (y % 6) + 128] = v
        for u in range(4):
            store_side(4 * i + u).start()
        return _

    lax.fori_loop(0, RADIUS, whole, 0)
    lax.fori_loop(0, slab // 4, middle, 0)
    for i in range(2 * RADIUS):
        store_edge(i).wait()
    for i in range(slab):
        store_side(i).wait()


def rim(own, other, mine, theirs, taps, two, place, nd, nh, slab, strip):
    hbm = pl.BlockSpec(memory_space=pl.ANY)
    vm = pl.BlockSpec(memory_space=pltpu.VMEM)
    sm = pl.BlockSpec(memory_space=pltpu.SMEM)
    edge = (6, 64, (strip + 6) * 128)
    side = (slab, 64, 6 * 128)
    return pl.pallas_call(
        functools.partial(rim_kernel, nd, nh, slab, strip),
        out_shape=(jax.ShapeDtypeStruct(edge, F32), jax.ShapeDtypeStruct(side, F32)),
        in_specs=[vm] * 6 + [sm],
        out_specs=(hbm, hbm),
        scratch_shapes=[
            pltpu.VMEM((1, 3 * slab, 24, 128), F32),
            pltpu.VMEM((64 * (strip + 8), 512), BF16),
            pltpu.VMEM((1, slab + 10, 48, 128), BF16),
            pltpu.VMEM((1, slab + 10, 48, 128), BF16),
            pltpu.VMEM((slab + 8, 64, (strip + 8) * 128), BF16),
            pltpu.VMEM(edge, F32),
            pltpu.VMEM(side, F32),
            pltpu.SemaphoreType.DMA((6,)),
            pltpu.SemaphoreType.DMA((slab,)),
        ],
        compiler_params=pltpu.CompilerParams(vmem_limit_bytes=52 * 1024 * 1024),
        cost_estimate=pl.CostEstimate(flops=6 * 10 ** 9, bytes_accessed=10 ** 7, transcendentals=0),
        name="rim",
    )(own, other, mine, theirs, taps, two, place)


def parameters(conv_one, gain_one, shift_one, conv_two, gain_two, shift_two):
    w = conv_one.reshape(64, 3, 3, 3)
    base = jnp.pad(jnp.transpose(w, (0, 1, 3, 2)), ((0, 0), (0, 0), (0, 0), (0, 13))).reshape(64, 144)
    base = jnp.concatenate([base, base, base, jnp.zeros((64, 80), F32)], axis=1)
    flat = conv_one.reshape(64, 27)
    products = (flat[:, :, None] * flat[:, None, :]).reshape(64, 729)
    quad = jnp.dot(products, pair_table(), precision=lax.Precision.HIGHEST)
    pairs = jnp.concatenate([quad, flat, jnp.zeros((64, 5), F32)], axis=1)
    two = conv_two.reshape(3, 3, 3, 64, 64).transpose(2, 4, 0, 1, 3).reshape(192, 576)
    par = jnp.stack([jnp.concatenate([v, v]) for v in (gain_one, shift_one, gain_two, shift_two)])
    return base, pairs, two, par


def block_swap(rows):
    rows = list(rows)
    lane = lax.broadcasted_iota(jnp.int32, rows[0].shape, 1)
    for bit in range(4):
        step = 1 << bit
        low = (lane // (TILE * step)) % 2 == 0
        for q in range(16):
            if q & step:
                continue
            a, c = rows[q], rows[q + step]
            rows[q] = jnp.where(low, a, pltpu.roll(c, TILE * step, 1))
            rows[q + step] = jnp.where(low, pltpu.roll(a, 128 - TILE * step, 1), c)
    return rows


def match_kernel(slab, strip, edge_hbm, side_hbm, raw_hbm, sums_ref, par_ref, place_ref, sharp_ref, out_ref,
                 edge_ref, side_ref, raw_ref, turned, even, odd, fixed, score, peak, found,
                 edge_sem, side_sem, raw_sem):
    ch = raw_ref.shape[2]
    def load_edge(i):
        return pltpu.make_async_copy(edge_hbm.at[i], edge_ref.at[i], edge_sem.at[i])

    def load_side(i):
        return pltpu.make_async_copy(side_hbm.at[i], side_ref.at[i], side_sem.at[i])

    def load_raw(i):
        return pltpu.make_async_copy(raw_hbm.at[i], raw_ref.at[i], raw_sem.at[i])

    ahead = [load_edge(i) for i in range(RADIUS)]
    ahead += [load(i) for i in range(slab) for load in (load_side, load_raw)]
    ahead += [load_edge(RADIUS + i) for i in range(RADIUS)]
    for load in ahead:
        load.start()
    tall, wide = slab + 2 * RADIUS, strip + 2 * RADIUS
    groups = slab // 4
    span = 4 + 2 * RADIUS
    z0, y0 = place_ref[0], place_ref[1]
    zn, yn = place_ref[2], place_ref[3]

    sums = jnp.sum(sums_ref[...], axis=0) / (zn * yn * 128).astype(F32)
    mean, square = sums[0:1], sums[1:2]
    scale = lax.rsqrt(square - mean * mean + 1e-05) * par_ref[2:3]
    offset = par_ref[3:4] - mean * scale
    scale = jnp.broadcast_to(scale, (128, 128)).T
    offset = jnp.broadcast_to(offset, (128, 128)).T

    def feature(raw, scan):
        v = raw * scale[64 * scan:64 * scan + 64] + offset[64 * scan:64 * scan + 64]
        return leaky(v).astype(BF16).astype(F32)

    row16 = lax.broadcasted_iota(jnp.int32, (16, 128), 0)
    col16 = lax.broadcasted_iota(jnp.int32, (16, 128), 1)
    onehot_x = jnp.where((col16 == 80 + row16) | ((col16 >= 67) & (col16 < 70)), 1.0, 0.0)
    sub8 = lax.broadcasted_iota(jnp.int32, (8, 128), 0)
    blank = jnp.zeros((8, 128), F32)
    for i in range(2):
        turned[i] = jnp.zeros((136, 128), F32)

    def plane(z, middle):
        if middle:
            load_side(z - RADIUS).wait()
            load_raw(z - RADIUS).wait()
        else:
            at = jnp.where(z < RADIUS, z, z - slab)
            load_edge(at).wait()
        zz = z0 + z - RADIUS
        for y in range(wide):
            if not middle:
                raw = edge_ref[at, :, y * 128:(y + 1) * 128]
            elif RADIUS <= y < RADIUS + strip:
                raw = raw_ref[z - RADIUS, 1, :, (y - RADIUS) * 128:(y - RADIUS + 1) * 128]
            else:
                c = y if y < RADIUS else y - strip
                raw = side_ref[z - RADIUS, :, c * 128:(c + 1) * 128]
            f = feature(raw, 1)
            yy = y0 + y - RADIUS
            f = jnp.where((zz >= 0) & (zz < zn) & (yy >= 0) & (yy < yn), f, 0.0)
            norm = jnp.sum(f * f, axis=0, keepdims=True)
            hi = norm.astype(BF16).astype(F32)
            mid = (norm - hi).astype(BF16).astype(F32)
            low = norm - hi - mid
            extra = jnp.where(sub8 == 0, hi, jnp.where(sub8 == 1, mid, jnp.where(sub8 == 2, low, 0.0)))
            turned[y % 2, 4:132, 0:80] = jnp.concatenate([f, extra, blank], axis=0).astype(BF16).T.astype(F32)
            ones = jnp.where((col16 == 96 + y) | (col16 == 112 + z), 1.0, onehot_x).astype(BF16)[None]
            even[z, y] = (turned[y % 2, 0:128].astype(BF16).reshape(8, 16, 128) + ones).reshape(128, 128)
            odd[z, y] = (turned[y % 2, 8:136].astype(BF16).reshape(8, 16, 128) + ones).reshape(128, 128)

    def among(z, _):
        plane(z, True)
        return _

    def after(z, _):
        plane(z, False)
        return _

    lax.fori_loop(0, RADIUS, after, 0)
    lax.fori_loop(RADIUS, RADIUS + slab, among, 0)
    lax.fori_loop(RADIUS + slab, tall, after, 0)

    k = lax.broadcasted_iota(jnp.int32, (64, 128 * groups), 0)
    lane = lax.broadcasted_iota(jnp.int32, (64, 128 * groups), 1)
    fx, fy, fz = lane % 8, (lane // 8) % 4, lane // 32
    span_x = jnp.abs(k - fx - 4)
    span_y = jnp.abs(k - 16 - fy - 3)
    span_z = jnp.abs(k - 32 - fz - 3)
    apart = jnp.where(k < 16, span_x, jnp.where(k < 32, span_y, jnp.where(k < 48, span_z, 0)))
    tail = jnp.where(apart > RADIUS, FAR, 0.0)
    tail = tail.astype(BF16)
    for j in range(16):
        fixed[j, 80:128, :] = tail[0:48]
    row16f = lax.broadcasted_iota(jnp.int32, (16, 128), 0)
    for g in range(groups):
        norms = [jnp.zeros((16, 128), F32)] * 16
        for part in range(ch // 16):
            rows = []
            for q in range(16):
                raw = raw_ref[4 * g + q // 4, 0, part * 16:(part + 1) * 16, (q % 4) * 128:(q % 4 + 1) * 128]
                at = slice(part * 16, part * 16 + 16)
                rows.append(leaky(raw * scale[at] + offset[at]).astype(BF16))
            for j, v in enumerate(block_swap(rows)):
                fixed[j, part * 16:(part + 1) * 16, g * 128:(g + 1) * 128] = v
                norms[j] = norms[j] + v.astype(F32) * v.astype(F32)
        for j in range(16):
            norm = -0.5 * jnp.sum(norms[j], axis=0, keepdims=True)
            hi = norm.astype(BF16).astype(F32)
            mid = (norm - hi).astype(BF16).astype(F32)
            end = jnp.where(row16f < 3, -0.5, jnp.where(row16f == 3, hi, jnp.where(row16f == 4, mid, jnp.where(row16f == 5, norm - hi - mid, 0.0))))
            fixed[j, 64:80, g * 128:(g + 1) * 128] = end.astype(BF16)

    factor = sharp_ref[0] * (2.0 * LOG2E / ch)
    count = wide * 16
    lane1 = lax.broadcasted_iota(jnp.int32, (1, 128), 1)
    x_in, y_in, z_in = lane1 % 8, (lane1 // 8) % 4, lane1 // 32
    pos = lax.broadcasted_iota(jnp.int32, (16, 128), 0).astype(F32)

    marks = sorted({0, tall} | {4 * g for g in range(groups)} | {4 * g + span for g in range(groups)})

    def scores(m, parity):
        held = (even, odd)[parity]
        weights = fixed[2 * m + parity]
        best = [jnp.full((8, 128), -3e38, F32) for _g in range(groups)]
        for low, high in zip(marks[:-1], marks[1:]):
            items = held[low:high, :, pl.ds(pl.multiple_of(16 * m, 16), 16), :].reshape((high - low) * count, 128)
            users = [g for g in range(groups) if 4 * g <= low < 4 * g + span]
            s = jnp.dot(items, weights[:, users[0] * 128:(users[-1] + 1) * 128], preferred_element_type=F32)
            for i, g in enumerate(users):
                part = s[:, i * 128:(i + 1) * 128]
                score[parity, g, low - 4 * g:high - 4 * g] = part.reshape(high - low, count, 128)
                best[g] = jnp.maximum(best[g], jnp.max(part.reshape(-1, 8, 128), axis=0))
        for g in range(groups):
            peak[parity, g] = best[g]

    def sums_of(weight):
        zero = jnp.zeros((16, 128), F32)
        state = [[zero] * 4 for _g in range(groups)]
        for y in range(wide - 1, -1, -1):
            for g, at in enumerate(weight(y)):
                by_x, acc_z, part, acc_y = state[g]
                run, acc = zero, zero
                for z in range(span - 1, -1, -1):
                    run = run + at(z)
                    if z:
                        acc = acc + run
                if y:
                    part = part + run
                    acc_y = acc_y + part
                state[g] = [by_x + run, acc_z + acc, part, acc_y]
        return [[jnp.sum(v, axis=0, keepdims=True) for v in (by_x, acc_z, acc_y, by_x * pos)] for by_x, acc_z, _p, acc_y in state]

    def settle(g, j, total, acc_z, acc_y, acc_x):
        inv = 1.0 / total
        dz = acc_z * inv - (z_in + RADIUS).astype(F32)
        dy = acc_y * inv - (y_in + RADIUS).astype(F32)
        dx = acc_x * inv - (x_in + 4).astype(F32)
        found[g, j] = jnp.concatenate([dz, dy, dx, total, jnp.zeros((4, 128), F32)], axis=0)

    def tiles(m, least):
        for parity, held in enumerate((even, odd)):
            weights = fixed[2 * m + parity]

            def weight(y):
                items = held[:, y, pl.ds(pl.multiple_of(16 * m, 16), 16), :].reshape(tall * 16, 128)
                s = jnp.dot(items, weights, preferred_element_type=F32)

                def of(g):
                    first = 64 * g
                    return lambda z: jnp.exp2(s[first + 16 * z:first + 16 * z + 16, 128 * g:128 * g + 128] * factor)

                return [of(g) for g in range(groups)]

            for g, sums in enumerate(sums_of(weight)):
                settle(g, 2 * m + parity, *sums)
                least = jnp.minimum(least, sums[0])
        return least

    least = lax.fori_loop(0, 8, tiles, jnp.full((1, 128), 1.0, F32))

    @pl.when(jnp.logical_not(jnp.min(least) > 1e-18))
    def again():
        def tiles_again(m, _):
            for parity in range(2):
                scores(m, parity)
                tops = [jnp.max(peak[parity, g], axis=0, keepdims=True) * factor for g in range(groups)]

                def weight(y):
                    def of(g):
                        return lambda z: jnp.exp2(score[parity, g, z, 16 * y:16 * y + 16] * factor - tops[g])

                    return [of(g) for g in range(groups)]

                for g, sums in enumerate(sums_of(weight)):
                    settle(g, 2 * m + parity, *sums)
            return _

        lax.fori_loop(0, 8, tiles_again, 0)

    for g in range(groups):
        for q, v in enumerate(block_swap([found[g, j] for j in range(16)])):
            for comp in range(3):
                out_ref[comp, 4 * g + q // 4, pl.ds(q % 4, 1), :] = v[comp:comp + 1]


def match(edge, side, raw, sums, par, place, sharpness, slab, strip):
    tall, wide = slab + 2 * RADIUS, strip + 2 * RADIUS
    groups = slab // 4
    vm = pl.BlockSpec(memory_space=pltpu.VMEM)
    sm = pl.BlockSpec(memory_space=pltpu.SMEM)
    hbm = pl.BlockSpec(memory_space=pl.ANY)
    return pl.pallas_call(
        functools.partial(match_kernel, slab, strip),
        out_shape=jax.ShapeDtypeStruct((3, slab, strip, 128), F32),
        in_specs=[hbm] * 3 + [vm, vm, sm, sm],
        out_specs=vm,
        scratch_shapes=[
            pltpu.VMEM(edge.shape, F32),
            pltpu.VMEM(side.shape, F32),
            pltpu.VMEM(raw.shape, F32),
            pltpu.VMEM((2, 136, 128), F32),
            pltpu.VMEM((tall, wide, 128, 128), BF16),
            pltpu.VMEM((tall, wide, 128, 128), BF16),
            pltpu.VMEM((16, 128, 128 * groups), BF16),
            pltpu.VMEM((2, groups, 4 + 2 * RADIUS, wide * 16, 128), F32),
            pltpu.VMEM((2, groups, 8, 128), F32),
            pltpu.VMEM((groups, 16, 8, 128), F32),
            pltpu.SemaphoreType.DMA((2 * RADIUS,)),
            pltpu.SemaphoreType.DMA((slab,)),
            pltpu.SemaphoreType.DMA((slab,)),
        ],
        compiler_params=pltpu.CompilerParams(vmem_limit_bytes=60 * 1024 * 1024),
        name="match",
    )(edge, side, raw, sums, par, place, sharpness)


def gathered(fixed_image, moving_image):
    depth, height = lax.axis_size("depth"), lax.axis_size("height")
    slab, strip, width = fixed_image.shape
    both = jnp.stack([fixed_image, moving_image]).reshape(2, slab * strip, width)
    power = jnp.clip(jnp.floor(jnp.log2(jnp.max(jnp.abs(both), axis=(1, 2), keepdims=True))) - 13.0, -113.0, 113.0)
    scaled = jnp.pad(both * jnp.exp2(-power), ((0, 0), (0, 8), (0, 0)))
    spot = lax.broadcasted_iota(jnp.int32, scaled.shape, 1)
    sent = jnp.where(spot < slab * strip, scaled, power).astype(jnp.float16)
    sent = jnp.broadcast_to(sent[None, :, None], (depth // 2, 2, height) + sent.shape[1:])
    return lax.all_to_all(sent.reshape((depth * height,) + sent.shape[3:]), AXES, 0, 0)


def restored(blocks):
    power = jnp.exp2(blocks[:, -8:-7].astype(F32))
    return blocks[:, :-8].astype(F32) * power


def local(fixed_image, moving_image, conv_one, gain_one, shift_one, conv_two, gain_two, shift_two, sharpness):
    depth, height = lax.axis_size("depth"), lax.axis_size("height")
    slab, strip, _ = fixed_image.shape
    swap = [(i, i ^ 1) for i in range(depth)]
    blocks = gathered(fixed_image, moving_image)
    base, pairs, two, par = parameters(conv_one, gain_one, shift_one, conv_two, gain_two, shift_two)
    row, column = lax.axis_index("depth"), lax.axis_index("height")
    place = jnp.stack([row * slab, column * strip, slab * depth, strip * height, row % 2, row, column]).astype(jnp.int32)
    other = restored(lax.ppermute(blocks, "depth", swap))
    own = restored(blocks)
    mine = moments(own, pairs, par, depth, height, slab, strip)
    theirs = lax.ppermute(mine, "depth", swap)
    raw, sums = encode(own, other, mine, theirs, base, two, place, depth, height, slab, strip)
    sums = lax.all_to_all(sums, AXES, 0, 0)
    edge, side = rim(own, other, mine, theirs, base, two, place, depth, height, slab, strip)
    return match(edge, side, raw, sums, par, place, sharpness, slab, strip)


def solution(mesh):
    image = P("depth", "height", None)
    return jax.shard_map(
        local,
        mesh=mesh,
        in_specs=(image, image) + (P(),) * 7,
        out_specs=P(None, "depth", "height", None),
        check_vma=False,
    )
```

```python
import functools

import jax
import jax.numpy as jnp
import numpy as np
from jax import lax
from jax.experimental import pallas as pl
from jax.experimental.pallas import tpu as pltpu
from jax.sharding import PartitionSpec as P

RADIUS = 3
TILE = 8
F32 = jnp.float32
BF16 = jnp.bfloat16
FAR = -1e30
LOG2E = 1.4426950408889634
NUM = (((1,), (0,)), ((), ()))
AXES = ("depth", "height")


def leaky(v):
    return jnp.maximum(v, 0.01 * v)


def lag_list(far):
    return [(y, x) for y in range(-2, 3) for x in range(-2, 3) if (far, y, x) >= (0, 0, 0)]


def lag_index():
    keys = [("a", "a", far, y, x, "a") for far in range(3) for y, x in lag_list(far)]
    keys += [(e, "a", 0, y, x, "a") for e in "fl" for y, x in lag_list(0)]
    keys += [("a", e, far, 0, x, "a") for e in "fl" for far in range(3) for y, x in lag_list(far) if y == 0]
    keys += [(d, e, 0, 0, x, "a") for d in "fl" for e in "fl" for y, x in lag_list(0) if y == 0]
    keys += [k[:5] + (e,) for e in "fl" for k in list(keys) if k[4] == 0]
    return {k: i for i, k in enumerate(keys)}


LAGS = lag_index()


def pair_table():
    table = np.zeros((729, 256), np.float32)
    taps = [(a, b, c) for a in range(3) for b in range(3) for c in range(3)]
    for i, k in enumerate(taps):
        for j, l in enumerate(taps):
            p, q = (k, l) if l >= k else (l, k)
            lag = tuple(v - u for u, v in zip(p, q))
            kinds = [[("a", 1)] + ([("f" if u == 2 else "l", -1)] if u == v != 1 else []) for u, v in zip(p, q)]
            for d, sd in kinds[0]:
                for h, sh in kinds[1]:
                    for w, sw in kinds[2]:
                        table[i * 27 + j, LAGS[(d, h) + lag + (w,)]] += sd * sh * sw
    return table


def moments_kernel(nd, nh, slab, strip, own_ref, pairs_ref, par_ref, out_ref, img, slid, pieces):
    zn, yn = nd * slab, nh * strip
    count = float(zn * yn * 128)
    lane8 = lax.broadcasted_iota(jnp.int32, (8, 128), 1)
    sub8 = lax.broadcasted_iota(jnp.int32, (8, 128), 0)
    row_y = lax.broadcasted_iota(jnp.int32, (yn, 128), 0)
    side = lax.broadcasted_iota(jnp.int32, (yn, 128), 1)
    gain, shift = [jnp.broadcast_to(par_ref[i:i + 1, :], (128, 128)).T[0:64] for i in range(2)]

    img[0:2] = jnp.zeros((2, yn + 16, 128), F32)
    img[:, 0:8, :] = jnp.zeros((zn + 2, 8, 128), F32)
    img[:, 8 + yn:16 + yn, :] = jnp.zeros((zn + 2, 8, 128), F32)
    slid[:, :, 0:8, :] = jnp.zeros((4, zn, 8, 128), F32)
    slid[:, :, 8 + yn:16 + yn, :] = jnp.zeros((4, zn, 8, 128), F32)

    def gather(d, _):
        for p in range(nh // 2):
            pair = own_ref[pl.ds(d * nh + 2 * p, 2)]
            for z in range(slab):
                both = jnp.concatenate([pair[0, strip * z:strip * (z + 1)], pair[1, strip * z:strip * (z + 1)]], axis=0)
                img[2 + slab * d + z, 8 + 8 * p:16 + 8 * p, :] = both
        return _

    lax.fori_loop(0, nd, gather, 0)

    def slide(i, _):
        at = 8 * i
        for u in range(8):
            v = img[2 + at + u, 8:8 + yn]
            for n, move in enumerate((-2, -1, 1, 2)):
                kept = (side + move >= 0) & (side + move < 128)
                slid[n, at + u, 8:8 + yn] = jnp.where(kept, pltpu.roll(v, (128 - move) % 128, 1), 0.0)
        return _

    lax.fori_loop(0, zn // 8, slide, 0)

    def other(z, y, x):
        if x == 0:
            return img[2 + z, y:y + 8, :]
        return slid[x + 2 if x < 0 else x + 1, z, y:y + 8, :]

    def put(key, v):
        at = 8 * LAGS[key]
        pieces[at:at + 8, :] = v
        if key[4] == 0:
            for e, end in (("f", 0), ("l", 127)):
                at = 8 * LAGS[key[:5] + (e,)]
                pieces[at:at + 8, :] = jnp.where(lane8 == end, v, 0.0)

    def products(z, y, lags, state, fars):
        state = [list(v) for v in state]
        for i in range(yn // 8):
            held = {far: img[2 + z - far, 8 + 8 * i:16 + 8 * i, :] for far in fars}
            moved = {x: other(z, 8 + 8 * i + y, x) for x in range(-2, 3)}
            part = 0 if y or 0 < i < yn // 8 - 1 else 1 if i == 0 else 2
            for n, (far, x) in enumerate(lags):
                if far in fars:
                    state[part][n] = state[part][n] + held[far] * moved[x]
        return tuple(tuple(v) for v in state)

    def record(d, y, lags, state, fars):
        for n, (far, x) in enumerate(lags):
            if far not in fars:
                continue
            if y == 0:
                put((d, "a", far, y, x, "a"), state[0][n] + state[1][n] + state[2][n])
                put((d, "f", far, y, x, "a"), jnp.where(sub8 == 0, state[1][n], 0.0))
                put((d, "l", far, y, x, "a"), jnp.where(sub8 == 7, state[2][n], 0.0))
            else:
                put((d, "a", far, y, x, "a"), state[0][n])

    nothing = jnp.zeros((8, 128), F32)
    pieces[8 * len(LAGS):2048, :] = jnp.zeros((2048 - 8 * len(LAGS), 128), F32)
    for y in range(-2, 3):
        lags = [(far, x) for far in range(3) for x in range(-2, 3) if (far, y, x) >= (0, 0, 0)]
        empty = ((nothing,) * len(lags),) * (1 if y else 3)
        def several(i, state):
            for u in range(4):
                state = products(4 * i + u, y, lags, state, (0, 1, 2))
            return state

        state = lax.fori_loop(0, zn // 4, several, empty)
        record("a", y, lags, state, (0, 1, 2))
        if y >= 0:
            for d, z in (("f", 0), ("l", zn - 1)):
                record(d, y, lags, products(z, y, lags, empty, (0,)), (0,))

    def add(z, total):
        return total + img[2 + z, 8:8 + yn, :]

    whole = lax.fori_loop(0, zn, add, jnp.zeros((yn, 128), F32))
    first, last = img[2, 8:8 + yn, :], img[1 + zn, 8:8 + yn, :]
    for kz in range(3):
        plane = (whole - last, whole, whole - first)[kz]
        for ky in range(3):
            v = plane
            if ky == 0:
                v = jnp.where(row_y == yn - 1, 0.0, v)
            if ky == 2:
                v = jnp.where(row_y == 0, 0.0, v)
            v = jnp.sum(v.reshape(yn // 8, 8, 128), axis=0)
            for kx in range(3):
                w = v
                if kx == 0:
                    w = jnp.where(lane8 == 127, 0.0, w)
                if kx == 2:
                    w = jnp.where(lane8 == 0, 0.0, w)
                at = 2048 + (kz * 9 + ky * 3 + kx) * 8
                pieces[at:at + 8, :] = w
    pieces[2264:2304, :] = jnp.zeros((40, 128), F32)
    rows = pieces[pl.ds(0, 288, stride=8), :]
    for s in range(1, 8):
        rows = rows + pieces[pl.ds(s, 288, stride=8), :]
    second = lax.dot_general(pairs_ref[:, 0:256], rows[0:256], NUM, precision=lax.Precision.HIGHEST, preferred_element_type=F32)
    mean = lax.dot_general(pairs_ref[:, 256:288], rows[256:288], NUM, precision=lax.Precision.HIGHEST, preferred_element_type=F32)
    mean = jnp.sum(mean, axis=1, keepdims=True) / count
    second = jnp.sum(second, axis=1, keepdims=True) / count
    scale = lax.rsqrt(second - mean * mean + 1e-05) * gain
    out_ref[0:64, :] = jnp.broadcast_to(scale, (64, 128))
    out_ref[64:128, :] = jnp.broadcast_to(shift - mean * scale, (64, 128))


def moments(own, pairs, par, nd, nh, slab, strip):
    zn, yn = nd * slab, nh * strip
    vm = pl.BlockSpec(memory_space=pltpu.VMEM)
    return pl.pallas_call(
        functools.partial(moments_kernel, nd, nh, slab, strip),
        out_shape=jax.ShapeDtypeStruct((128, 128), F32),
        in_specs=[vm] * 3,
        out_specs=vm,
        scratch_shapes=[
            pltpu.VMEM((zn + 2, yn + 16, 128), F32),
            pltpu.VMEM((4, zn, yn + 16, 128), F32),
            pltpu.VMEM((2304, 128), F32),
        ],
        compiler_params=pltpu.CompilerParams(vmem_limit_bytes=40 * 1024 * 1024),
        cost_estimate=pl.CostEstimate(flops=10 ** 9, bytes_accessed=10 ** 6, transcendentals=0),
        name="moments",
    )(own, pairs, par)


def joined(weights, taps, wide, lane64):
    raw = jnp.dot(weights, taps, preferred_element_type=F32)
    rows = []
    for y in range(wide):
        cut = slice(128 * y, 128 * y + 128)
        before = jnp.where(lane64 == 0, 0.0, pltpu.roll(raw[0:64, cut], 1, 1))
        after = jnp.where(lane64 == 127, 0.0, pltpu.roll(raw[128:192, cut], 127, 1))
        rows.append(before + raw[64:128, cut] + after)
    return rows


def banded(taps_ref, toep, rows):
    base = taps_ref[...]
    spot = lax.broadcasted_iota(jnp.int32, base.shape, 1)
    base_hi = base.astype(BF16).astype(F32)
    base = jnp.where((spot >= 144) & (spot < 288), (base - base_hi).astype(BF16).astype(F32), base_hi)
    for yo in range(rows):
        toep[64 * yo:64 * yo + 64, :] = (pltpu.roll(base, yo, 1) if yo else base).astype(BF16)


def first_layer(scans, slab, strip, near, group, nd, nh, own_ref, other_ref, mine_ref, theirs_ref, place_ref, win, toep, plane_hi, plane_lo, feat):
    planes, rows = slab + 2 * near, strip + 2 * near
    zn, yn = nd * slab, nh * strip
    z0, y0, core = place_ref[0], place_ref[1], place_ref[4]
    row, column = place_ref[5], place_ref[6]
    lane = lax.broadcasted_iota(jnp.int32, (16, 128), 1)
    reach = -(-(near + 1) // strip)
    for s, scan in enumerate(scans):
        win[s, :, 16:24, :] = jnp.zeros((3 * slab, 8, 128), F32)
        mine = core == scan
        for i in range(-1, 2):
            for j in range(-reach, reach + 1):
                d, h = row + i, column + j
                inside = (d >= 0) & (d < nd) & (h >= 0) & (h < nh)
                at = jnp.where(inside, d * nh + h, 0)
                block = jnp.where(mine, own_ref[at], other_ref[at])
                block = jnp.where(inside, block, 0.0)
                for z in range(slab):
                    win[s, slab * (i + 1) + z, strip * (j + 2):strip * (j + 3), :] = block[strip * z:strip * (z + 1)]
        for i in range(planes + 2):
            low = 2 * strip - near - 1
            v = win[s, slab - near - 1 + i, low:low + 16, :]
            before = jnp.where(lane == 0, 0.0, pltpu.roll(v, 1, 1))
            after = jnp.where(lane == 127, 0.0, pltpu.roll(v, 127, 1))
            v = jnp.concatenate([before, v, after], axis=0)
            hi = v.astype(BF16)
            plane_hi[s, i] = hi
            plane_lo[s, i] = (v - hi.astype(F32)).astype(BF16)
    scales = [jnp.where(core == scan, mine_ref[0:64], theirs_ref[0:64]) for scan in scans]
    offsets = [jnp.where(core == scan, mine_ref[64:128], theirs_ref[64:128]) for scan in scans]

    def first(i, _):
        sides = []
        for s in range(len(scans)):
            for u in range(group):
                hi = plane_hi[s, pl.ds(group * i + u, 3)].reshape(144, 128)
                lo = plane_lo[s, pl.ds(group * i + u, 3)].reshape(144, 128)
                sides.append(jnp.concatenate([hi, hi, lo, jnp.zeros((80, 128), BF16)], axis=0))
        raw = jnp.dot(toep[0:64 * rows, :], jnp.concatenate(sides, axis=1), preferred_element_type=F32)
        for s in range(len(scans)):
            for u in range(group):
                z = z0 - near + group * i + u
                cut = slice(128 * (s * group + u), 128 * (s * group + u) + 128)
                for yo in range(rows):
                    y = y0 - near + yo
                    v = leaky(raw[64 * yo:64 * yo + 64, cut] * scales[s] + offsets[s])
                    v = jnp.where((z >= 0) & (z < zn) & (y >= 0) & (y < yn), v, 0.0)
                    to = 128 * (s * rows + yo)
                    feat[group * i + u, :, to:to + 128] = v.astype(BF16)
        return _

    lax.fori_loop(0, planes // group, first, 0)


def encode_kernel(nd, nh, slab, strip, own_ref, other_ref, mine_ref, theirs_ref, taps_ref, two_ref, place_ref,
                  raw_hbm, sums_ref, win, toep, plane_hi, plane_lo, feat, raw, sem):
    rows = strip + 2
    banded(taps_ref, toep, rows)
    first_layer((0, 1), slab, strip, 1, 5, nd, nh, own_ref, other_ref, mine_ref, theirs_ref, place_ref, win, toep, plane_hi, plane_lo, feat)
    lane64 = lax.broadcasted_iota(jnp.int32, (64, 128), 1)
    zero = jnp.zeros((64, 128), F32)

    def store(z):
        return pltpu.make_async_copy(raw.at[z], raw_hbm.at[z], sem.at[z])

    def plane(i, state):
        state = list(state)
        taps = []
        for a in range(3):
            for b in range(3):
                cuts = [feat[4 * i + u + a, :, 128 * (s * rows + b):128 * (s * rows + b + strip)] for u in range(4) for s in range(2)]
                taps.append(jnp.concatenate(cuts, axis=1))
        for n, v in enumerate(joined(two_ref[...], jnp.concatenate(taps, axis=0), 8 * strip, lane64)):
            u, s, y = n // (2 * strip), n // strip % 2, n % strip
            raw[4 * i + u, s, :, 128 * y:128 * y + 128] = v
            state[s] = state[s] + v
            state[2 + s] = state[2 + s] + v * v
        for u in range(4):
            store(4 * i + u).start()
        return tuple(state)

    sums = lax.fori_loop(0, slab // 4, plane, (zero,) * 4)
    total = jnp.sum(jnp.concatenate(sums[0:2], axis=0).T, axis=0, keepdims=True)
    square = jnp.sum(jnp.concatenate(sums[2:4], axis=0).T, axis=0, keepdims=True)
    both = jnp.concatenate([total, square], axis=0)
    sums_ref[...] = jnp.broadcast_to(both[None], sums_ref.shape)
    for z in range(slab):
        store(z).wait()


def encode(own, other, mine, theirs, taps, two, place, nd, nh, slab, strip):
    vm = pl.BlockSpec(memory_space=pltpu.VMEM)
    sm = pl.BlockSpec(memory_space=pltpu.SMEM)
    hbm = pl.BlockSpec(memory_space=pl.ANY)
    return pl.pallas_call(
        functools.partial(encode_kernel, nd, nh, slab, strip),
        out_shape=(
            jax.ShapeDtypeStruct((slab, 2, 64, strip * 128), F32),
            jax.ShapeDtypeStruct((nd * nh, 2, 128), F32),
        ),
        in_specs=[vm] * 6 + [sm],
        out_specs=(hbm, vm),
        scratch_shapes=[
            pltpu.VMEM((2, 3 * slab, 24, 128), F32),
            pltpu.VMEM((64 * (strip + 2), 512), BF16),
            pltpu.VMEM((2, slab + 4, 48, 128), BF16),
            pltpu.VMEM((2, slab + 4, 48, 128), BF16),
            pltpu.VMEM((slab + 2, 64, 2 * (strip + 2) * 128), BF16),
            pltpu.VMEM((slab, 2, 64, strip * 128), F32),
            pltpu.SemaphoreType.DMA((slab,)),
        ],
        compiler_params=pltpu.CompilerParams(vmem_limit_bytes=52 * 1024 * 1024),
        name="encode",
    )(own, other, mine, theirs, taps, two, place)


def rim_kernel(nd, nh, slab, strip, own_ref, other_ref, mine_ref, theirs_ref, taps_ref, two_ref, place_ref,
               edge_ref, side_ref, win, toep, plane_hi, plane_lo, feat, edge, side, edge_sem, side_sem):
    lane64 = lax.broadcasted_iota(jnp.int32, (64, 128), 1)
    wide = strip + 6
    banded(taps_ref, toep, strip + 8)
    first_layer((1,), slab, strip, 4, 8, nd, nh, own_ref, other_ref, mine_ref, theirs_ref, place_ref, win, toep, plane_hi, plane_lo, feat)

    def store_edge(i):
        return pltpu.make_async_copy(edge.at[i], edge_ref.at[i], edge_sem.at[i])

    def store_side(i):
        return pltpu.make_async_copy(side.at[i], side_ref.at[i], side_sem.at[i])

    def whole(i, _):
        at = [jnp.where(n < RADIUS, n, n + slab) for n in (2 * i, 2 * i + 1)]
        taps = []
        for a in range(3):
            for b in range(3):
                taps.append(jnp.concatenate([feat[z + a, :, 128 * b:128 * (b + wide)] for z in at], axis=1))
        for n, v in enumerate(joined(two_ref[...], jnp.concatenate(taps, axis=0), 2 * wide, lane64)):
            y = n % wide
            edge[2 * i + n // wide, :, 128 * y:128 * y + 128] = v
        store_edge(2 * i).start()
        store_edge(2 * i + 1).start()
        return _

    def middle(i, _):
        z = RADIUS + 4 * i
        taps = []
        for a in range(3):
            for b in range(3):
                cuts = [feat[z + u + a, :, 128 * (c + b):128 * (c + b + 3)] for u in range(4) for c in (0, strip + 3)]
                taps.append(jnp.concatenate(cuts, axis=1))
        for y, v in enumerate(joined(two_ref[...], jnp.concatenate(taps, axis=0), 24, lane64)):
            side[4 * i + y // 6, :, 128 * (y % 6):128 * (y % 6) + 128] = v
        for u in range(4):
            store_side(4 * i + u).start()
        return _

    lax.fori_loop(0, RADIUS, whole, 0)
    lax.fori_loop(0, slab // 4, middle, 0)
    for i in range(2 * RADIUS):
        store_edge(i).wait()
    for i in range(slab):
        store_side(i).wait()


def rim(own, other, mine, theirs, taps, two, place, nd, nh, slab, strip):
    hbm = pl.BlockSpec(memory_space=pl.ANY)
    vm = pl.BlockSpec(memory_space=pltpu.VMEM)
    sm = pl.BlockSpec(memory_space=pltpu.SMEM)
    edge = (6, 64, (strip + 6) * 128)
    side = (slab, 64, 6 * 128)
    return pl.pallas_call(
        functools.partial(rim_kernel, nd, nh, slab, strip),
        out_shape=(jax.ShapeDtypeStruct(edge, F32), jax.ShapeDtypeStruct(side, F32)),
        in_specs=[vm] * 6 + [sm],
        out_specs=(hbm, hbm),
        scratch_shapes=[
            pltpu.VMEM((1, 3 * slab, 24, 128), F32),
            pltpu.VMEM((64 * (strip + 8), 512), BF16),
            pltpu.VMEM((1, slab + 10, 48, 128), BF16),
            pltpu.VMEM((1, slab + 10, 48, 128), BF16),
            pltpu.VMEM((slab + 8, 64, (strip + 8) * 128), BF16),
            pltpu.VMEM(edge, F32),
            pltpu.VMEM(side, F32),
            pltpu.SemaphoreType.DMA((6,)),
            pltpu.SemaphoreType.DMA((slab,)),
        ],
        compiler_params=pltpu.CompilerParams(vmem_limit_bytes=52 * 1024 * 1024),
        cost_estimate=pl.CostEstimate(flops=6 * 10 ** 9, bytes_accessed=10 ** 7, transcendentals=0),
        name="rim",
    )(own, other, mine, theirs, taps, two, place)


def parameters(conv_one, gain_one, shift_one, conv_two, gain_two, shift_two):
    w = conv_one.reshape(64, 3, 3, 3)
    base = jnp.pad(jnp.transpose(w, (0, 1, 3, 2)), ((0, 0), (0, 0), (0, 0), (0, 13))).reshape(64, 144)
    base = jnp.concatenate([base, base, base, jnp.zeros((64, 80), F32)], axis=1)
    flat = conv_one.reshape(64, 27)
    products = (flat[:, :, None] * flat[:, None, :]).reshape(64, 729)
    quad = jnp.dot(products, pair_table(), precision=lax.Precision.HIGHEST)
    pairs = jnp.concatenate([quad, flat, jnp.zeros((64, 5), F32)], axis=1)
    two = conv_two.reshape(3, 3, 3, 64, 64).transpose(2, 4, 0, 1, 3).reshape(192, 576)
    par = jnp.stack([jnp.concatenate([v, v]) for v in (gain_one, shift_one, gain_two, shift_two)])
    return base, pairs, two, par


def block_swap(rows):
    rows = list(rows)
    lane = lax.broadcasted_iota(jnp.int32, rows[0].shape, 1)
    for bit in range(4):
        step = 1 << bit
        low = (lane // (TILE * step)) % 2 == 0
        for q in range(16):
            if q & step:
                continue
            a, c = rows[q], rows[q + step]
            rows[q] = jnp.where(low, a, pltpu.roll(c, TILE * step, 1))
            rows[q + step] = jnp.where(low, pltpu.roll(a, 128 - TILE * step, 1), c)
    return rows


def match_kernel(slab, strip, edge_hbm, side_hbm, raw_hbm, sums_ref, par_ref, place_ref, sharp_ref, out_ref,
                 edge_ref, side_ref, raw_ref, turned, even, odd, fixed, score, peak, found,
                 edge_sem, side_sem, raw_sem):
    ch = raw_ref.shape[2]
    def load_edge(i):
        return pltpu.make_async_copy(edge_hbm.at[i], edge_ref.at[i], edge_sem.at[i])

    def load_side(i):
        return pltpu.make_async_copy(side_hbm.at[i], side_ref.at[i], side_sem.at[i])

    def load_raw(i):
        return pltpu.make_async_copy(raw_hbm.at[i], raw_ref.at[i], raw_sem.at[i])

    ahead = [load_edge(i) for i in range(RADIUS)]
    ahead += [load(i) for i in range(slab) for load in (load_side, load_raw)]
    ahead += [load_edge(RADIUS + i) for i in range(RADIUS)]
    for load in ahead:
        load.start()
    tall, wide = slab + 2 * RADIUS, strip + 2 * RADIUS
    groups = slab // 4
    span = 4 + 2 * RADIUS
    z0, y0 = place_ref[0], place_ref[1]
    zn, yn = place_ref[2], place_ref[3]

    sums = jnp.sum(sums_ref[...], axis=0) / (zn * yn * 128).astype(F32)
    mean, square = sums[0:1], sums[1:2]
    scale = lax.rsqrt(square - mean * mean + 1e-05) * par_ref[2:3]
    offset = par_ref[3:4] - mean * scale
    scale = jnp.broadcast_to(scale, (128, 128)).T
    offset = jnp.broadcast_to(offset, (128, 128)).T

    def feature(raw, scan):
        v = raw * scale[64 * scan:64 * scan + 64] + offset[64 * scan:64 * scan + 64]
        return leaky(v).astype(BF16).astype(F32)

    row16 = lax.broadcasted_iota(jnp.int32, (16, 128), 0)
    col16 = lax.broadcasted_iota(jnp.int32, (16, 128), 1)
    onehot_x = jnp.where((col16 == 80 + row16) | ((col16 >= 67) & (col16 < 70)), 1.0, 0.0)
    sub8 = lax.broadcasted_iota(jnp.int32, (8, 128), 0)
    blank = jnp.zeros((8, 128), F32)
    for i in range(2):
        turned[i] = jnp.zeros((136, 128), F32)

    def plane(z, middle):
        if middle:
            load_side(z - RADIUS).wait()
            load_raw(z - RADIUS).wait()
        else:
            at = jnp.where(z < RADIUS, z, z - slab)
            load_edge(at).wait()
        zz = z0 + z - RADIUS
        for y in range(wide):
            if not middle:
                raw = edge_ref[at, :, y * 128:(y + 1) * 128]
            elif RADIUS <= y < RADIUS + strip:
                raw = raw_ref[z - RADIUS, 1, :, (y - RADIUS) * 128:(y - RADIUS + 1) * 128]
            else:
                c = y if y < RADIUS else y - strip
                raw = side_ref[z - RADIUS, :, c * 128:(c + 1) * 128]
            f = feature(raw, 1)
            yy = y0 + y - RADIUS
            f = jnp.where((zz >= 0) & (zz < zn) & (yy >= 0) & (yy < yn), f, 0.0)
            norm = jnp.sum(f * f, axis=0, keepdims=True)
            hi = norm.astype(BF16).astype(F32)
            mid = (norm - hi).astype(BF16).astype(F32)
            low = norm - hi - mid
            extra = jnp.where(sub8 == 0, hi, jnp.where(sub8 == 1, mid, jnp.where(sub8 == 2, low, 0.0)))
            turned[y % 2, 4:132, 0:80] = jnp.concatenate([f, extra, blank], axis=0).astype(BF16).T.astype(F32)
            ones = jnp.where((col16 == 96 + y) | (col16 == 112 + z), 1.0, onehot_x).astype(BF16)[None]
            even[z, y] = (turned[y % 2, 0:128].astype(BF16).reshape(8, 16, 128) + ones).reshape(128, 128)
            odd[z, y] = (turned[y % 2, 8:136].astype(BF16).reshape(8, 16, 128) + ones).reshape(128, 128)

    def among(z, _):
        plane(z, True)
        return _

    def after(z, _):
        plane(z, False)
        return _

    lax.fori_loop(0, RADIUS, after, 0)
    lax.fori_loop(RADIUS, RADIUS + slab, among, 0)
    lax.fori_loop(RADIUS + slab, tall, after, 0)

    k = lax.broadcasted_iota(jnp.int32, (64, 128 * groups), 0)
    lane = lax.broadcasted_iota(jnp.int32, (64, 128 * groups), 1)
    fx, fy, fz = lane % 8, (lane // 8) % 4, lane // 32
    span_x = jnp.abs(k - fx - 4)
    span_y = jnp.abs(k - 16 - fy - 3)
    span_z = jnp.abs(k - 32 - fz - 3)
    apart = jnp.where(k < 16, span_x, jnp.where(k < 32, span_y, jnp.where(k < 48, span_z, 0)))
    tail = jnp.where(apart > RADIUS, FAR, 0.0)
    tail = tail.astype(BF16)
    for j in range(16):
        fixed[j, 80:128, :] = tail[0:48]
    row16f = lax.broadcasted_iota(jnp.int32, (16, 128), 0)
    for g in range(groups):
        norms = [jnp.zeros((16, 128), F32)] * 16
        for part in range(ch // 16):
            rows = []
            for q in range(16):
                raw = raw_ref[4 * g + q // 4, 0, part * 16:(part + 1) * 16, (q % 4) * 128:(q % 4 + 1) * 128]
                at = slice(part * 16, part * 16 + 16)
                rows.append(leaky(raw * scale[at] + offset[at]).astype(BF16))
            for j, v in enumerate(block_swap(rows)):
                fixed[j, part * 16:(part + 1) * 16, g * 128:(g + 1) * 128] = v
                norms[j] = norms[j] + v.astype(F32) * v.astype(F32)
        for j in range(16):
            norm = -0.5 * jnp.sum(norms[j], axis=0, keepdims=True)
            hi = norm.astype(BF16).astype(F32)
            mid = (norm - hi).astype(BF16).astype(F32)
            end = jnp.where(row16f < 3, -0.5, jnp.where(row16f == 3, hi, jnp.where(row16f == 4, mid, jnp.where(row16f == 5, norm - hi - mid, 0.0))))
            fixed[j, 64:80, g * 128:(g + 1) * 128] = end.astype(BF16)

    factor = sharp_ref[0] * (2.0 * LOG2E / ch)
    count = wide * 16
    lane1 = lax.broadcasted_iota(jnp.int32, (1, 128), 1)
    x_in, y_in, z_in = lane1 % 8, (lane1 // 8) % 4, lane1 // 32
    pos = lax.broadcasted_iota(jnp.int32, (16, 128), 0).astype(F32)

    marks = sorted({0, tall} | {4 * g for g in range(groups)} | {4 * g + span for g in range(groups)})

    def scores(m, parity):
        held = (even, odd)[parity]
        weights = fixed[2 * m + parity]
        best = [jnp.full((8, 128), -3e38, F32) for _g in range(groups)]
        for low, high in zip(marks[:-1], marks[1:]):
            items = held[low:high, :, pl.ds(pl.multiple_of(16 * m, 16), 16), :].reshape((high - low) * count, 128)
            users = [g for g in range(groups) if 4 * g <= low < 4 * g + span]
            s = jnp.dot(items, weights[:, users[0] * 128:(users[-1] + 1) * 128], preferred_element_type=F32)
            for i, g in enumerate(users):
                part = s[:, i * 128:(i + 1) * 128]
                score[parity, g, low - 4 * g:high - 4 * g] = part.reshape(high - low, count, 128)
                best[g] = jnp.maximum(best[g], jnp.max(part.reshape(-1, 8, 128), axis=0))
        for g in range(groups):
            peak[parity, g] = best[g]

    def sums_of(weight):
        zero = jnp.zeros((16, 128), F32)
        state = [[zero] * 4 for _g in range(groups)]
        for y in range(wide - 1, -1, -1):
            for g, at in enumerate(weight(y)):
                by_x, acc_z, part, acc_y = state[g]
                run, acc = zero, zero
                for z in range(span - 1, -1, -1):
                    run = run + at(z)
                    if z:
                        acc = acc + run
                if y:
                    part = part + run
                    acc_y = acc_y + part
                state[g] = [by_x + run, acc_z + acc, part, acc_y]
        return [[jnp.sum(v, axis=0, keepdims=True) for v in (by_x, acc_z, acc_y, by_x * pos)] for by_x, acc_z, _p, acc_y in state]

    def settle(g, j, total, acc_z, acc_y, acc_x):
        inv = 1.0 / total
        dz = acc_z * inv - (z_in + RADIUS).astype(F32)
        dy = acc_y * inv - (y_in + RADIUS).astype(F32)
        dx = acc_x * inv - (x_in + 4).astype(F32)
        found[g, j] = jnp.concatenate([dz, dy, dx, total, jnp.zeros((4, 128), F32)], axis=0)

    def tiles(m, least):
        for parity, held in enumerate((even, odd)):
            weights = fixed[2 * m + parity]

            def weight(y):
                items = held[:, y, pl.ds(pl.multiple_of(16 * m, 16), 16), :].reshape(tall * 16, 128)
                s = jnp.dot(items, weights, preferred_element_type=F32)

                def of(g):
                    first = 64 * g
                    return lambda z: jnp.exp2(s[first + 16 * z:first + 16 * z + 16, 128 * g:128 * g + 128] * factor)

                return [of(g) for g in range(groups)]

            for g, sums in enumerate(sums_of(weight)):
                settle(g, 2 * m + parity, *sums)
                least = jnp.minimum(least, sums[0])
        return least

    least = lax.fori_loop(0, 8, tiles, jnp.full((1, 128), 1.0, F32))

    @pl.when(jnp.logical_not(jnp.min(least) > 1e-18))
    def again():
        def tiles_again(m, _):
            for parity in range(2):
                scores(m, parity)
                tops = [jnp.max(peak[parity, g], axis=0, keepdims=True) * factor for g in range(groups)]

                def weight(y):
                    def of(g):
                        return lambda z: jnp.exp2(score[parity, g, z, 16 * y:16 * y + 16] * factor - tops[g])

                    return [of(g) for g in range(groups)]

                for g, sums in enumerate(sums_of(weight)):
                    settle(g, 2 * m + parity, *sums)
            return _

        lax.fori_loop(0, 8, tiles_again, 0)

    for g in range(groups):
        for q, v in enumerate(block_swap([found[g, j] for j in range(16)])):
            for comp in range(3):
                out_ref[comp, 4 * g + q // 4, pl.ds(q % 4, 1), :] = v[comp:comp + 1]


def match(edge, side, raw, sums, par, place, sharpness, slab, strip):
    tall, wide = slab + 2 * RADIUS, strip + 2 * RADIUS
    groups = slab // 4
    vm = pl.BlockSpec(memory_space=pltpu.VMEM)
    sm = pl.BlockSpec(memory_space=pltpu.SMEM)
    hbm = pl.BlockSpec(memory_space=pl.ANY)
    return pl.pallas_call(
        functools.partial(match_kernel, slab, strip),
        out_shape=jax.ShapeDtypeStruct((3, slab, strip, 128), F32),
        in_specs=[hbm] * 3 + [vm, vm, sm, sm],
        out_specs=vm,
        scratch_shapes=[
            pltpu.VMEM(edge.shape, F32),
            pltpu.VMEM(side.shape, F32),
            pltpu.VMEM(raw.shape, F32),
            pltpu.VMEM((2, 136, 128), F32),
            pltpu.VMEM((tall, wide, 128, 128), BF16),
            pltpu.VMEM((tall, wide, 128, 128), BF16),
            pltpu.VMEM((16, 128, 128 * groups), BF16),
            pltpu.VMEM((2, groups, 4 + 2 * RADIUS, wide * 16, 128), F32),
            pltpu.VMEM((2, groups, 8, 128), F32),
            pltpu.VMEM((groups, 16, 8, 128), F32),
            pltpu.SemaphoreType.DMA((2 * RADIUS,)),
            pltpu.SemaphoreType.DMA((slab,)),
            pltpu.SemaphoreType.DMA((slab,)),
        ],
        compiler_params=pltpu.CompilerParams(vmem_limit_bytes=60 * 1024 * 1024),
        name="match",
    )(edge, side, raw, sums, par, place, sharpness)


def gathered(fixed_image, moving_image):
    depth, height = lax.axis_size("depth"), lax.axis_size("height")
    slab, strip, width = fixed_image.shape
    both = jnp.stack([fixed_image, moving_image]).reshape(2, slab * strip, width)
    power = jnp.clip(jnp.floor(jnp.log2(jnp.max(jnp.abs(both), axis=(1, 2), keepdims=True))) - 13.0, -113.0, 113.0)
    scaled = jnp.pad(both * jnp.exp2(-power), ((0, 0), (0, 8), (0, 0)))
    spot = lax.broadcasted_iota(jnp.int32, scaled.shape, 1)
    sent = jnp.where(spot < slab * strip, scaled, power).astype(jnp.float16)
    sent = jnp.broadcast_to(sent[None, :, None], (depth // 2, 2, height) + sent.shape[1:])
    return lax.all_to_all(sent.reshape((depth * height,) + sent.shape[3:]), AXES, 0, 0)


def restored(blocks):
    power = jnp.exp2(blocks[:, -8:-7].astype(F32))
    return blocks[:, :-8].astype(F32) * power


def local(fixed_image, moving_image, conv_one, gain_one, shift_one, conv_two, gain_two, shift_two, sharpness):
    depth, height = lax.axis_size("depth"), lax.axis_size("height")
    slab, strip, _ = fixed_image.shape
    swap = [(i, i ^ 1) for i in range(depth)]
    blocks = gathered(fixed_image, moving_image)
    base, pairs, two, par = parameters(conv_one, gain_one, shift_one, conv_two, gain_two, shift_two)
    row, column = lax.axis_index("depth"), lax.axis_index("height")
    place = jnp.stack([row * slab, column * strip, slab * depth, strip * height, row % 2, row, column]).astype(jnp.int32)
    other = restored(lax.ppermute(blocks, "depth", swap))
    own = restored(blocks)
    mine = moments(own, pairs, par, depth, height, slab, strip)
    theirs = lax.ppermute(mine, "depth", swap)
    raw, sums = encode(own, other, mine, theirs, base, two, place, depth, height, slab, strip)
    sums = lax.all_to_all(sums, AXES, 0, 0)
    edge, side = rim(own, other, mine, theirs, base, two, place, depth, height, slab, strip)
    return match(edge, side, raw, sums, par, place, sharpness, slab, strip)


def solution(mesh):
    image = P("depth", "height", None)
    return jax.shard_map(
        local,
        mesh=mesh,
        in_specs=(image, image) + (P(),) * 7,
        out_specs=P(None, "depth", "height", None),
        check_vma=False,
    )
```
